32 devices in a mesh: pool: 8 (over z, y), tp: 4 (over x, core).
Axes of the slice: x: 2, y: 2, z: 4, core: 2. Of those that a mesh axis runs over, the one named last changes fastest.
Arguments:
- queries: bfloat16 [1024, 64, 128], P(('pool', 'tp')), may hold values from -6 to 6
- fresh_key_values: bfloat16 [1024, 4, 2, 128], P(('pool', 'tp')), may hold values from -5 to 5
- pooled_page_cache: bfloat16 [5, 8, 8, 4, 2, 128], P(None, 'pool', None, 'tp'), may hold values from -5 to 5
- leaf_cache: bfloat16 [8, 256, 4, 2, 128], P('pool', None, 'tp'), may hold values from -5 to 5
- parent: int32 [13], replicated, may hold values from 0 to 4, as said below
- node_pages: int32 [5], replicated, may hold values from 4 to 8
- node_owner: int32 [5], replicated, may hold values from 0 to 7
- leaf_len: int32 [8], P('pool'), may hold values from 1 to 32
Outputs:
- attended: bfloat16 [1024, 64, 128], P(('pool', 'tp'))
The draws below stay inside these ranges and needn't reach their ends.
Inputs may be any that keep to these rules, and one draw needn't show every extreme that they name: Nodes 0 to 4 have parent 0; node 5 + r is request r's own node and its parent is one of nodes 1 to 4.
All inputs are finite; a program needn't handle non-finite values.
Results may differ from the reference program's by a relative error of at most 0.008.
Values may be sent and summed in bfloat16 or wider, within the bound.
No kernel may reach another device: no remote copies, remote signals or barrier semaphores. Data moves between devices by JAX's collectives and lax.ppermute only.
A program may use at most 64 MiB of HBM per device.

```python
import jax
import jax.numpy as jnp
from jax import lax

QUERY_HEADS = 64
KEY_VALUE_HEADS = 4
HEAD_SIZE = 128
REQUEST_TOKENS = 128
PAGE_TOKENS = 8
LEAF_PAGES = 32
MIDS = 4
LEAF_SLOTS = 256
SHARED_NODES = 5
REQUEST_COUNT = 8
TOKEN_COUNT = 1024
N_POOL = 8


def draw_queries(key, part):
    key = jax.random.fold_in(key, 11)
    values_drawn = jnp.clip(jax.random.normal(key, (TOKEN_COUNT, QUERY_HEADS, HEAD_SIZE), jnp.float32), -5.0, 5.0)
    return values_drawn.astype(jnp.bfloat16)


def draw_leaf_cache(key, part):
    key = jax.random.fold_in(key, 13)
    array_shape = (REQUEST_COUNT, LEAF_SLOTS, KEY_VALUE_HEADS, 2, HEAD_SIZE)
    values_drawn = jnp.clip(jax.random.normal(key, array_shape, jnp.float32), -5.0, 5.0)
    return values_drawn.astype(jnp.bfloat16)


def draw_parent(key, part):
    key = jax.random.fold_in(key, 17)
    upper = jnp.zeros((1 + MIDS,), jnp.int32)
    lower = jax.random.randint(key, (REQUEST_COUNT,), 1, MIDS + 1).astype(jnp.int32)
    forced = jax.random.randint(jax.random.fold_in(key, 1), (), 0, REQUEST_COUNT)
    lower = lower.at[forced].set(MIDS)
    return jnp.concatenate([upper, lower], 0)


def draw_node_pages(key, part):
    key = jax.random.fold_in(key, 19)
    counts = jax.random.randint(key, (SHARED_NODES,), N_POOL // 2, N_POOL + 1).astype(jnp.int32)
    picked = jax.random.permutation(jax.random.fold_in(key, 1), SHARED_NODES)
    counts = counts.at[picked[0]].set(N_POOL)
    counts = counts.at[picked[1]].set(N_POOL // 2)
    return counts


def draw_leaf_len(key, part):
    key = jax.random.fold_in(key, 23)
    counts = jax.random.randint(key, (REQUEST_COUNT,), 1, LEAF_PAGES + 1).astype(jnp.int32)
    forced = jax.random.randint(jax.random.fold_in(key, 1), (), 0, REQUEST_COUNT)
    return counts.at[forced].set(LEAF_PAGES)


def touch_ends(entries, own_key, smallest, largest):
    place = [jax.random.randint(jax.random.fold_in(own_key, axis), (), 0, length) for axis, length in enumerate(entries.shape)]
    longest = entries.shape.index(max(entries.shape))
    next_to = place[:longest] + [(place[longest] + 1) % entries.shape[longest]] + place[longest + 1:]
    return entries.at[tuple(place)].set(smallest).at[tuple(next_to)].set(largest)


def level_of(own_key, dims, shards, least, high):
    loudness = 1.0
    for position, blocks in shards:
        heights = jax.random.uniform(jax.random.fold_in(jax.random.fold_in(own_key, 6), position), (blocks,), jnp.float32, least / len(shards), high / len(shards))
        loudness = loudness * jnp.repeat(jnp.exp(heights), dims[position] // blocks).reshape((-1,) + (1,) * (len(dims) - 1 - position))
    return loudness


def bell_draw(rng, extent, deviation, bound, shards=(), held_as=jnp.bfloat16):
    gain = level_of(rng, extent, shards, -0.22, 0.18) if shards else 1.0
    values = jax.random.normal(rng, extent, jnp.float32) * deviation * gain
    return jnp.minimum(jnp.maximum(values, -bound), bound).astype(held_as)


def setup_inputs(seed: int = 0) -> dict:
    key_list = jax.random.split(jax.random.key(seed), 9)
    queries = draw_queries(jax.random.fold_in(key_list[8], 71), 0)
    fresh_key_values = bell_draw(key_list[1], (TOKEN_COUNT, KEY_VALUE_HEADS, 2, HEAD_SIZE), 1.0, 5.0, ((0, 32),))
    pooled_page_cache = bell_draw(key_list[2], (SHARED_NODES, N_POOL, PAGE_TOKENS, KEY_VALUE_HEADS, 2, HEAD_SIZE), 1.0, 5.0, ((1, 8), (3, 4)))
    leaf_cache = draw_leaf_cache(jax.random.fold_in(key_list[8], 71), 0)
    parent = draw_parent(jax.random.fold_in(key_list[8], 71), 0)
    node_pages = draw_node_pages(jax.random.fold_in(key_list[8], 71), 0)
    node_owner = touch_ends(jax.random.randint(key_list[6], (SHARED_NODES,), 0, N_POOL), jax.random.fold_in(key_list[6], 1), 0, N_POOL - 1).astype(jnp.int32)
    leaf_len = draw_leaf_len(jax.random.fold_in(key_list[8], 71), 0)
    return {"queries": queries, "fresh_key_values": fresh_key_values, "pooled_page_cache": pooled_page_cache, "leaf_cache": leaf_cache, "parent": parent, "node_pages": node_pages, "node_owner": node_owner, "leaf_len": leaf_len}


def stripe_valid(page_count, owner_slot):
    slot_ids = jnp.arange(N_POOL, dtype=jnp.int32)
    usable = jnp.mod(slot_ids - owner_slot, N_POOL) < page_count
    return jnp.repeat(usable, PAGE_TOKENS)

def reference(queries, fresh_key_values, pooled_page_cache, leaf_cache, parent, node_pages, node_owner, leaf_len):
    query_group_width = QUERY_HEADS // KEY_VALUE_HEADS
    inv_root = 1.0 / jnp.sqrt(jnp.float32(HEAD_SIZE))

    def per_request(request):
        request = request.astype(jnp.int32)
        first_row = (request * REQUEST_TOKENS).astype(jnp.int32)
        query_matrix = lax.dynamic_slice_in_dim(queries, first_row, REQUEST_TOKENS, 0)
        query_matrix = query_matrix.astype(jnp.float32).reshape(REQUEST_TOKENS, KEY_VALUE_HEADS, query_group_width, HEAD_SIZE)
        mid_node = parent[1 + MIDS + request]
        root_key_values = pooled_page_cache[0].reshape(N_POOL * PAGE_TOKENS, KEY_VALUE_HEADS, 2, HEAD_SIZE)
        middle_key_values = lax.dynamic_index_in_dim(pooled_page_cache, mid_node, 0, keepdims=False)
        middle_key_values = middle_key_values.reshape(N_POOL * PAGE_TOKENS, KEY_VALUE_HEADS, 2, HEAD_SIZE)
        leaf_pairs = lax.dynamic_index_in_dim(leaf_cache, request, 0, keepdims=False)
        suffix_pairs = lax.dynamic_slice_in_dim(fresh_key_values, first_row, REQUEST_TOKENS, 0)
        key_pairs = jnp.concatenate([root_key_values, middle_key_values, leaf_pairs, suffix_pairs], 0).astype(jnp.float32)
        root_mask = stripe_valid(node_pages[0], node_owner[0])
        mid_mask = stripe_valid(node_pages[mid_node], node_owner[mid_node])
        leaf_mask = jnp.arange(LEAF_SLOTS, dtype=jnp.int32) < leaf_len[request] * PAGE_TOKENS
        row_ids = jnp.arange(REQUEST_TOKENS, dtype=jnp.int32)
        causal = row_ids[None, :] <= row_ids[:, None]
        prefix_mask = jnp.concatenate([root_mask, mid_mask, leaf_mask], 0)
        key_mask = jnp.concatenate([jnp.broadcast_to(prefix_mask[None, :], (REQUEST_TOKENS, prefix_mask.shape[0])), causal], 1)
        scores = jnp.einsum('tkgd,skd->tkgs', query_matrix, key_pairs[:, :, 0, :]) * inv_root
        wide_mask = key_mask[:, None, None, :]
        scores = jnp.where(wide_mask, scores, jnp.float32(-1e+30))
        row_max = lax.optimization_barrier(jnp.max(scores, axis=-1, keepdims=True))
        weights = jnp.where(wide_mask, jnp.exp(scores - row_max), jnp.float32(0.0))
        totals = lax.optimization_barrier(jnp.sum(weights, axis=-1))
        rounded = lax.optimization_barrier(weights.astype(jnp.bfloat16)).astype(jnp.float32)
        attended = jnp.einsum('tkgs,skd->tkgd', rounded, key_pairs[:, :, 1, :]) / totals[..., None]
        return attended.astype(jnp.bfloat16).reshape(REQUEST_TOKENS, QUERY_HEADS, HEAD_SIZE)
    everything = lax.map(per_request, jnp.arange(REQUEST_COUNT, dtype=jnp.int32))
    return everything.reshape(TOKEN_COUNT, QUERY_HEADS, HEAD_SIZE)
```

```python
import functools

import jax
import jax.numpy as jnp
from jax import lax
from jax.experimental import pallas as pl
from jax.experimental.pallas import tpu as pltpu
from jax.sharding import PartitionSpec as P

LOG2_E = 1.4426950408889634
MASKED = -1e30
LONG = pl.CostEstimate(flops=5 * 10**10, bytes_accessed=10**6, transcendentals=0)
SHORT = pl.CostEstimate(flops=10**6, bytes_accessed=10**5, transcendentals=0)


def pick(shape, source_row):
    row = lax.broadcasted_iota(jnp.int32, shape, 0)
    column = lax.broadcasted_iota(jnp.int32, shape, 1)
    return jnp.where(column == source_row(row), 1.0, 0.0).astype(jnp.bfloat16)


def dot(a, b):
    return lax.dot_general(a, b, (((1,), (0,)), ((), ())), preferred_element_type=jnp.float32)


def select_kernel(
    page, parent_hbm, pages_hbm, owner_hbm, pool_hbm, leaf_hbm, fresh_hbm,
    out_hbm, local_ref, bias_ref,
    parent_ref, pages_ref, owner_ref, pool_ref, rows_ref, block_ref, sems,
):
    leaf_rows, fresh_rows = leaf_hbm.shape[0], fresh_hbm.shape[0]
    pairs = [
        (pool_hbm, pool_ref),
        (parent_hbm, parent_ref),
        (pages_hbm, pages_ref),
        (owner_hbm, owner_ref),
        (leaf_hbm, local_ref.at[pl.ds(0, leaf_rows)]),
        (fresh_hbm, local_ref.at[pl.ds(leaf_rows, fresh_rows)]),
    ]
    fetches = [pltpu.make_async_copy(*pair, sems.at[i]) for i, pair in enumerate(pairs)]
    for fetch in fetches:
        fetch.start()
    node_count = pool_ref.shape[0] // (2 * page)
    copies, requests = out_hbm.shape[:2]
    fetches[0].wait()
    rows_ref[...] = pool_ref[...].astype(jnp.float32)
    root = [rows_ref[pl.ds(kind, page, stride=2)] for kind in range(2)]
    fetches[1].wait()

    def one(request, carry):
        mid = parent_ref[node_count + request] * (2 * page)
        for kind in range(2):
            chosen = rows_ref[pl.ds(mid + kind, page, stride=2)]
            block_ref[kind, request] = jnp.concatenate([root[kind], chosen], 0).astype(jnp.bfloat16)
        return carry

    lax.fori_loop(0, requests, one, 0, unroll=requests <= 8)
    sends = [
        pltpu.make_async_copy(block_ref.at[copy % 2], out_hbm.at[copy], sems.at[len(pairs) + copy])
        for copy in range(copies)
    ]
    for send in sends:
        send.start()

    fetches[2].wait()
    fetches[3].wait()
    mid = parent_ref[node_count + lax.axis_index("pool")]
    key = lax.broadcasted_iota(jnp.int32, bias_ref.shape, 1)
    stripe, is_mid = key // (2 * page), (key % (2 * page)) >= page
    offset = stripe - jnp.where(is_mid, owner_ref[mid], owner_ref[0])
    offset = jnp.where(offset < 0, offset + requests, offset)
    used = offset < jnp.where(is_mid, pages_ref[mid], pages_ref[0])
    bias_ref[...] = jnp.where(used, 0.0, MASKED)
    for copy in fetches[4:] + sends:
        copy.wait()


def hand_over_kernel(*refs):
    pass


def hand_over(cost, *arrays):
    anywhere = pl.BlockSpec(memory_space=pl.ANY)
    return pl.pallas_call(
        hand_over_kernel,
        out_shape=[jax.ShapeDtypeStruct(array.shape, array.dtype) for array in arrays],
        in_specs=[anywhere] * len(arrays),
        out_specs=[anywhere] * len(arrays),
        input_output_aliases={i: i for i in range(len(arrays))},
        compiler_params=pltpu.CompilerParams(vmem_limit_bytes=2**20),
        cost_estimate=cost,
    )(*arrays)


def scores_of(rows, keys):
    scores = lax.dot_general(rows, keys, (((1,), (1,)), ((), ())), preferred_element_type=jnp.float32)
    return scores * (LOG2_E * 128 ** (-0.5))


def weigh(weights, values):
    sums = dot(weights.astype(jnp.bfloat16), jnp.concatenate([values, jnp.ones_like(values)], 1))
    return sums[:, : values.shape[1]], sums[:, values.shape[1] :]


def own_kernel(leaf_len_ref, q_ref, *rest, page):
    local_refs = rest[:4]
    result_ref, level_ref, bias_ref, kf_ref, vf_ref = rest[4:]
    tokens, q_heads, dim = q_ref.shape
    group = q_heads // 4
    leaf_slots = bias_ref.shape[0] - 4 * tokens
    rank = lax.axis_index("tp")

    key = lax.broadcasted_iota(jnp.int32, (leaf_slots, dim), 0)
    bias_ref[0:leaf_slots] = jnp.where(key < leaf_len_ref[0] * page, 0.0, MASKED).astype(jnp.bfloat16)
    key = lax.broadcasted_iota(jnp.int32, (tokens, dim), 0)
    row = lax.broadcasted_iota(jnp.int32, (tokens, dim), 1)
    for step in range(4):
        seen = key <= row if step == 0 else jnp.full((tokens, dim), rank ^ step, jnp.int32) < rank
        bias_ref[leaf_slots + step * tokens : leaf_slots + (step + 1) * tokens] = jnp.where(
            seen, 0.0, MASKED
        ).astype(jnp.bfloat16)

    fresh_rows = local_refs[0].shape[0] - 2 * leaf_slots

    def fresh_source(out_row):
        head, kind, token = out_row // (2 * tokens), (out_row // tokens) % 2, out_row % tokens
        return token * 8 + head * 2 + kind

    fresh_pick = pick((fresh_rows, fresh_rows), fresh_source)
    for step in range(4):
        parts = dot(fresh_pick, local_refs[step][2 * leaf_slots :]).astype(jnp.bfloat16)
        for head in range(4):
            base = head * 2 * tokens
            kf_ref[head, step * tokens : (step + 1) * tokens] = parts[base : base + tokens]
            vf_ref[head, step * tokens : (step + 1) * tokens] = parts[base + tokens : base + 2 * tokens]

    chunk = 256
    half = chunk // 2
    leaf_pick = pick((chunk, chunk), lambda out_row: (out_row % half) * 2 + out_row // half)
    bias = bias_ref[...]
    token = lax.broadcasted_iota(jnp.int32, (tokens * group, dim), 0) // group
    column = lax.broadcasted_iota(jnp.int32, (tokens * group, dim), 1)
    own_row = jnp.where(token == column, 1.0, 0.0).astype(jnp.bfloat16)
    for step in range(4):
        head = rank ^ step
        leaf_k, leaf_v = [], []
        for piece in range(leaf_slots // half):
            parts = dot(leaf_pick, local_refs[step][piece * chunk : (piece + 1) * chunk]).astype(jnp.bfloat16)
            leaf_k.append(parts[:half])
            leaf_v.append(parts[half:])
        keys = jnp.concatenate([jnp.concatenate(leaf_k + [kf_ref[head]], 0), bias], 1)
        values = jnp.concatenate(leaf_v + [vf_ref[head]], 0)
        rows = q_ref[:, pl.ds(pl.multiple_of(head * group, group), group), :].reshape(tokens * group, dim)
        scores = scores_of(jnp.concatenate([rows, own_row], 1), keys)
        top = jnp.max(scores, axis=1, keepdims=True)
        sums, totals = weigh(jnp.exp2(scores - top), values)
        result_ref[step] = sums / totals
        level_ref[step] = jnp.log2(totals) + top


def shared_kernel(q_ref, bias_ref, other_ref, level_ref, mine_ref, theirs_ref, out_hbm, stage_ref, sems):
    tokens, q_heads, dim = q_ref.shape
    group = q_heads // 4
    shared_keys = bias_ref.shape[1]
    rank = lax.axis_index("tp")
    has_keys = rank % 2 == 0
    bias = bias_ref[0:1]
    places = [pl.ds(pl.multiple_of((rank ^ step) * group, group), group) for step in range(4)]

    def above_level(step):
        head = rank ^ step
        keys = jnp.where(has_keys, mine_ref[head], theirs_ref[head]).reshape(shared_keys, dim)
        scores = scores_of(q_ref[:, places[step], :].reshape(tokens * group, dim), keys)
        return scores + bias - jnp.concatenate([level_ref[step]] * (shared_keys // dim), 1)

    def weighted(step, weights):
        head = rank ^ step
        values = jnp.where(has_keys, theirs_ref[head], mine_ref[head]).reshape(shared_keys, dim)
        return weigh(weights, values)

    def write(step, result):
        stage_ref[step] = result.astype(jnp.bfloat16).reshape(tokens, group, dim)
        copy = pltpu.make_async_copy(stage_ref.at[step], out_hbm.at[:, places[step]], sems.at[step])
        copy.start()
        return copy

    scores = [above_level(step) for step in range(4)]
    highest = functools.reduce(jnp.maximum, scores)
    writes = []
    for step in range(4):
        sums, totals = weighted(step, jnp.exp2(scores[step]))
        writes.append(write(step, (sums + other_ref[step]) / (totals + 1.0)))
    too_high = jnp.max(highest) > 100.0
    for copy in writes:
        copy.wait()

    @pl.when(too_high)
    def _():
        for step in range(4):
            scores = above_level(step)
            top = jnp.maximum(jnp.max(scores, axis=1, keepdims=True), 0.0)
            sums, totals = weighted(step, jnp.exp2(scores - top))
            other = jnp.exp2(-top)
            write(step, (sums + other_ref[step] * other) / (totals + other)).wait()


def per_device(queries, fresh, pool, leaf, parent, node_pages, node_owner, leaf_len):
    tp = lax.axis_size("tp")
    stripes = lax.axis_size("pool")
    shared_count, _, page, _, _, dim = pool.shape
    tokens, q_heads, _ = queries.shape
    vmem = pl.BlockSpec(memory_space=pltpu.VMEM)
    swap = lambda array, bit: lax.ppermute(array, "tp", [(i, i ^ bit) for i in range(tp)])
    hbm = pl.BlockSpec(memory_space=pltpu.HBM)

    pool_rows = pool.reshape(-1, dim)
    leaf_rows = leaf.reshape(-1, dim)
    fresh_rows = fresh.reshape(-1, dim)
    operands = (parent, node_pages, node_owner, pool_rows, leaf_rows, fresh_rows)
    sent, local_0, bias = pl.pallas_call(
        functools.partial(select_kernel, page),
        out_shape=[
            jax.ShapeDtypeStruct((tp, stripes, 2 * page, dim), jnp.bfloat16),
            jax.ShapeDtypeStruct((leaf_rows.shape[0] + fresh_rows.shape[0], dim), jnp.bfloat16),
            jax.ShapeDtypeStruct((8, stripes * 2 * page), jnp.float32),
        ],
        in_specs=[hbm] * 6,
        out_specs=[hbm, vmem, vmem],
        scratch_shapes=[
            pltpu.SMEM(parent.shape, jnp.int32),
            pltpu.SMEM(node_pages.shape, jnp.int32),
            pltpu.SMEM(node_owner.shape, jnp.int32),
            pltpu.VMEM(pool_rows.shape, jnp.bfloat16),
            pltpu.VMEM(pool_rows.shape, jnp.float32),
            pltpu.VMEM((2, stripes, 2 * page, dim), jnp.bfloat16),
            pltpu.SemaphoreType.DMA((6 + tp,)),
        ],
        compiler_params=pltpu.CompilerParams(vmem_limit_bytes=16 * 2**20),
        cost_estimate=LONG,
    )(*[pltpu.with_memory_space_constraint(operand, pltpu.HBM) for operand in operands])
    local_2 = swap(local_0, 2)
    mine = lax.all_to_all(
        sent.reshape(tp * stripes, 2 * page, dim), ("tp", "pool"), split_axis=0, concat_axis=0, tiled=True
    ).reshape(tp, stripes, 2 * page, dim)
    local_0, local_2 = hand_over(LONG, local_0, local_2)
    local_1, local_3 = swap(local_0, 1), swap(local_2, 1)

    rows = tokens * q_heads // tp
    other, level = pl.pallas_call(
        functools.partial(own_kernel, page=page),
        out_shape=[jax.ShapeDtypeStruct((tp, rows, dim), jnp.float32)] * 2,
        in_specs=[pl.BlockSpec(memory_space=pltpu.SMEM)] + [vmem] * 5,
        out_specs=[vmem] * 2,
        scratch_shapes=[pltpu.VMEM((leaf.shape[1] + tp * tokens, dim), jnp.bfloat16)]
        + [pltpu.VMEM((tp, tp * tokens, dim), jnp.bfloat16)] * 2,
        compiler_params=pltpu.CompilerParams(vmem_limit_bytes=24 * 2**20),
        cost_estimate=SHORT,
    )(leaf_len, queries, local_0, local_1, local_2, local_3)
    mine, level = hand_over(SHORT, mine, level)
    theirs = swap(mine, 1)
    return pl.pallas_call(
        shared_kernel,
        out_shape=jax.ShapeDtypeStruct(queries.shape, jnp.bfloat16),
        in_specs=[vmem] * 6,
        out_specs=hbm,
        scratch_shapes=[
            pltpu.VMEM((tp, tokens, q_heads // tp, dim), jnp.bfloat16),
            pltpu.SemaphoreType.DMA((tp,)),
        ],
        compiler_params=pltpu.CompilerParams(vmem_limit_bytes=(24 if stripes <= 8 else 48) * 2**20),
    )(queries, bias, other, level, mine, theirs)


def solution(mesh):
    return jax.shard_map(
        per_device,
        mesh=mesh,
        in_specs=(
            P(("pool", "tp"), None, None),
            P(("pool", "tp"), None, None, None),
            P(None, "pool", None, "tp", None, None),
            P("pool", None, "tp", None, None),
            P(),
            P(),
            P(),
            P("pool"),
        ),
        out_specs=P(("pool", "tp"), None, None),
        check_vma=False,
    )
```

```python
import functools

import jax
import jax.numpy as jnp
from jax import lax
from jax.experimental import pallas as pl
from jax.experimental.pallas import tpu as pltpu
from jax.sharding import PartitionSpec as P

LOG2_E = 1.4426950408889634
MASKED = -1e30
LONG = pl.CostEstimate(flops=5 * 10**10, bytes_accessed=10**6, transcendentals=0)
SHORT = pl.CostEstimate(flops=10**6, bytes_accessed=10**5, transcendentals=0)


def pick(shape, source_row):
    row = lax.broadcasted_iota(jnp.int32, shape, 0)
    column = lax.broadcasted_iota(jnp.int32, shape, 1)
    return jnp.where(column == source_row(row), 1.0, 0.0).astype(jnp.bfloat16)


def dot(a, b):
    return lax.dot_general(a, b, (((1,), (0,)), ((), ())), preferred_element_type=jnp.float32)


def select_kernel(
    page, parent_hbm, pages_hbm, owner_hbm, pool_hbm, leaf_hbm, fresh_hbm,
    out_ref, local_ref, bias_ref,
    parent_ref, pages_ref, owner_ref, pool_ref, rows_ref, sems,
):
    leaf_rows, fresh_rows = leaf_hbm.shape[0], fresh_hbm.shape[0]
    pairs = [
        (pool_hbm, pool_ref),
        (parent_hbm, parent_ref),
        (pages_hbm, pages_ref),
        (owner_hbm, owner_ref),
        (leaf_hbm, local_ref.at[pl.ds(0, leaf_rows)]),
        (fresh_hbm, local_ref.at[pl.ds(leaf_rows, fresh_rows)]),
    ]
    fetches = [pltpu.make_async_copy(*pair, sems.at[i]) for i, pair in enumerate(pairs)]
    for fetch in fetches:
        fetch.start()
    node_count = pool_ref.shape[0] // (2 * page)
    copies, requests = out_ref.shape[:2]
    fetches[0].wait()
    rows_ref[...] = pool_ref[...].astype(jnp.float32)
    root = [rows_ref[pl.ds(kind, page, stride=2)] for kind in range(2)]
    fetches[1].wait()

    def one(request, carry):
        mid = parent_ref[node_count + request] * (2 * page)
        for kind in range(2):
            chosen = rows_ref[pl.ds(mid + kind, page, stride=2)]
            block = jnp.concatenate([root[kind], chosen], 0).astype(jnp.bfloat16)
            for copy in range(kind, copies, 2):
                out_ref[copy, request] = block
        return carry

    lax.fori_loop(0, requests, one, 0, unroll=requests <= 8)
    fetches[2].wait()
    fetches[3].wait()
    mid = parent_ref[node_count + lax.axis_index("pool")]
    key = lax.broadcasted_iota(jnp.int32, bias_ref.shape, 1)
    stripe, is_mid = key // (2 * page), (key % (2 * page)) >= page
    offset = stripe - jnp.where(is_mid, owner_ref[mid], owner_ref[0])
    offset = jnp.where(offset < 0, offset + requests, offset)
    used = offset < jnp.where(is_mid, pages_ref[mid], pages_ref[0])
    bias_ref[...] = jnp.where(used, 0.0, MASKED)
    for fetch in fetches[4:]:
        fetch.wait()


def hand_over_kernel(*refs):
    pass


def hand_over(cost, *arrays):
    anywhere = pl.BlockSpec(memory_space=pl.ANY)
    return pl.pallas_call(
        hand_over_kernel,
        out_shape=[jax.ShapeDtypeStruct(array.shape, array.dtype) for array in arrays],
        in_specs=[anywhere] * len(arrays),
        out_specs=[anywhere] * len(arrays),
        input_output_aliases={i: i for i in range(len(arrays))},
        compiler_params=pltpu.CompilerParams(vmem_limit_bytes=2**20),
        cost_estimate=cost,
    )(*arrays)


def scores_of(rows, keys):
    scores = lax.dot_general(rows, keys, (((1,), (1,)), ((), ())), preferred_element_type=jnp.float32)
    return scores * (LOG2_E * 128 ** (-0.5))


def weigh(weights, values):
    sums = dot(weights.astype(jnp.bfloat16), jnp.concatenate([values, jnp.ones_like(values)], 1))
    return sums[:, : values.shape[1]], sums[:, values.shape[1] :]


def own_kernel(leaf_len_ref, q_ref, *rest, page):
    local_refs = rest[:4]
    result_ref, level_ref, bias_ref, kf_ref, vf_ref = rest[4:]
    tokens, q_heads, dim = q_ref.shape
    group = q_heads // 4
    leaf_slots = bias_ref.shape[0] - 4 * tokens
    rank = lax.axis_index("tp")

    key = lax.broadcasted_iota(jnp.int32, (leaf_slots, dim), 0)
    bias_ref[0:leaf_slots] = jnp.where(key < leaf_len_ref[0] * page, 0.0, MASKED).astype(jnp.bfloat16)
    key = lax.broadcasted_iota(jnp.int32, (tokens, dim), 0)
    row = lax.broadcasted_iota(jnp.int32, (tokens, dim), 1)
    for step in range(4):
        seen = key <= row if step == 0 else jnp.full((tokens, dim), rank ^ step, jnp.int32) < rank
        bias_ref[leaf_slots + step * tokens : leaf_slots + (step + 1) * tokens] = jnp.where(
            seen, 0.0, MASKED
        ).astype(jnp.bfloat16)

    fresh_rows = local_refs[0].shape[0] - 2 * leaf_slots

    def fresh_source(out_row):
        head, kind, token = out_row // (2 * tokens), (out_row // tokens) % 2, out_row % tokens
        return token * 8 + head * 2 + kind

    fresh_pick = pick((fresh_rows, fresh_rows), fresh_source)
    for step in range(4):
        parts = dot(fresh_pick, local_refs[step][2 * leaf_slots :]).astype(jnp.bfloat16)
        for head in range(4):
            base = head * 2 * tokens
            kf_ref[head, step * tokens : (step + 1) * tokens] = parts[base : base + tokens]
            vf_ref[head, step * tokens : (step + 1) * tokens] = parts[base + tokens : base + 2 * tokens]

    chunk = 256
    half = chunk // 2
    leaf_pick = pick((chunk, chunk), lambda out_row: (out_row % half) * 2 + out_row // half)
    bias = bias_ref[...]
    token = lax.broadcasted_iota(jnp.int32, (tokens * group, dim), 0) // group
    column = lax.broadcasted_iota(jnp.int32, (tokens * group, dim), 1)
    own_row = jnp.where(token == column, 1.0, 0.0).astype(jnp.bfloat16)
    for step in range(4):
        head = rank ^ step
        leaf_k, leaf_v = [], []
        for piece in range(leaf_slots // half):
            parts = dot(leaf_pick, local_refs[step][piece * chunk : (piece + 1) * chunk]).astype(jnp.bfloat16)
            leaf_k.append(parts[:half])
            leaf_v.append(parts[half:])
        keys = jnp.concatenate([jnp.concatenate(leaf_k + [kf_ref[head]], 0), bias], 1)
        values = jnp.concatenate(leaf_v + [vf_ref[head]], 0)
        rows = q_ref[:, pl.ds(pl.multiple_of(head * group, group), group), :].reshape(tokens * group, dim)
        scores = scores_of(jnp.concatenate([rows, own_row], 1), keys)
        top = jnp.max(scores, axis=1, keepdims=True)
        sums, totals = weigh(jnp.exp2(scores - top), values)
        result_ref[step] = sums / totals
        level_ref[step] = jnp.log2(totals) + top


def shared_kernel(q_ref, bias_ref, other_ref, level_ref, mine_ref, theirs_ref, out_hbm, stage_ref, sems):
    tokens, q_heads, dim = q_ref.shape
    group = q_heads // 4
    shared_keys = bias_ref.shape[1]
    rank = lax.axis_index("tp")
    has_keys = rank % 2 == 0
    bias = bias_ref[0:1]
    places = [pl.ds(pl.multiple_of((rank ^ step) * group, group), group) for step in range(4)]

    def above_level(step):
        head = rank ^ step
        keys = jnp.where(has_keys, mine_ref[head], theirs_ref[head]).reshape(shared_keys, dim)
        scores = scores_of(q_ref[:, places[step], :].reshape(tokens * group, dim), keys)
        return scores + bias - jnp.concatenate([level_ref[step]] * (shared_keys // dim), 1)

    def weighted(step, weights):
        head = rank ^ step
        values = jnp.where(has_keys, theirs_ref[head], mine_ref[head]).reshape(shared_keys, dim)
        return weigh(weights, values)

    def write(step, result):
        stage_ref[step] = result.astype(jnp.bfloat16).reshape(tokens, group, dim)
        copy = pltpu.make_async_copy(stage_ref.at[step], out_hbm.at[:, places[step]], sems.at[step])
        copy.start()
        return copy

    scores = [above_level(step) for step in range(4)]
    highest = functools.reduce(jnp.maximum, scores)
    writes = []
    for step in range(4):
        sums, totals = weighted(step, jnp.exp2(scores[step]))
        writes.append(write(step, (sums + other_ref[step]) / (totals + 1.0)))
    too_high = jnp.max(highest) > 100.0
    for copy in writes:
        copy.wait()

    @pl.when(too_high)
    def _():
        for step in range(4):
            scores = above_level(step)
            top = jnp.maximum(jnp.max(scores, axis=1, keepdims=True), 0.0)
            sums, totals = weighted(step, jnp.exp2(scores - top))
            other = jnp.exp2(-top)
            write(step, (sums + other_ref[step] * other) / (totals + other)).wait()


def per_device(queries, fresh, pool, leaf, parent, node_pages, node_owner, leaf_len):
    tp = lax.axis_size("tp")
    stripes = lax.axis_size("pool")
    shared_count, _, page, _, _, dim = pool.shape
    tokens, q_heads, _ = queries.shape
    vmem = pl.BlockSpec(memory_space=pltpu.VMEM)
    swap = lambda array, bit: lax.ppermute(array, "tp", [(i, i ^ bit) for i in range(tp)])
    hbm = pl.BlockSpec(memory_space=pltpu.HBM)

    pool_rows = pool.reshape(-1, dim)
    leaf_rows = leaf.reshape(-1, dim)
    fresh_rows = fresh.reshape(-1, dim)
    operands = (parent, node_pages, node_owner, pool_rows, leaf_rows, fresh_rows)
    sent, local_0, bias = pl.pallas_call(
        functools.partial(select_kernel, page),
        out_shape=[
            pltpu.VMEM((tp, stripes, 2 * page, dim), jnp.bfloat16),
            jax.ShapeDtypeStruct((leaf_rows.shape[0] + fresh_rows.shape[0], dim), jnp.bfloat16),
            jax.ShapeDtypeStruct((8, stripes * 2 * page), jnp.float32),
        ],
        in_specs=[hbm] * 6,
        out_specs=[vmem] * 3,
        scratch_shapes=[
            pltpu.SMEM(parent.shape, jnp.int32),
            pltpu.SMEM(node_pages.shape, jnp.int32),
            pltpu.SMEM(node_owner.shape, jnp.int32),
            pltpu.VMEM(pool_rows.shape, jnp.bfloat16),
            pltpu.VMEM(pool_rows.shape, jnp.float32),
            pltpu.SemaphoreType.DMA((6,)),
        ],
        compiler_params=pltpu.CompilerParams(vmem_limit_bytes=16 * 2**20),
        cost_estimate=LONG,
    )(*[pltpu.with_memory_space_constraint(operand, pltpu.HBM) for operand in operands])
    local_2 = swap(local_0, 2)
    mine = lax.all_to_all(
        sent.reshape(tp * stripes, 2 * page, dim), ("tp", "pool"), split_axis=0, concat_axis=0, tiled=True
    ).reshape(tp, stripes, 2 * page, dim)
    local_0, local_2 = hand_over(LONG, local_0, local_2)
    local_1, local_3 = swap(local_0, 1), swap(local_2, 1)

    rows = tokens * q_heads // tp
    other, level = pl.pallas_call(
        functools.partial(own_kernel, page=page),
        out_shape=[jax.ShapeDtypeStruct((tp, rows, dim), jnp.float32)] * 2,
        in_specs=[pl.BlockSpec(memory_space=pltpu.SMEM)] + [vmem] * 5,
        out_specs=[vmem] * 2,
        scratch_shapes=[pltpu.VMEM((leaf.shape[1] + tp * tokens, dim), jnp.bfloat16)]
        + [pltpu.VMEM((tp, tp * tokens, dim), jnp.bfloat16)] * 2,
        compiler_params=pltpu.CompilerParams(vmem_limit_bytes=24 * 2**20),
        cost_estimate=SHORT,
    )(leaf_len, queries, local_0, local_1, local_2, local_3)
    mine, level = hand_over(SHORT, mine, level)
    theirs = swap(mine, 1)
    return pl.pallas_call(
        shared_kernel,
        out_shape=jax.ShapeDtypeStruct(queries.shape, jnp.bfloat16),
        in_specs=[vmem] * 6,
        out_specs=hbm,
        scratch_shapes=[
            pltpu.VMEM((tp, tokens, q_heads // tp, dim), jnp.bfloat16),
            pltpu.SemaphoreType.DMA((tp,)),
        ],
        compiler_params=pltpu.CompilerParams(vmem_limit_bytes=(24 if stripes <= 8 else 48) * 2**20),
    )(queries, bias, other, level, mine, theirs)


def solution(mesh):
    return jax.shard_map(
        per_device,
        mesh=mesh,
        in_specs=(
            P(("pool", "tp"), None, None),
            P(("pool", "tp"), None, None, None),
            P(None, "pool", None, "tp", None, None),
            P("pool", None, "tp", None, None),
            P(),
            P(),
            P(),
            P("pool"),
        ),
        out_specs=P(("pool", "tp"), None, None),
        check_vma=False,
    )
```

```python
import functools

import jax
import jax.numpy as jnp
from jax import lax
from jax.experimental import pallas as pl
from jax.experimental.pallas import tpu as pltpu
from jax.sharding import PartitionSpec as P

LOG2_E = 1.4426950408889634
MASKED = -1e30
LONG = pl.CostEstimate(flops=5 * 10**10, bytes_accessed=10**6, transcendentals=0)
SHORT = pl.CostEstimate(flops=10**6, bytes_accessed=10**5, transcendentals=0)


def pick(shape, source_row):
    row = lax.broadcasted_iota(jnp.int32, shape, 0)
    column = lax.broadcasted_iota(jnp.int32, shape, 1)
    return jnp.where(column == source_row(row), 1.0, 0.0).astype(jnp.bfloat16)


def dot(a, b):
    return lax.dot_general(a, b, (((1,), (0,)), ((), ())), preferred_element_type=jnp.float32)


def select_kernel(
    page, parent_hbm, pages_hbm, owner_hbm, pool_hbm, leaf_hbm, fresh_hbm,
    out_hbm, local_ref, bias_ref,
    parent_ref, pages_ref, owner_ref, pool_ref, rows_ref, block_ref, sems,
):
    leaf_rows, fresh_rows = leaf_hbm.shape[0], fresh_hbm.shape[0]
    pairs = [
        (pool_hbm, pool_ref),
        (parent_hbm, parent_ref),
        (pages_hbm, pages_ref),
        (owner_hbm, owner_ref),
        (leaf_hbm, local_ref.at[pl.ds(0, leaf_rows)]),
        (fresh_hbm, local_ref.at[pl.ds(leaf_rows, fresh_rows)]),
    ]
    fetches = [pltpu.make_async_copy(*pair, sems.at[i]) for i, pair in enumerate(pairs)]
    for fetch in fetches:
        fetch.start()
    node_count = pool_ref.shape[0] // (2 * page)
    copies, requests = out_hbm.shape[:2]
    fetches[0].wait()
    rows_ref[...] = pool_ref[...].astype(jnp.float32)
    root = [rows_ref[pl.ds(kind, page, stride=2)] for kind in range(2)]
    fetches[1].wait()

    def one(request, carry):
        mid = parent_ref[node_count + request] * (2 * page)
        for kind in range(2):
            chosen = rows_ref[pl.ds(mid + kind, page, stride=2)]
            block_ref[kind, request] = jnp.concatenate([root[kind], chosen], 0).astype(jnp.bfloat16)
        return carry

    lax.fori_loop(0, requests, one, 0, unroll=requests <= 8)
    sends = [
        pltpu.make_async_copy(block_ref.at[copy % 2], out_hbm.at[copy], sems.at[len(pairs) + copy])
        for copy in range(copies)
    ]
    for send in sends:
        send.start()

    fetches[2].wait()
    fetches[3].wait()
    mid = parent_ref[node_count + lax.axis_index("pool")]
    rank = lax.axis_index("tp")
    dim = bias_ref.shape[1]
    shared_keys = requests * 2 * page
    tokens = (bias_ref.shape[0] - shared_keys) // 4
    key = lax.broadcasted_iota(jnp.int32, (shared_keys, dim), 0)
    stripe, is_mid = key // (2 * page), (key % (2 * page)) >= page
    offset = stripe - jnp.where(is_mid, owner_ref[mid], owner_ref[0])
    offset = jnp.where(offset < 0, offset + requests, offset)
    used = offset < jnp.where(is_mid, pages_ref[mid], pages_ref[0])
    bias_ref[0:shared_keys] = jnp.where(used, 0.0, MASKED).astype(jnp.bfloat16)
    key = lax.broadcasted_iota(jnp.int32, (tokens, dim), 0)
    row = lax.broadcasted_iota(jnp.int32, (tokens, dim), 1)
    for step in range(4):
        seen = key <= row if step == 0 else jnp.full((tokens, dim), rank ^ step, jnp.int32) < rank
        first = shared_keys + step * tokens
        bias_ref[first : first + tokens] = jnp.where(seen, 0.0, MASKED).astype(jnp.bfloat16)
    for copy in fetches[4:] + sends:
        copy.wait()


def hand_over_kernel(*refs):
    pass


def hand_over(cost, *arrays):
    anywhere = pl.BlockSpec(memory_space=pl.ANY)
    return pl.pallas_call(
        hand_over_kernel,
        out_shape=[jax.ShapeDtypeStruct(array.shape, array.dtype) for array in arrays],
        in_specs=[anywhere] * len(arrays),
        out_specs=[anywhere] * len(arrays),
        input_output_aliases={i: i for i in range(len(arrays))},
        compiler_params=pltpu.CompilerParams(vmem_limit_bytes=2**20),
        cost_estimate=cost,
    )(*arrays)


def scores_of(rows, keys):
    scores = lax.dot_general(rows, keys, (((1,), (1,)), ((), ())), preferred_element_type=jnp.float32)
    return scores * (LOG2_E * 128 ** (-0.5))


def weigh(weights, values):
    sums = dot(weights.astype(jnp.bfloat16), jnp.concatenate([values, jnp.ones_like(values)], 1))
    return sums[:, : values.shape[1]], sums[:, values.shape[1] :]


def leaf_kernel(steps, fresh, leaf_len_ref, q_ref, *refs, page):
    count = 4 if fresh else len(steps)
    local_refs, (result_ref, level_ref, *fresh_refs) = refs[:count], refs[count:]
    tokens, q_heads, dim = q_ref.shape
    group = q_heads // 4
    leaf_rows = local_refs[0].shape[0] - 8 * tokens
    leaf_slots = leaf_rows // 2
    rank = lax.axis_index("tp")

    chunk = 256
    half = chunk // 2
    leaf_pick = pick((chunk, chunk), lambda out_row: (out_row % half) * 2 + out_row // half)
    key = lax.broadcasted_iota(jnp.int32, (leaf_slots, dim), 0)
    bias = jnp.where(key < leaf_len_ref[0] * page, 0.0, MASKED).astype(jnp.bfloat16)
    column = lax.broadcasted_iota(jnp.int32, (tokens * group, dim), 1)
    first = jnp.where(column == 0, 1.0, 0.0).astype(jnp.bfloat16)
    for place, step in enumerate(steps):
        local_ref = local_refs[step if fresh else place]
        heads = pl.ds(pl.multiple_of((rank ^ step) * group, group), group)
        leaf_k, leaf_v = [], []
        for piece in range(leaf_slots // half):
            parts = dot(leaf_pick, local_ref[piece * chunk : (piece + 1) * chunk]).astype(jnp.bfloat16)
            leaf_k.append(parts[:half])
            leaf_v.append(parts[half:])
        keys = jnp.concatenate([jnp.concatenate(leaf_k, 0), bias], 1)
        rows = jnp.concatenate([q_ref[:, heads, :].reshape(tokens * group, dim), first], 1)
        scores = scores_of(rows, keys)
        top = jnp.max(scores, axis=1, keepdims=True)
        sums, totals = weigh(jnp.exp2(scores - top), jnp.concatenate(leaf_v, 0))
        result_ref[place] = sums / totals
        level_ref[place] = jnp.log2(totals) + top
    if not fresh:
        return

    def fresh_source(out_row):
        head, kind, token = out_row // (2 * tokens), (out_row // tokens) % 2, out_row % tokens
        return token * 8 + head * 2 + kind

    kf_ref, vf_ref = fresh_refs
    fresh_pick = pick((8 * tokens, 8 * tokens), fresh_source)
    for step in range(4):
        parts = dot(fresh_pick, local_refs[step][leaf_rows:]).astype(jnp.bfloat16)
        for head in range(4):
            base = head * 2 * tokens
            kf_ref[head, step * tokens : (step + 1) * tokens] = parts[base : base + tokens]
            vf_ref[head, step * tokens : (step + 1) * tokens] = parts[base + tokens : base + 2 * tokens]


def shared_kernel(q_ref, bias_ref, *refs):
    other_refs, level_refs = refs[0:3], refs[3:6]
    kf_ref, vf_ref, mine_ref, theirs_ref, out_hbm, stage_ref, sems = refs[6:]
    tokens, q_heads, dim = q_ref.shape
    group = q_heads // 4
    shared_keys = bias_ref.shape[0] - 4 * tokens
    rank = lax.axis_index("tp")
    has_keys = rank % 2 == 0
    bias = bias_ref[...]
    token = lax.broadcasted_iota(jnp.int32, (tokens * group, dim), 0) // group
    column = lax.broadcasted_iota(jnp.int32, (tokens * group, dim), 1)
    own_row = jnp.where(token == column, 1.0, 0.0).astype(jnp.bfloat16)
    places = [pl.ds(pl.multiple_of((rank ^ step) * group, group), group) for step in range(4)]
    found = [(0, 0), (0, 1), (1, 0), (2, 0)]

    def above_level(step):
        head = rank ^ step
        shared = jnp.where(has_keys, mine_ref[head], theirs_ref[head]).reshape(shared_keys, dim)
        keys = jnp.concatenate([jnp.concatenate([shared, kf_ref[head]], 0), bias], 1)
        rows = jnp.concatenate([q_ref[:, places[step], :].reshape(tokens * group, dim), own_row], 1)
        which, place = found[step]
        level = level_refs[which][place]
        return scores_of(rows, keys) - jnp.concatenate([level] * (keys.shape[0] // dim), 1)

    def weighted(step, weights):
        head = rank ^ step
        shared = jnp.where(has_keys, theirs_ref[head], mine_ref[head]).reshape(shared_keys, dim)
        return weigh(weights, jnp.concatenate([shared, vf_ref[head]], 0))

    def other(step):
        which, place = found[step]
        return other_refs[which][place]

    def write(step, result):
        stage_ref[step] = result.astype(jnp.bfloat16).reshape(tokens, group, dim)
        copy = pltpu.make_async_copy(stage_ref.at[step], out_hbm.at[:, places[step]], sems.at[step])
        copy.start()
        return copy

    scores = [above_level(step) for step in range(4)]
    highest = functools.reduce(jnp.maximum, scores)
    writes = []
    for step in range(4):
        sums, totals = weighted(step, jnp.exp2(scores[step]))
        writes.append(write(step, (sums + other(step)) / (totals + 1.0)))
    too_high = jnp.max(highest) > 100.0
    for copy in writes:
        copy.wait()

    @pl.when(too_high)
    def _():
        for step in range(4):
            scores = above_level(step)
            top = jnp.maximum(jnp.max(scores, axis=1, keepdims=True), 0.0)
            sums, totals = weighted(step, jnp.exp2(scores - top))
            rest = jnp.exp2(-top)
            write(step, (sums + other(step) * rest) / (totals + rest)).wait()


def per_device(queries, fresh, pool, leaf, parent, node_pages, node_owner, leaf_len):
    tp = lax.axis_size("tp")
    stripes = lax.axis_size("pool")
    shared_count, _, page, _, _, dim = pool.shape
    tokens, q_heads, _ = queries.shape
    vmem = pl.BlockSpec(memory_space=pltpu.VMEM)
    swap = lambda array, bit: lax.ppermute(array, "tp", [(i, i ^ bit) for i in range(tp)])
    hbm = pl.BlockSpec(memory_space=pltpu.HBM)

    pool_rows = pool.reshape(-1, dim)
    leaf_rows = leaf.reshape(-1, dim)
    fresh_rows = fresh.reshape(-1, dim)
    operands = (parent, node_pages, node_owner, pool_rows, leaf_rows, fresh_rows)
    sent, local_0, bias = pl.pallas_call(
        functools.partial(select_kernel, page),
        out_shape=[
            jax.ShapeDtypeStruct((tp, stripes, 2 * page, dim), jnp.bfloat16),
            jax.ShapeDtypeStruct((leaf_rows.shape[0] + fresh_rows.shape[0], dim), jnp.bfloat16),
            jax.ShapeDtypeStruct((stripes * 2 * page + tp * tokens, dim), jnp.bfloat16),
        ],
        in_specs=[hbm] * 6,
        out_specs=[hbm, vmem, vmem],
        scratch_shapes=[
            pltpu.SMEM(parent.shape, jnp.int32),
            pltpu.SMEM(node_pages.shape, jnp.int32),
            pltpu.SMEM(node_owner.shape, jnp.int32),
            pltpu.VMEM(pool_rows.shape, jnp.bfloat16),
            pltpu.VMEM(pool_rows.shape, jnp.float32),
            pltpu.VMEM((2, stripes, 2 * page, dim), jnp.bfloat16),
            pltpu.SemaphoreType.DMA((6 + tp,)),
        ],
        compiler_params=pltpu.CompilerParams(vmem_limit_bytes=16 * 2**20),
        cost_estimate=LONG,
    )(*[pltpu.with_memory_space_constraint(operand, pltpu.HBM) for operand in operands])
    mine = lax.all_to_all(
        sent.reshape(tp * stripes, 2 * page, dim), ("tp", "pool"), split_axis=0, concat_axis=0, tiled=True
    ).reshape(tp, stripes, 2 * page, dim)
    local_1, local_2 = swap(local_0, 1), swap(local_0, 2)

    rows = tokens * q_heads // tp

    def leaf_call(steps, fresh, locals_):
        fresh_out = [jax.ShapeDtypeStruct((tp, tp * tokens, dim), jnp.bfloat16)] * 2 if fresh else []
        return pl.pallas_call(
            functools.partial(leaf_kernel, steps, fresh, page=page),
            out_shape=[jax.ShapeDtypeStruct((len(steps), rows, dim), jnp.float32)] * 2 + fresh_out,
            in_specs=[pl.BlockSpec(memory_space=pltpu.SMEM)] + [vmem] * (1 + len(locals_)),
            out_specs=[vmem] * (2 + len(fresh_out)),
            compiler_params=pltpu.CompilerParams(vmem_limit_bytes=24 * 2**20),
            cost_estimate=SHORT,
        )(leaf_len, queries, *locals_)

    other_a, level_a = leaf_call((0, 1), False, (local_0, local_1))
    local_2, level_a = hand_over(SHORT, local_2, level_a)
    local_3 = swap(local_2, 1)
    other_b, level_b = leaf_call((2,), False, (local_2,))
    mine, level_b = hand_over(SHORT, mine, level_b)
    theirs = swap(mine, 1)
    other_c, level_c, fresh_k, fresh_v = leaf_call((3,), True, (local_0, local_1, local_2, local_3))
    return pl.pallas_call(
        shared_kernel,
        out_shape=jax.ShapeDtypeStruct(queries.shape, jnp.bfloat16),
        in_specs=[vmem] * 12,
        out_specs=hbm,
        scratch_shapes=[
            pltpu.VMEM((tp, tokens, q_heads // tp, dim), jnp.bfloat16),
            pltpu.SemaphoreType.DMA((tp,)),
        ],
        compiler_params=pltpu.CompilerParams(vmem_limit_bytes=(24 if stripes <= 8 else 48) * 2**20),
    )(
        queries, bias, other_a, other_b, other_c, level_a, level_b, level_c,
        fresh_k, fresh_v, mine, theirs,
    )


def solution(mesh):
    return jax.shard_map(
        per_device,
        mesh=mesh,
        in_specs=(
            P(("pool", "tp"), None, None),
            P(("pool", "tp"), None, None, None),
            P(None, "pool", None, "tp", None, None),
            P("pool", None, "tp", None, None),
            P(),
            P(),
            P(),
            P("pool"),
        ),
        out_specs=P(("pool", "tp"), None, None),
        check_vma=False,
    )
```

```python
import functools

import jax
import jax.numpy as jnp
from jax import lax
from jax.experimental import pallas as pl
from jax.experimental.pallas import tpu as pltpu
from jax.sharding import PartitionSpec as P

LOG2_E = 1.4426950408889634
MASKED = -1e30
LONG = pl.CostEstimate(flops=5 * 10**10, bytes_accessed=10**6, transcendentals=0)
SHORT = pl.CostEstimate(flops=10**6, bytes_accessed=10**5, transcendentals=0)


def pick(shape, source_row):
    row = lax.broadcasted_iota(jnp.int32, shape, 0)
    column = lax.broadcasted_iota(jnp.int32, shape, 1)
    return jnp.where(column == source_row(row), 1.0, 0.0).astype(jnp.bfloat16)


def dot(a, b):
    return lax.dot_general(a, b, (((1,), (0,)), ((), ())), preferred_element_type=jnp.float32)


def select_kernel(
    page, parent_hbm, pages_hbm, owner_hbm, pool_hbm, leaf_hbm, fresh_hbm,
    out_hbm, local_ref, bias_ref,
    parent_ref, pages_ref, owner_ref, pool_ref, rows_ref, block_ref, sems,
):
    leaf_rows, fresh_rows = leaf_hbm.shape[0], fresh_hbm.shape[0]
    pairs = [
        (pool_hbm, pool_ref),
        (parent_hbm, parent_ref),
        (pages_hbm, pages_ref),
        (owner_hbm, owner_ref),
        (leaf_hbm, local_ref.at[pl.ds(0, leaf_rows)]),
        (fresh_hbm, local_ref.at[pl.ds(leaf_rows, fresh_rows)]),
    ]
    fetches = [pltpu.make_async_copy(*pair, sems.at[i]) for i, pair in enumerate(pairs)]
    for fetch in fetches:
        fetch.start()
    node_count = pool_ref.shape[0] // (2 * page)
    copies, requests = out_hbm.shape[:2]
    fetches[0].wait()
    rows_ref[...] = pool_ref[...].astype(jnp.float32)
    root = [rows_ref[pl.ds(kind, page, stride=2)] for kind in range(2)]
    fetches[1].wait()

    def one(request, carry):
        mid = parent_ref[node_count + request] * (2 * page)
        for kind in range(2):
            chosen = rows_ref[pl.ds(mid + kind, page, stride=2)]
            block_ref[kind, requests - 1 - request] = jnp.concatenate([root[kind], chosen], 0).astype(jnp.bfloat16)
        return carry

    lax.fori_loop(0, requests, one, 0, unroll=requests <= 8)
    sends = [
        pltpu.make_async_copy(block_ref.at[copy % 2], out_hbm.at[copies - 1 - copy], sems.at[len(pairs) + copy])
        for copy in range(copies)
    ]
    for send in sends:
        send.start()

    fetches[2].wait()
    fetches[3].wait()
    mid = parent_ref[node_count + lax.axis_index("pool")]
    key = lax.broadcasted_iota(jnp.int32, bias_ref.shape, 1)
    stripe, is_mid = requests - 1 - key // (2 * page), (key % (2 * page)) >= page
    offset = stripe - jnp.where(is_mid, owner_ref[mid], owner_ref[0])
    offset = jnp.where(offset < 0, offset + requests, offset)
    used = offset < jnp.where(is_mid, pages_ref[mid], pages_ref[0])
    bias_ref[...] = jnp.where(used, 0.0, MASKED)
    for copy in fetches[4:] + sends:
        copy.wait()


def hand_over_kernel(*refs):
    pass


def hand_over(cost, *arrays):
    anywhere = pl.BlockSpec(memory_space=pl.ANY)
    return pl.pallas_call(
        hand_over_kernel,
        out_shape=[jax.ShapeDtypeStruct(array.shape, array.dtype) for array in arrays],
        in_specs=[anywhere] * len(arrays),
        out_specs=[anywhere] * len(arrays),
        input_output_aliases={i: i for i in range(len(arrays))},
        compiler_params=pltpu.CompilerParams(vmem_limit_bytes=2**20),
        cost_estimate=cost,
    )(*arrays)


def scores_of(rows, keys):
    scores = lax.dot_general(rows, keys, (((1,), (1,)), ((), ())), preferred_element_type=jnp.float32)
    return scores * (LOG2_E * 128 ** (-0.5))


def weigh(weights, values):
    sums = dot(weights.astype(jnp.bfloat16), jnp.concatenate([values, jnp.ones_like(values)], 1))
    return sums[:, : values.shape[1]], sums[:, values.shape[1] :]


def own_kernel(leaf_len_ref, q_ref, *rest, page):
    local_refs = rest[:4]
    result_ref, level_ref, bias_ref, kf_ref, vf_ref = rest[4:]
    tokens, q_heads, dim = q_ref.shape
    group = q_heads // 4
    leaf_slots = bias_ref.shape[0] - 4 * tokens
    rank = lax.axis_index("tp")

    key = lax.broadcasted_iota(jnp.int32, (leaf_slots, dim), 0)
    bias_ref[0:leaf_slots] = jnp.where(key < leaf_len_ref[0] * page, 0.0, MASKED).astype(jnp.bfloat16)
    key = lax.broadcasted_iota(jnp.int32, (tokens, dim), 0)
    row = lax.broadcasted_iota(jnp.int32, (tokens, dim), 1)
    for step in range(4):
        seen = key <= row if step == 0 else jnp.full((tokens, dim), rank ^ step, jnp.int32) < rank
        bias_ref[leaf_slots + step * tokens : leaf_slots + (step + 1) * tokens] = jnp.where(
            seen, 0.0, MASKED
        ).astype(jnp.bfloat16)

    fresh_rows = local_refs[0].shape[0] - 2 * leaf_slots

    def fresh_source(out_row):
        head, kind, token = out_row // (2 * tokens), (out_row // tokens) % 2, out_row % tokens
        return token * 8 + head * 2 + kind

    fresh_pick = pick((fresh_rows, fresh_rows), fresh_source)
    for step in range(4):
        parts = dot(fresh_pick, local_refs[step][2 * leaf_slots :]).astype(jnp.bfloat16)
        for head in range(4):
            base = head * 2 * tokens
            kf_ref[head, step * tokens : (step + 1) * tokens] = parts[base : base + tokens]
            vf_ref[head, step * tokens : (step + 1) * tokens] = parts[base + tokens : base + 2 * tokens]

    chunk = 256
    half = chunk // 2
    leaf_pick = pick((chunk, chunk), lambda out_row: (out_row % half) * 2 + out_row // half)
    bias = bias_ref[...]
    token = lax.broadcasted_iota(jnp.int32, (tokens * group, dim), 0) // group
    column = lax.broadcasted_iota(jnp.int32, (tokens * group, dim), 1)
    own_row = jnp.where(token == column, 1.0, 0.0).astype(jnp.bfloat16)
    for step in range(4):
        head = rank ^ step
        leaf_k, leaf_v = [], []
        for piece in range(leaf_slots // half):
            parts = dot(leaf_pick, local_refs[step][piece * chunk : (piece + 1) * chunk]).astype(jnp.bfloat16)
            leaf_k.append(parts[:half])
            leaf_v.append(parts[half:])
        keys = jnp.concatenate([jnp.concatenate(leaf_k + [kf_ref[head]], 0), bias], 1)
        values = jnp.concatenate(leaf_v + [vf_ref[head]], 0)
        rows = q_ref[:, pl.ds(pl.multiple_of(head * group, group), group), :].reshape(tokens * group, dim)
        scores = scores_of(jnp.concatenate([rows, own_row], 1), keys)
        top = jnp.max(scores, axis=1, keepdims=True)
        sums, totals = weigh(jnp.exp2(scores - top), values)
        result_ref[step] = sums / totals
        level_ref[step] = jnp.log2(totals) + top


def shared_kernel(q_ref, bias_ref, other_ref, level_ref, mine_ref, theirs_ref, out_hbm, stage_ref, sems):
    tokens, q_heads, dim = q_ref.shape
    group = q_heads // 4
    shared_keys = bias_ref.shape[1]
    rank = lax.axis_index("tp")
    has_keys = rank % 2 == 0
    bias = bias_ref[0:1]
    places = [pl.ds(pl.multiple_of((rank ^ step) * group, group), group) for step in range(4)]

    def above_level(step):
        head = rank ^ step
        keys = jnp.where(has_keys, mine_ref[3 - head], theirs_ref[3 - head]).reshape(shared_keys, dim)
        scores = scores_of(q_ref[:, places[step], :].reshape(tokens * group, dim), keys)
        return scores + bias - jnp.concatenate([level_ref[step]] * (shared_keys // dim), 1)

    def weighted(step, weights):
        head = rank ^ step
        values = jnp.where(has_keys, theirs_ref[3 - head], mine_ref[3 - head]).reshape(shared_keys, dim)
        return weigh(weights, values)

    def write(step, result):
        stage_ref[step] = result.astype(jnp.bfloat16).reshape(tokens, group, dim)
        copy = pltpu.make_async_copy(stage_ref.at[step], out_hbm.at[:, places[step]], sems.at[step])
        copy.start()
        return copy

    scores = [above_level(step) for step in range(4)]
    highest = functools.reduce(jnp.maximum, scores)
    writes = []
    for step in range(4):
        sums, totals = weighted(step, jnp.exp2(scores[step]))
        writes.append(write(step, (sums + other_ref[step]) / (totals + 1.0)))
    too_high = jnp.max(highest) > 100.0
    for copy in writes:
        copy.wait()

    @pl.when(too_high)
    def _():
        for step in range(4):
            scores = above_level(step)
            top = jnp.maximum(jnp.max(scores, axis=1, keepdims=True), 0.0)
            sums, totals = weighted(step, jnp.exp2(scores - top))
            other = jnp.exp2(-top)
            write(step, (sums + other_ref[step] * other) / (totals + other)).wait()


def per_device(queries, fresh, pool, leaf, parent, node_pages, node_owner, leaf_len):
    tp = lax.axis_size("tp")
    stripes = lax.axis_size("pool")
    shared_count, _, page, _, _, dim = pool.shape
    tokens, q_heads, _ = queries.shape
    vmem = pl.BlockSpec(memory_space=pltpu.VMEM)
    swap = lambda array, bit: lax.ppermute(array, "tp", [(i, i ^ bit) for i in range(tp)])
    hbm = pl.BlockSpec(memory_space=pltpu.HBM)

    pool_rows = pool.reshape(-1, dim)
    leaf_rows = leaf.reshape(-1, dim)
    fresh_rows = fresh.reshape(-1, dim)
    operands = (parent, node_pages, node_owner, pool_rows, leaf_rows, fresh_rows)
    sent, local_0, bias = pl.pallas_call(
        functools.partial(select_kernel, page),
        out_shape=[
            jax.ShapeDtypeStruct((tp, stripes, 2 * page, dim), jnp.bfloat16),
            jax.ShapeDtypeStruct((leaf_rows.shape[0] + fresh_rows.shape[0], dim), jnp.bfloat16),
            jax.ShapeDtypeStruct((8, stripes * 2 * page), jnp.float32),
        ],
        in_specs=[hbm] * 6,
        out_specs=[hbm, vmem, vmem],
        scratch_shapes=[
            pltpu.SMEM(parent.shape, jnp.int32),
            pltpu.SMEM(node_pages.shape, jnp.int32),
            pltpu.SMEM(node_owner.shape, jnp.int32),
            pltpu.VMEM(pool_rows.shape, jnp.bfloat16),
            pltpu.VMEM(pool_rows.shape, jnp.float32),
            pltpu.VMEM((2, stripes, 2 * page, dim), jnp.bfloat16),
            pltpu.SemaphoreType.DMA((6 + tp,)),
        ],
        compiler_params=pltpu.CompilerParams(vmem_limit_bytes=16 * 2**20),
        cost_estimate=LONG,
    )(*[pltpu.with_memory_space_constraint(operand, pltpu.HBM) for operand in operands])
    local_2 = swap(local_0, 2)
    mine = lax.all_to_all(
        sent.reshape(tp * stripes, 2 * page, dim),
        ("tp", "pool"),
        split_axis=0,
        concat_axis=0,
        axis_index_groups=[list(reversed(range(tp * stripes)))],
        tiled=True,
    ).reshape(tp, stripes, 2 * page, dim)
    local_0, local_2 = hand_over(LONG, local_0, local_2)
    local_1, local_3 = swap(local_0, 1), swap(local_2, 1)

    rows = tokens * q_heads // tp
    other, level = pl.pallas_call(
        functools.partial(own_kernel, page=page),
        out_shape=[jax.ShapeDtypeStruct((tp, rows, dim), jnp.float32)] * 2,
        in_specs=[pl.BlockSpec(memory_space=pltpu.SMEM)] + [vmem] * 5,
        out_specs=[vmem] * 2,
        scratch_shapes=[pltpu.VMEM((leaf.shape[1] + tp * tokens, dim), jnp.bfloat16)]
        + [pltpu.VMEM((tp, tp * tokens, dim), jnp.bfloat16)] * 2,
        compiler_params=pltpu.CompilerParams(vmem_limit_bytes=24 * 2**20),
        cost_estimate=SHORT,
    )(leaf_len, queries, local_0, local_1, local_2, local_3)
    mine, level = hand_over(SHORT, mine, level)
    theirs = swap(mine, 1)
    return pl.pallas_call(
        shared_kernel,
        out_shape=jax.ShapeDtypeStruct(queries.shape, jnp.bfloat16),
        in_specs=[vmem] * 6,
        out_specs=hbm,
        scratch_shapes=[
            pltpu.VMEM((tp, tokens, q_heads // tp, dim), jnp.bfloat16),
            pltpu.SemaphoreType.DMA((tp,)),
        ],
        compiler_params=pltpu.CompilerParams(vmem_limit_bytes=(24 if stripes <= 8 else 48) * 2**20),
    )(queries, bias, other, level, mine, theirs)


def solution(mesh):
    return jax.shard_map(
        per_device,
        mesh=mesh,
        in_specs=(
            P(("pool", "tp"), None, None),
            P(("pool", "tp"), None, None, None),
            P(None, "pool", None, "tp", None, None),
            P("pool", None, "tp", None, None),
            P(),
            P(),
            P(),
            P("pool"),
        ),
        out_specs=P(("pool", "tp"), None, None),
        check_vma=False,
    )
```

```python
import functools

import jax
import jax.numpy as jnp
from jax import lax
from jax.experimental import pallas as pl
from jax.experimental.pallas import tpu as pltpu
from jax.sharding import PartitionSpec as P

LOG2_E = 1.4426950408889634
MASKED = -1e30
HEAD_SIZE = 128
LONG = pl.CostEstimate(flops=5 * 10**10, bytes_accessed=10**6, transcendentals=0)
SHORT = pl.CostEstimate(flops=10**6, bytes_accessed=10**5, transcendentals=0)


def pick(shape, source_row):
    row = lax.broadcasted_iota(jnp.int32, shape, 0)
    column = lax.broadcasted_iota(jnp.int32, shape, 1)
    return jnp.where(column == source_row(row), 1.0, 0.0).astype(jnp.bfloat16)


def dot(a, b):
    return lax.dot_general(a, b, (((1,), (0,)), ((), ())), preferred_element_type=jnp.float32)


def select_kernel(
    page, parent_hbm, pages_hbm, owner_hbm, pool_hbm, leaf_hbm, fresh_hbm,
    out_hbm, local_ref, bias_ref,
    parent_ref, pages_ref, owner_ref, pool_ref, rows_ref, block_ref, sems,
):
    leaf_rows, fresh_rows = leaf_hbm.shape[0], fresh_hbm.shape[0]
    pairs = [
        (pool_hbm, pool_ref),
        (parent_hbm, parent_ref),
        (pages_hbm, pages_ref),
        (owner_hbm, owner_ref),
        (leaf_hbm, local_ref.at[pl.ds(0, leaf_rows)]),
        (fresh_hbm, local_ref.at[pl.ds(leaf_rows, fresh_rows)]),
    ]
    fetches = [pltpu.make_async_copy(*pair, sems.at[i]) for i, pair in enumerate(pairs)]
    for fetch in fetches:
        fetch.start()
    node_count = pool_ref.shape[0] // (2 * page)
    copies, requests = out_hbm.shape[:2]
    fetches[0].wait()
    rows_ref[...] = pool_ref[...].astype(jnp.float32)
    root = [rows_ref[pl.ds(kind, page, stride=2)] for kind in range(2)]
    fetches[1].wait()

    def one(request, carry):
        mid = parent_ref[node_count + request] * (2 * page)
        for kind in range(2):
            chosen = rows_ref[pl.ds(mid + kind, page, stride=2)]
            block_ref[kind, request] = jnp.concatenate([root[kind], chosen], 0).astype(jnp.bfloat16)
        return carry

    lax.fori_loop(0, requests, one, 0, unroll=requests <= 8)
    sends = [
        pltpu.make_async_copy(block_ref.at[copy % 2], out_hbm.at[copy], sems.at[len(pairs) + copy])
        for copy in range(copies)
    ]
    for send in sends:
        send.start()

    fetches[2].wait()
    fetches[3].wait()
    mid = parent_ref[node_count + lax.axis_index("pool")]
    key = lax.broadcasted_iota(jnp.int32, bias_ref.shape, 1)
    stripe, is_mid = key // (2 * page), (key % (2 * page)) >= page
    offset = stripe - jnp.where(is_mid, owner_ref[mid], owner_ref[0])
    offset = jnp.where(offset < 0, offset + requests, offset)
    used = offset < jnp.where(is_mid, pages_ref[mid], pages_ref[0])
    bias_ref[...] = jnp.where(used, 0.0, MASKED)
    for copy in fetches[4:] + sends:
        copy.wait()


def hand_over_kernel(*refs):
    pass


def hand_over(cost, *arrays):
    anywhere = pl.BlockSpec(memory_space=pl.ANY)
    return pl.pallas_call(
        hand_over_kernel,
        out_shape=[jax.ShapeDtypeStruct(array.shape, array.dtype) for array in arrays],
        in_specs=[anywhere] * len(arrays),
        out_specs=[anywhere] * len(arrays),
        input_output_aliases={i: i for i in range(len(arrays))},
        compiler_params=pltpu.CompilerParams(vmem_limit_bytes=2**20),
        cost_estimate=cost,
    )(*arrays)


def scores_of(rows, keys):
    scores = lax.dot_general(rows, keys, (((1,), (1,)), ((), ())), preferred_element_type=jnp.float32)
    return scores * (LOG2_E * HEAD_SIZE ** (-0.5))


def weigh(weights, values):
    sums = dot(weights.astype(jnp.bfloat16), jnp.concatenate([values, jnp.ones_like(values)], 1))
    return sums[:, : values.shape[1]], sums[:, values.shape[1] :]


def own_kernel(leaf_len_ref, q_ref, *rest, page):
    local_refs = rest[:4]
    result_ref, level_ref, bias_ref, kf_ref, vf_ref = rest[4:]
    tokens, q_heads, dim = q_ref.shape
    group = q_heads // 4
    leaf_slots = bias_ref.shape[0] - 4 * tokens
    rank = lax.axis_index("tp")

    key = lax.broadcasted_iota(jnp.int32, (leaf_slots, dim), 0)
    bias_ref[0:leaf_slots] = jnp.where(key < leaf_len_ref[0] * page, 0.0, MASKED).astype(jnp.bfloat16)
    key = lax.broadcasted_iota(jnp.int32, (tokens, dim), 0)
    row = lax.broadcasted_iota(jnp.int32, (tokens, dim), 1)
    for step in range(4):
        seen = key <= row if step == 0 else jnp.full((tokens, dim), rank ^ step, jnp.int32) < rank
        bias_ref[leaf_slots + step * tokens : leaf_slots + (step + 1) * tokens] = jnp.where(
            seen, 0.0, MASKED
        ).astype(jnp.bfloat16)

    fresh_rows = local_refs[0].shape[0] - 2 * leaf_slots

    def fresh_source(out_row):
        head, kind, token = out_row // (2 * tokens), (out_row // tokens) % 2, out_row % tokens
        return token * 8 + head * 2 + kind

    fresh_pick = pick((fresh_rows, fresh_rows), fresh_source)
    for step in range(4):
        parts = dot(fresh_pick, local_refs[step][2 * leaf_slots :]).astype(jnp.bfloat16)
        for head in range(4):
            base = head * 2 * tokens
            kf_ref[head, step * tokens : (step + 1) * tokens] = parts[base : base + tokens]
            vf_ref[head, step * tokens : (step + 1) * tokens] = parts[base + tokens : base + 2 * tokens]

    chunk = 256
    half = chunk // 2
    leaf_pick = pick((chunk, chunk), lambda out_row: (out_row % half) * 2 + out_row // half)
    bias = bias_ref[...]
    token = lax.broadcasted_iota(jnp.int32, (tokens * group, dim), 0) // group
    column = lax.broadcasted_iota(jnp.int32, (tokens * group, dim), 1)
    own_row = jnp.where(token == column, 1.0, 0.0).astype(jnp.bfloat16)
    for step in range(4):
        head = rank ^ step
        leaf_k, leaf_v = [], []
        for piece in range(leaf_slots // half):
            parts = dot(leaf_pick, local_refs[step][piece * chunk : (piece + 1) * chunk]).astype(jnp.bfloat16)
            leaf_k.append(parts[:half])
            leaf_v.append(parts[half:])
        keys = jnp.concatenate([jnp.concatenate(leaf_k + [kf_ref[head]], 0), bias], 1)
        values = jnp.concatenate(leaf_v + [vf_ref[head]], 0)
        rows = q_ref[:, pl.ds(pl.multiple_of(head * group, group), group), :].reshape(tokens * group, dim)
        scores = scores_of(jnp.concatenate([rows, own_row], 1), keys)
        top = jnp.max(scores, axis=1, keepdims=True)
        sums, totals = weigh(jnp.exp2(scores - top), values)
        result_ref[step] = sums / totals
        level_ref[step] = jnp.log2(totals) + top


def blocks(a, b):
    zero = jnp.zeros_like(a)
    return jnp.concatenate([jnp.concatenate([a, zero], 1), jnp.concatenate([zero, b], 1)], 0)


def shared_kernel(q_ref, bias_ref, other_ref, level_ref, mine_ref, theirs_ref, out_hbm, stage_ref, sems):
    tokens, q_heads, dim = q_ref.shape
    group = q_heads // 4
    shared_keys = bias_ref.shape[1]
    rank = lax.axis_index("tp")
    has_keys = rank % 2 == 0
    bias = bias_ref[0:1]
    places = [pl.ds(pl.multiple_of((rank ^ step) * group, group), group) for step in range(4)]
    pairs = ((0, 1), (2, 3))
    ones = jnp.ones((shared_keys, dim), jnp.bfloat16)
    ones = blocks(ones, ones)

    def above_level(pair):
        keys, rows, levels = [], [], []
        for step in pair:
            head = rank ^ step
            keys.append(jnp.where(has_keys, mine_ref[head], theirs_ref[head]).reshape(shared_keys, dim))
            rows.append(q_ref[:, places[step], :].reshape(tokens * group, dim))
            levels += [bias - level_ref[step]] if shared_keys == dim else [
                bias - jnp.concatenate([level_ref[step]] * (shared_keys // dim), 1)
            ]
        return scores_of(jnp.concatenate(rows, 1), blocks(*keys)) + jnp.concatenate(levels, 1)

    def weighted(pair, weights):
        values = []
        for step in pair:
            head = rank ^ step
            values.append(jnp.where(has_keys, theirs_ref[head], mine_ref[head]).reshape(shared_keys, dim))
        weights = weights.astype(jnp.bfloat16)
        return dot(weights, blocks(*values)), dot(weights, ones)

    def write(pair, result):
        copies = []
        for place, step in enumerate(pair):
            part = result[:, place * dim : (place + 1) * dim]
            stage_ref[step] = part.astype(jnp.bfloat16).reshape(tokens, group, dim)
            copies.append(pltpu.make_async_copy(stage_ref.at[step], out_hbm.at[:, places[step]], sems.at[step]))
            copies[-1].start()
        return copies

    def other(pair):
        return jnp.concatenate([other_ref[step] for step in pair], 1)

    scores = [above_level(pair) for pair in pairs]
    writes = []
    for pair, score in zip(pairs, scores):
        sums, totals = weighted(pair, jnp.exp2(score))
        writes += write(pair, (sums + other(pair)) / (totals + 1.0))
    too_high = jnp.max(functools.reduce(jnp.maximum, scores)) > 100.0
    for copy in writes:
        copy.wait()

    @pl.when(too_high)
    def _():
        for pair in pairs:
            score = above_level(pair)
            tops = [
                jnp.maximum(jnp.max(score[:, i * shared_keys : (i + 1) * shared_keys], axis=1, keepdims=True), 0.0)
                for i in range(2)
            ]
            wide = [jnp.broadcast_to(top, (tokens * group, shared_keys)) for top in tops]
            sums, totals = weighted(pair, jnp.exp2(score - jnp.concatenate(wide, 1)))
            rest = jnp.concatenate([jnp.broadcast_to(jnp.exp2(-top), (tokens * group, dim)) for top in tops], 1)
            for copy in write(pair, (sums + other(pair) * rest) / (totals + rest)):
                copy.wait()


def per_device(queries, fresh, pool, leaf, parent, node_pages, node_owner, leaf_len):
    tp = lax.axis_size("tp")
    stripes = lax.axis_size("pool")
    shared_count, _, page, _, _, dim = pool.shape
    tokens, q_heads, _ = queries.shape
    vmem = pl.BlockSpec(memory_space=pltpu.VMEM)
    swap = lambda array, bit: lax.ppermute(array, "tp", [(i, i ^ bit) for i in range(tp)])
    hbm = pl.BlockSpec(memory_space=pltpu.HBM)

    pool_rows = pool.reshape(-1, dim)
    leaf_rows = leaf.reshape(-1, dim)
    fresh_rows = fresh.reshape(-1, dim)
    operands = (parent, node_pages, node_owner, pool_rows, leaf_rows, fresh_rows)
    sent, local_0, bias = pl.pallas_call(
        functools.partial(select_kernel, page),
        out_shape=[
            jax.ShapeDtypeStruct((tp, stripes, 2 * page, dim), jnp.bfloat16),
            jax.ShapeDtypeStruct((leaf_rows.shape[0] + fresh_rows.shape[0], dim), jnp.bfloat16),
            jax.ShapeDtypeStruct((8, stripes * 2 * page), jnp.float32),
        ],
        in_specs=[hbm] * 6,
        out_specs=[hbm, vmem, vmem],
        scratch_shapes=[
            pltpu.SMEM(parent.shape, jnp.int32),
            pltpu.SMEM(node_pages.shape, jnp.int32),
            pltpu.SMEM(node_owner.shape, jnp.int32),
            pltpu.VMEM(pool_rows.shape, jnp.bfloat16),
            pltpu.VMEM(pool_rows.shape, jnp.float32),
            pltpu.VMEM((2, stripes, 2 * page, dim), jnp.bfloat16),
            pltpu.SemaphoreType.DMA((6 + tp,)),
        ],
        compiler_params=pltpu.CompilerParams(vmem_limit_bytes=16 * 2**20),
        cost_estimate=LONG,
    )(*[pltpu.with_memory_space_constraint(operand, pltpu.HBM) for operand in operands])
    local_2 = swap(local_0, 2)
    mine = lax.all_to_all(
        sent.reshape(tp * stripes, 2 * page, dim), ("tp", "pool"), split_axis=0, concat_axis=0, tiled=True
    ).reshape(tp, stripes, 2 * page, dim)
    local_0, local_2 = hand_over(LONG, local_0, local_2)
    local_1, local_3 = swap(local_0, 1), swap(local_2, 1)

    rows = tokens * q_heads // tp
    other, level = pl.pallas_call(
        functools.partial(own_kernel, page=page),
        out_shape=[jax.ShapeDtypeStruct((tp, rows, dim), jnp.float32)] * 2,
        in_specs=[pl.BlockSpec(memory_space=pltpu.SMEM)] + [vmem] * 5,
        out_specs=[vmem] * 2,
        scratch_shapes=[pltpu.VMEM((leaf.shape[1] + tp * tokens, dim), jnp.bfloat16)]
        + [pltpu.VMEM((tp, tp * tokens, dim), jnp.bfloat16)] * 2,
        compiler_params=pltpu.CompilerParams(vmem_limit_bytes=24 * 2**20),
        cost_estimate=SHORT,
    )(leaf_len, queries, local_0, local_1, local_2, local_3)
    mine, level = hand_over(SHORT, mine, level)
    theirs = swap(mine, 1)
    return pl.pallas_call(
        shared_kernel,
        out_shape=jax.ShapeDtypeStruct(queries.shape, jnp.bfloat16),
        in_specs=[vmem] * 6,
        out_specs=hbm,
        scratch_shapes=[
            pltpu.VMEM((tp, tokens, q_heads // tp, dim), jnp.bfloat16),
            pltpu.SemaphoreType.DMA((tp,)),
        ],
        compiler_params=pltpu.CompilerParams(vmem_limit_bytes=(24 if stripes <= 8 else 48) * 2**20),
    )(queries, bias, other, level, mine, theirs)


def solution(mesh):
    return jax.shard_map(
        per_device,
        mesh=mesh,
        in_specs=(
            P(("pool", "tp"), None, None),
            P(("pool", "tp"), None, None, None),
            P(None, "pool", None, "tp", None, None),
            P("pool", None, "tp", None, None),
            P(),
            P(),
            P(),
            P("pool"),
        ),
        out_specs=P(("pool", "tp"), None, None),
        check_vma=False,
    )
```

```python
import functools

import jax
import jax.numpy as jnp
from jax import lax
from jax.experimental import pallas as pl
from jax.experimental.pallas import tpu as pltpu
from jax.sharding import PartitionSpec as P

LOG2_E = 1.4426950408889634
MASKED = -1e30
LONG = pl.CostEstimate(flops=5 * 10**10, bytes_accessed=10**6, transcendentals=0)
SHORT = pl.CostEstimate(flops=10**6, bytes_accessed=10**5, transcendentals=0)


def pick(shape, source_row):
    row = lax.broadcasted_iota(jnp.int32, shape, 0)
    column = lax.broadcasted_iota(jnp.int32, shape, 1)
    return jnp.where(column == source_row(row), 1.0, 0.0).astype(jnp.bfloat16)


def dot(a, b):
    return lax.dot_general(a, b, (((1,), (0,)), ((), ())), preferred_element_type=jnp.float32)


def select_kernel(
    page, parent_hbm, pages_hbm, owner_hbm, pool_hbm, leaf_hbm, fresh_hbm,
    out_hbm, local_ref, bias_ref,
    parent_ref, pages_ref, owner_ref, pool_ref, rows_ref, block_ref, sems,
):
    leaf_rows, fresh_rows = leaf_hbm.shape[0], fresh_hbm.shape[0]
    pairs = [
        (pool_hbm, pool_ref),
        (parent_hbm, parent_ref),
        (pages_hbm, pages_ref),
        (owner_hbm, owner_ref),
        (leaf_hbm, local_ref.at[pl.ds(0, leaf_rows)]),
        (fresh_hbm, local_ref.at[pl.ds(leaf_rows, fresh_rows)]),
    ]
    fetches = [pltpu.make_async_copy(*pair, sems.at[i]) for i, pair in enumerate(pairs)]
    for fetch in fetches:
        fetch.start()
    node_count = pool_ref.shape[0] // (2 * page)
    copies, requests = out_hbm.shape[:2]
    fetches[0].wait()
    rows_ref[...] = pool_ref[...].astype(jnp.float32)
    root = [rows_ref[pl.ds(kind, page, stride=2)] for kind in range(2)]
    fetches[1].wait()

    def one(request, carry):
        mid = parent_ref[node_count + request] * (2 * page)
        for kind in range(2):
            chosen = rows_ref[pl.ds(mid + kind, page, stride=2)]
            block_ref[kind, request] = jnp.concatenate([root[kind], chosen], 0).astype(jnp.bfloat16)
        return carry

    lax.fori_loop(0, requests, one, 0, unroll=requests <= 8)
    sends = [
        pltpu.make_async_copy(block_ref.at[copy % 2], out_hbm.at[copy], sems.at[len(pairs) + copy])
        for copy in range(copies)
    ]
    for send in sends:
        send.start()

    fetches[2].wait()
    fetches[3].wait()
    mid = parent_ref[node_count + lax.axis_index("pool")]
    key = lax.broadcasted_iota(jnp.int32, bias_ref.shape, 1)
    stripe, is_mid = key // (2 * page), (key % (2 * page)) >= page
    offset = stripe - jnp.where(is_mid, owner_ref[mid], owner_ref[0])
    offset = jnp.where(offset < 0, offset + requests, offset)
    used = offset < jnp.where(is_mid, pages_ref[mid], pages_ref[0])
    bias_ref[...] = jnp.where(used, 0.0, MASKED)
    for copy in fetches[4:] + sends:
        copy.wait()


def hand_over_kernel(*refs):
    pass


def hand_over(cost, *arrays):
    anywhere = pl.BlockSpec(memory_space=pl.ANY)
    return pl.pallas_call(
        hand_over_kernel,
        out_shape=[jax.ShapeDtypeStruct(array.shape, array.dtype) for array in arrays],
        in_specs=[anywhere] * len(arrays),
        out_specs=[anywhere] * len(arrays),
        input_output_aliases={i: i for i in range(len(arrays))},
        compiler_params=pltpu.CompilerParams(vmem_limit_bytes=2**20),
        cost_estimate=cost,
    )(*arrays)


def scores_of(rows, keys):
    scores = lax.dot_general(rows, keys, (((1,), (1,)), ((), ())), preferred_element_type=jnp.float32)
    return scores * (LOG2_E * 128 ** (-0.5))


def weigh(weights, values):
    sums = dot(weights.astype(jnp.bfloat16), jnp.concatenate([values, jnp.ones_like(values)], 1))
    return sums[:, : values.shape[1]], sums[:, values.shape[1] :]


def own_kernel(leaf_len_ref, q_ref, *rest, page):
    local_refs = rest[:4]
    result_ref, level_ref, bias_ref, kf_ref, vf_ref = rest[4:]
    tokens, q_heads, dim = q_ref.shape
    group = q_heads // 4
    leaf_slots = bias_ref.shape[0] - 4 * tokens
    rank = lax.axis_index("tp")

    key = lax.broadcasted_iota(jnp.int32, (leaf_slots, dim), 0)
    bias_ref[0:leaf_slots] = jnp.where(key < leaf_len_ref[0] * page, 0.0, MASKED).astype(jnp.bfloat16)
    key = lax.broadcasted_iota(jnp.int32, (tokens, dim), 0)
    row = lax.broadcasted_iota(jnp.int32, (tokens, dim), 1)
    for step in range(4):
        seen = key <= row if step == 0 else jnp.full((tokens, dim), rank ^ step, jnp.int32) < rank
        bias_ref[leaf_slots + step * tokens : leaf_slots + (step + 1) * tokens] = jnp.where(
            seen, 0.0, MASKED
        ).astype(jnp.bfloat16)

    fresh_rows = local_refs[0].shape[0] - 2 * leaf_slots

    def fresh_source(out_row):
        head, kind, token = out_row // (2 * tokens), (out_row // tokens) % 2, out_row % tokens
        return token * 8 + head * 2 + kind

    fresh_pick = pick((fresh_rows, fresh_rows), fresh_source)
    for step in range(4):
        parts = dot(fresh_pick, local_refs[step][2 * leaf_slots :]).astype(jnp.bfloat16)
        for head in range(4):
            base = head * 2 * tokens
            kf_ref[head, step * tokens : (step + 1) * tokens] = parts[base : base + tokens]
            vf_ref[head, step * tokens : (step + 1) * tokens] = parts[base + tokens : base + 2 * tokens]

    chunk = 256
    half = chunk // 2
    leaf_pick = pick((chunk, chunk), lambda out_row: (out_row % half) * 2 + out_row // half)
    bias = bias_ref[...]
    token = lax.broadcasted_iota(jnp.int32, (tokens * group, dim), 0) // group
    column = lax.broadcasted_iota(jnp.int32, (tokens * group, dim), 1)
    own_row = jnp.where(token == column, 1.0, 0.0).astype(jnp.bfloat16)
    for step in range(4):
        head = rank ^ step
        leaf_k, leaf_v = [], []
        for piece in range(leaf_slots // half):
            parts = dot(leaf_pick, local_refs[step][piece * chunk : (piece + 1) * chunk]).astype(jnp.bfloat16)
            leaf_k.append(parts[:half])
            leaf_v.append(parts[half:])
        keys = jnp.concatenate([jnp.concatenate(leaf_k + [kf_ref[head]], 0), bias], 1)
        values = jnp.concatenate(leaf_v + [vf_ref[head]], 0)
        rows = q_ref[:, pl.ds(pl.multiple_of(head * group, group), group), :].reshape(tokens * group, dim)
        scores = scores_of(jnp.concatenate([rows, own_row], 1), keys)
        top = jnp.max(scores, axis=1, keepdims=True)
        sums, totals = weigh(jnp.exp2(scores - top), values)
        result_ref[step] = sums / totals
        level_ref[step] = jnp.log2(totals) + top


def shared_kernel(q_ref, bias_ref, other_ref, level_ref, mine_ref, theirs_ref, out_hbm, stage_ref, sems):
    tokens, q_heads, dim = q_ref.shape
    group = q_heads // 4
    shared_keys = bias_ref.shape[1]
    rank = lax.axis_index("tp")
    has_keys = rank % 2 == 0
    bias = bias_ref[0:1]
    places = [pl.ds(pl.multiple_of((rank ^ step) * group, group), group) for step in range(4)]
    part = tokens // 2
    parts = [(step, half) for step in range(4) for half in range(2)]

    def rows_of(ref, step, half):
        return ref[step, half * part * group : (half + 1) * part * group]

    def above_level(step, half):
        head = rank ^ step
        keys = jnp.where(has_keys, mine_ref[head], theirs_ref[head]).reshape(shared_keys, dim)
        rows = q_ref[half * part : (half + 1) * part, places[step], :].reshape(part * group, dim)
        level = rows_of(level_ref, step, half)
        return scores_of(rows, keys) + bias - jnp.concatenate([level] * (shared_keys // dim), 1)

    def weighted(step, weights):
        head = rank ^ step
        values = jnp.where(has_keys, theirs_ref[head], mine_ref[head]).reshape(shared_keys, dim)
        return weigh(weights, values)

    def write(step, half, result):
        tile = slice(half * part, (half + 1) * part)
        stage_ref[step, tile] = result.astype(jnp.bfloat16).reshape(part, group, dim)
        copy = pltpu.make_async_copy(stage_ref.at[step, tile], out_hbm.at[tile, places[step]], sems.at[2 * step + half])
        copy.start()
        return copy

    ahead = 2
    scores = [above_level(*parts[i]) for i in range(ahead)]
    highest = functools.reduce(jnp.maximum, scores)
    writes = []
    for i, (step, half) in enumerate(parts):
        if i + ahead < len(parts):
            scores.append(above_level(*parts[i + ahead]))
            highest = jnp.maximum(highest, scores[-1])
        sums, totals = weighted(step, jnp.exp2(scores[i]))
        writes.append(write(step, half, (sums + rows_of(other_ref, step, half)) / (totals + 1.0)))
    too_high = jnp.max(highest) > 100.0
    for copy in writes:
        copy.wait()

    @pl.when(too_high)
    def _():
        for step, half in parts:
            scores = above_level(step, half)
            top = jnp.maximum(jnp.max(scores, axis=1, keepdims=True), 0.0)
            sums, totals = weighted(step, jnp.exp2(scores - top))
            other = jnp.exp2(-top)
            write(step, half, (sums + rows_of(other_ref, step, half) * other) / (totals + other)).wait()


def per_device(queries, fresh, pool, leaf, parent, node_pages, node_owner, leaf_len):
    tp = lax.axis_size("tp")
    stripes = lax.axis_size("pool")
    shared_count, _, page, _, _, dim = pool.shape
    tokens, q_heads, _ = queries.shape
    vmem = pl.BlockSpec(memory_space=pltpu.VMEM)
    swap = lambda array, bit: lax.ppermute(array, "tp", [(i, i ^ bit) for i in range(tp)])
    hbm = pl.BlockSpec(memory_space=pltpu.HBM)

    pool_rows = pool.reshape(-1, dim)
    leaf_rows = leaf.reshape(-1, dim)
    fresh_rows = fresh.reshape(-1, dim)
    operands = (parent, node_pages, node_owner, pool_rows, leaf_rows, fresh_rows)
    sent, local_0, bias = pl.pallas_call(
        functools.partial(select_kernel, page),
        out_shape=[
            jax.ShapeDtypeStruct((tp, stripes, 2 * page, dim), jnp.bfloat16),
            jax.ShapeDtypeStruct((leaf_rows.shape[0] + fresh_rows.shape[0], dim), jnp.bfloat16),
            jax.ShapeDtypeStruct((8, stripes * 2 * page), jnp.float32),
        ],
        in_specs=[hbm] * 6,
        out_specs=[hbm, vmem, vmem],
        scratch_shapes=[
            pltpu.SMEM(parent.shape, jnp.int32),
            pltpu.SMEM(node_pages.shape, jnp.int32),
            pltpu.SMEM(node_owner.shape, jnp.int32),
            pltpu.VMEM(pool_rows.shape, jnp.bfloat16),
            pltpu.VMEM(pool_rows.shape, jnp.float32),
            pltpu.VMEM((2, stripes, 2 * page, dim), jnp.bfloat16),
            pltpu.SemaphoreType.DMA((6 + tp,)),
        ],
        compiler_params=pltpu.CompilerParams(vmem_limit_bytes=16 * 2**20),
        cost_estimate=LONG,
    )(*[pltpu.with_memory_space_constraint(operand, pltpu.HBM) for operand in operands])
    local_2 = swap(local_0, 2)
    mine = lax.all_to_all(
        sent.reshape(tp * stripes, 2 * page, dim), ("tp", "pool"), split_axis=0, concat_axis=0, tiled=True
    ).reshape(tp, stripes, 2 * page, dim)
    local_0, local_2 = hand_over(LONG, local_0, local_2)
    local_1, local_3 = swap(local_0, 1), swap(local_2, 1)

    rows = tokens * q_heads // tp
    other, level = pl.pallas_call(
        functools.partial(own_kernel, page=page),
        out_shape=[jax.ShapeDtypeStruct((tp, rows, dim), jnp.float32)] * 2,
        in_specs=[pl.BlockSpec(memory_space=pltpu.SMEM)] + [vmem] * 5,
        out_specs=[vmem] * 2,
        scratch_shapes=[pltpu.VMEM((leaf.shape[1] + tp * tokens, dim), jnp.bfloat16)]
        + [pltpu.VMEM((tp, tp * tokens, dim), jnp.bfloat16)] * 2,
        compiler_params=pltpu.CompilerParams(vmem_limit_bytes=24 * 2**20),
        cost_estimate=SHORT,
    )(leaf_len, queries, local_0, local_1, local_2, local_3)
    mine, level = hand_over(SHORT, mine, level)
    theirs = swap(mine, 1)
    return pl.pallas_call(
        shared_kernel,
        out_shape=jax.ShapeDtypeStruct(queries.shape, jnp.bfloat16),
        in_specs=[vmem] * 6,
        out_specs=hbm,
        scratch_shapes=[
            pltpu.VMEM((tp, tokens, q_heads // tp, dim), jnp.bfloat16),
            pltpu.SemaphoreType.DMA((2 * tp,)),
        ],
        compiler_params=pltpu.CompilerParams(vmem_limit_bytes=(24 if stripes <= 8 else 48) * 2**20),
    )(queries, bias, other, level, mine, theirs)


def solution(mesh):
    return jax.shard_map(
        per_device,
        mesh=mesh,
        in_specs=(
            P(("pool", "tp"), None, None),
            P(("pool", "tp"), None, None, None),
            P(None, "pool", None, "tp", None, None),
            P("pool", None, "tp", None, None),
            P(),
            P(),
            P(),
            P("pool"),
        ),
        out_specs=P(("pool", "tp"), None, None),
        check_vma=False,
    )
```

```python
import functools

import jax
import jax.numpy as jnp
from jax import lax
from jax.experimental import pallas as pl
from jax.experimental.pallas import tpu as pltpu
from jax.sharding import PartitionSpec as P

LOG2_E = 1.4426950408889634
MASKED = -1e30
LONG = pl.CostEstimate(flops=5 * 10**10, bytes_accessed=10**6, transcendentals=0)
SHORT = pl.CostEstimate(flops=10**6, bytes_accessed=10**5, transcendentals=0)


def pick(shape, source_row):
    row = lax.broadcasted_iota(jnp.int32, shape, 0)
    column = lax.broadcasted_iota(jnp.int32, shape, 1)
    return jnp.where(column == source_row(row), 1.0, 0.0).astype(jnp.bfloat16)


def dot(a, b):
    return lax.dot_general(a, b, (((1,), (0,)), ((), ())), preferred_element_type=jnp.float32)


def select_kernel(
    page, parent_hbm, pages_hbm, owner_hbm, pool_hbm, leaf_hbm, fresh_hbm,
    out_hbm, local_ref, bias_ref,
    parent_ref, pages_ref, owner_ref, pool_ref, rows_ref, block_ref, sems,
):
    leaf_rows, fresh_rows = leaf_hbm.shape[0], fresh_hbm.shape[0]
    pairs = [
        (pool_hbm, pool_ref),
        (parent_hbm, parent_ref),
        (pages_hbm, pages_ref),
        (owner_hbm, owner_ref),
        (leaf_hbm, local_ref.at[pl.ds(0, leaf_rows)]),
        (fresh_hbm, local_ref.at[pl.ds(leaf_rows, fresh_rows)]),
    ]
    fetches = [pltpu.make_async_copy(*pair, sems.at[i]) for i, pair in enumerate(pairs)]
    for fetch in fetches:
        fetch.start()
    node_count = pool_ref.shape[0] // (2 * page)
    copies, requests = out_hbm.shape[:2]
    fetches[0].wait()
    rows_ref[...] = pool_ref[...].astype(jnp.float32)
    root = [rows_ref[pl.ds(kind, page, stride=2)] for kind in range(2)]
    fetches[1].wait()

    def one(request, carry):
        mid = parent_ref[node_count + request] * (2 * page)
        for kind in range(2):
            chosen = rows_ref[pl.ds(mid + kind, page, stride=2)]
            block_ref[kind, request] = jnp.concatenate([root[kind], chosen], 0).astype(jnp.bfloat16)
        return carry

    lax.fori_loop(0, requests, one, 0, unroll=requests <= 8)
    sends = [
        pltpu.make_async_copy(block_ref.at[copy % 2], out_hbm.at[copy], sems.at[len(pairs) + copy])
        for copy in range(copies)
    ]
    for send in sends:
        send.start()

    fetches[2].wait()
    fetches[3].wait()
    mid = parent_ref[node_count + lax.axis_index("pool")]
    key = lax.broadcasted_iota(jnp.int32, bias_ref.shape, 1)
    stripe, is_mid = key // (2 * page), (key % (2 * page)) >= page
    offset = stripe - jnp.where(is_mid, owner_ref[mid], owner_ref[0])
    offset = jnp.where(offset < 0, offset + requests, offset)
    used = offset < jnp.where(is_mid, pages_ref[mid], pages_ref[0])
    bias_ref[...] = jnp.where(used, 0.0, MASKED)
    for copy in fetches[4:] + sends:
        copy.wait()


def hand_over_kernel(*refs):
    pass


def hand_over(cost, *arrays):
    anywhere = pl.BlockSpec(memory_space=pl.ANY)
    return pl.pallas_call(
        hand_over_kernel,
        out_shape=[jax.ShapeDtypeStruct(array.shape, array.dtype) for array in arrays],
        in_specs=[anywhere] * len(arrays),
        out_specs=[anywhere] * len(arrays),
        input_output_aliases={i: i for i in range(len(arrays))},
        compiler_params=pltpu.CompilerParams(vmem_limit_bytes=2**20),
        cost_estimate=cost,
    )(*arrays)


def scores_of(rows, keys):
    scores = lax.dot_general(rows, keys, (((1,), (1,)), ((), ())), preferred_element_type=jnp.float32)
    return scores * (LOG2_E * 128 ** (-0.5))


def over(sums, totals):
    inverse = pl.reciprocal(totals, approx=True)
    return sums * (inverse * (2.0 - totals * inverse))


def weigh(weights, values):
    sums = dot(weights.astype(jnp.bfloat16), jnp.concatenate([values, jnp.ones_like(values)], 1))
    return sums[:, : values.shape[1]], sums[:, values.shape[1] :]


def own_kernel(leaf_len_ref, q_ref, *rest, page):
    local_refs = rest[:4]
    result_ref, level_ref, bias_ref, kf_ref, vf_ref = rest[4:]
    tokens, q_heads, dim = q_ref.shape
    group = q_heads // 4
    leaf_slots = bias_ref.shape[0] - 4 * tokens
    rank = lax.axis_index("tp")

    key = lax.broadcasted_iota(jnp.int32, (leaf_slots, dim), 0)
    bias_ref[0:leaf_slots] = jnp.where(key < leaf_len_ref[0] * page, 0.0, MASKED).astype(jnp.bfloat16)
    key = lax.broadcasted_iota(jnp.int32, (tokens, dim), 0)
    row = lax.broadcasted_iota(jnp.int32, (tokens, dim), 1)
    for step in range(4):
        seen = key <= row if step == 0 else jnp.full((tokens, dim), rank ^ step, jnp.int32) < rank
        bias_ref[leaf_slots + step * tokens : leaf_slots + (step + 1) * tokens] = jnp.where(
            seen, 0.0, MASKED
        ).astype(jnp.bfloat16)

    fresh_rows = local_refs[0].shape[0] - 2 * leaf_slots

    def fresh_source(out_row):
        head, kind, token = out_row // (2 * tokens), (out_row // tokens) % 2, out_row % tokens
        return token * 8 + head * 2 + kind

    fresh_pick = pick((fresh_rows, fresh_rows), fresh_source)
    for step in range(4):
        parts = dot(fresh_pick, local_refs[step][2 * leaf_slots :]).astype(jnp.bfloat16)
        for head in range(4):
            base = head * 2 * tokens
            kf_ref[head, step * tokens : (step + 1) * tokens] = parts[base : base + tokens]
            vf_ref[head, step * tokens : (step + 1) * tokens] = parts[base + tokens : base + 2 * tokens]

    chunk = 256
    half = chunk // 2
    leaf_pick = pick((chunk, chunk), lambda out_row: (out_row % half) * 2 + out_row // half)
    bias = bias_ref[...]
    token = lax.broadcasted_iota(jnp.int32, (tokens * group, dim), 0) // group
    column = lax.broadcasted_iota(jnp.int32, (tokens * group, dim), 1)
    own_row = jnp.where(token == column, 1.0, 0.0).astype(jnp.bfloat16)
    for step in range(4):
        head = rank ^ step
        leaf_k, leaf_v = [], []
        for piece in range(leaf_slots // half):
            parts = dot(leaf_pick, local_refs[step][piece * chunk : (piece + 1) * chunk]).astype(jnp.bfloat16)
            leaf_k.append(parts[:half])
            leaf_v.append(parts[half:])
        keys = jnp.concatenate([jnp.concatenate(leaf_k + [kf_ref[head]], 0), bias], 1)
        values = jnp.concatenate(leaf_v + [vf_ref[head]], 0)
        rows = q_ref[:, pl.ds(pl.multiple_of(head * group, group), group), :].reshape(tokens * group, dim)
        scores = scores_of(jnp.concatenate([rows, own_row], 1), keys)
        top = jnp.max(scores, axis=1, keepdims=True)
        sums, totals = weigh(jnp.exp2(scores - top), values)
        result_ref[step] = sums / totals
        level_ref[step] = jnp.log2(totals) + top


def shared_kernel(q_ref, bias_ref, other_ref, level_ref, mine_ref, theirs_ref, out_hbm, stage_ref, sems):
    tokens, q_heads, dim = q_ref.shape
    group = q_heads // 4
    shared_keys = bias_ref.shape[1]
    rank = lax.axis_index("tp")
    has_keys = rank % 2 == 0
    bias = bias_ref[0:1]
    places = [pl.ds(pl.multiple_of((rank ^ step) * group, group), group) for step in range(4)]

    def above_level(step):
        head = rank ^ step
        keys = jnp.where(has_keys, mine_ref[head], theirs_ref[head]).reshape(shared_keys, dim)
        scores = scores_of(q_ref[:, places[step], :].reshape(tokens * group, dim), keys)
        return scores + bias - jnp.concatenate([level_ref[step]] * (shared_keys // dim), 1)

    def weighted(step, weights):
        head = rank ^ step
        values = jnp.where(has_keys, theirs_ref[head], mine_ref[head]).reshape(shared_keys, dim)
        return weigh(weights, values)

    def write(step, result):
        stage_ref[step] = result.astype(jnp.bfloat16).reshape(tokens, group, dim)
        copy = pltpu.make_async_copy(stage_ref.at[step], out_hbm.at[:, places[step]], sems.at[step])
        copy.start()
        return copy

    scores = [above_level(step) for step in range(4)]
    writes, weights = [], []
    for step in range(4):
        weights.append(jnp.exp2(scores[step]).astype(jnp.bfloat16))
        sums, totals = weighted(step, weights[-1])
        writes.append(write(step, over(sums + other_ref[step], totals + 1.0)))
    too_high = jnp.max(functools.reduce(jnp.maximum, weights).astype(jnp.float32)) > 2.0**100
    for copy in writes:
        copy.wait()

    @pl.when(too_high)
    def _():
        for step in range(4):
            scores = above_level(step)
            top = jnp.maximum(jnp.max(scores, axis=1, keepdims=True), 0.0)
            sums, totals = weighted(step, jnp.exp2(scores - top))
            other = jnp.exp2(-top)
            write(step, over(sums + other_ref[step] * other, totals + other)).wait()


def per_device(queries, fresh, pool, leaf, parent, node_pages, node_owner, leaf_len):
    tp = lax.axis_size("tp")
    stripes = lax.axis_size("pool")
    shared_count, _, page, _, _, dim = pool.shape
    tokens, q_heads, _ = queries.shape
    vmem = pl.BlockSpec(memory_space=pltpu.VMEM)
    swap = lambda array, bit: lax.ppermute(array, "tp", [(i, i ^ bit) for i in range(tp)])
    hbm = pl.BlockSpec(memory_space=pltpu.HBM)

    pool_rows = pool.reshape(-1, dim)
    leaf_rows = leaf.reshape(-1, dim)
    fresh_rows = fresh.reshape(-1, dim)
    operands = (parent, node_pages, node_owner, pool_rows, leaf_rows, fresh_rows)
    sent, local_0, bias = pl.pallas_call(
        functools.partial(select_kernel, page),
        out_shape=[
            jax.ShapeDtypeStruct((tp, stripes, 2 * page, dim), jnp.bfloat16),
            jax.ShapeDtypeStruct((leaf_rows.shape[0] + fresh_rows.shape[0], dim), jnp.bfloat16),
            jax.ShapeDtypeStruct((8, stripes * 2 * page), jnp.float32),
        ],
        in_specs=[hbm] * 6,
        out_specs=[hbm, vmem, vmem],
        scratch_shapes=[
            pltpu.SMEM(parent.shape, jnp.int32),
            pltpu.SMEM(node_pages.shape, jnp.int32),
            pltpu.SMEM(node_owner.shape, jnp.int32),
            pltpu.VMEM(pool_rows.shape, jnp.bfloat16),
            pltpu.VMEM(pool_rows.shape, jnp.float32),
            pltpu.VMEM((2, stripes, 2 * page, dim), jnp.bfloat16),
            pltpu.SemaphoreType.DMA((6 + tp,)),
        ],
        compiler_params=pltpu.CompilerParams(vmem_limit_bytes=16 * 2**20),
        cost_estimate=LONG,
    )(*[pltpu.with_memory_space_constraint(operand, pltpu.HBM) for operand in operands])
    local_2 = swap(local_0, 2)
    mine = lax.all_to_all(
        sent.reshape(tp * stripes, 2 * page, dim), ("tp", "pool"), split_axis=0, concat_axis=0, tiled=True
    ).reshape(tp, stripes, 2 * page, dim)
    local_0, local_2 = hand_over(LONG, local_0, local_2)
    local_1, local_3 = swap(local_0, 1), swap(local_2, 1)

    rows = tokens * q_heads // tp
    other, level = pl.pallas_call(
        functools.partial(own_kernel, page=page),
        out_shape=[jax.ShapeDtypeStruct((tp, rows, dim), jnp.float32)] * 2,
        in_specs=[pl.BlockSpec(memory_space=pltpu.SMEM)] + [vmem] * 5,
        out_specs=[vmem] * 2,
        scratch_shapes=[pltpu.VMEM((leaf.shape[1] + tp * tokens, dim), jnp.bfloat16)]
        + [pltpu.VMEM((tp, tp * tokens, dim), jnp.bfloat16)] * 2,
        compiler_params=pltpu.CompilerParams(vmem_limit_bytes=24 * 2**20),
        cost_estimate=SHORT,
    )(leaf_len, queries, local_0, local_1, local_2, local_3)
    mine, level = hand_over(SHORT, mine, level)
    theirs = swap(mine, 1)
    return pl.pallas_call(
        shared_kernel,
        out_shape=jax.ShapeDtypeStruct(queries.shape, jnp.bfloat16),
        in_specs=[vmem] * 6,
        out_specs=hbm,
        scratch_shapes=[
            pltpu.VMEM((tp, tokens, q_heads // tp, dim), jnp.bfloat16),
            pltpu.SemaphoreType.DMA((tp,)),
        ],
        compiler_params=pltpu.CompilerParams(vmem_limit_bytes=(24 if stripes <= 8 else 48) * 2**20),
    )(queries, bias, other, level, mine, theirs)


def solution(mesh):
    return jax.shard_map(
        per_device,
        mesh=mesh,
        in_specs=(
            P(("pool", "tp"), None, None),
            P(("pool", "tp"), None, None, None),
            P(None, "pool", None, "tp", None, None),
            P("pool", None, "tp", None, None),
            P(),
            P(),
            P(),
            P("pool"),
        ),
        out_specs=P(("pool", "tp"), None, None),
        check_vma=False,
    )
```

```python
import functools

import jax
import jax.numpy as jnp
from jax import lax
from jax.experimental import pallas as pl
from jax.experimental.pallas import tpu as pltpu
from jax.sharding import PartitionSpec as P

LOG2_E = 1.4426950408889634
MASKED = -1e30
LONG = pl.CostEstimate(flops=5 * 10**10, bytes_accessed=10**6, transcendentals=0)
SHORT = pl.CostEstimate(flops=10**6, bytes_accessed=10**5, transcendentals=0)


def pick(shape, source_row):
    row = lax.broadcasted_iota(jnp.int32, shape, 0)
    column = lax.broadcasted_iota(jnp.int32, shape, 1)
    return jnp.where(column == source_row(row), 1.0, 0.0).astype(jnp.bfloat16)


def dot(a, b):
    return lax.dot_general(a, b, (((1,), (0,)), ((), ())), preferred_element_type=jnp.float32)


def select_kernel(
    page, parent_hbm, pages_hbm, owner_hbm, pool_hbm, leaf_hbm, fresh_hbm,
    out_hbm, local_ref, bias_ref,
    parent_ref, pages_ref, owner_ref, pool_ref, rows_ref, block_ref, sems,
):
    leaf_rows, fresh_rows = leaf_hbm.shape[0], fresh_hbm.shape[0]
    pairs = [
        (pool_hbm, pool_ref),
        (parent_hbm, parent_ref),
        (pages_hbm, pages_ref),
        (owner_hbm, owner_ref),
        (leaf_hbm, local_ref.at[pl.ds(0, leaf_rows)]),
        (fresh_hbm, local_ref.at[pl.ds(leaf_rows, fresh_rows)]),
    ]
    fetches = [pltpu.make_async_copy(*pair, sems.at[i]) for i, pair in enumerate(pairs)]
    for fetch in fetches:
        fetch.start()
    node_count = pool_ref.shape[0] // (2 * page)
    copies, requests = out_hbm.shape[:2]
    fetches[0].wait()
    rows_ref[...] = pool_ref[...].astype(jnp.float32)
    root = [rows_ref[pl.ds(kind, page, stride=2)] for kind in range(2)]
    fetches[1].wait()

    def one(request, carry):
        mid = parent_ref[node_count + request] * (2 * page)
        for kind in range(2):
            chosen = rows_ref[pl.ds(mid + kind, page, stride=2)]
            block_ref[kind, request] = jnp.concatenate([root[kind], chosen], 0).astype(jnp.bfloat16)
        return carry

    lax.fori_loop(0, requests, one, 0, unroll=requests <= 8)
    sends = [
        pltpu.make_async_copy(block_ref.at[copy % 2], out_hbm.at[copy], sems.at[len(pairs) + copy])
        for copy in range(copies)
    ]
    for send in sends:
        send.start()

    fetches[2].wait()
    fetches[3].wait()
    mid = parent_ref[node_count + lax.axis_index("pool")]
    key = lax.broadcasted_iota(jnp.int32, bias_ref.shape, 1)
    stripe, is_mid = key // (2 * page), (key % (2 * page)) >= page
    offset = stripe - jnp.where(is_mid, owner_ref[mid], owner_ref[0])
    offset = jnp.where(offset < 0, offset + requests, offset)
    used = offset < jnp.where(is_mid, pages_ref[mid], pages_ref[0])
    bias_ref[...] = jnp.where(used, 0.0, MASKED)
    for copy in fetches[4:] + sends:
        copy.wait()


def hand_over_kernel(*refs):
    pass


def hand_over(cost, *arrays):
    anywhere = pl.BlockSpec(memory_space=pl.ANY)
    return pl.pallas_call(
        hand_over_kernel,
        out_shape=[jax.ShapeDtypeStruct(array.shape, array.dtype) for array in arrays],
        in_specs=[anywhere] * len(arrays),
        out_specs=[anywhere] * len(arrays),
        input_output_aliases={i: i for i in range(len(arrays))},
        compiler_params=pltpu.CompilerParams(vmem_limit_bytes=2**20),
        cost_estimate=cost,
    )(*arrays)


def scores_of(rows, keys):
    scores = lax.dot_general(rows, keys, (((1,), (1,)), ((), ())), preferred_element_type=jnp.float32)
    return scores * (LOG2_E * 128 ** (-0.5))


def over(sums, totals):
    inverse = pl.reciprocal(totals, approx=True)
    return sums * (inverse * (2.0 - totals * inverse))


def weigh(weights, values):
    sums = dot(weights.astype(jnp.bfloat16), jnp.concatenate([values, jnp.ones_like(values)], 1))
    return sums[:, : values.shape[1]], sums[:, values.shape[1] :]


def own_kernel(leaf_len_ref, q_ref, *rest, page):
    local_refs = rest[:4]
    result_ref, level_ref, bias_ref, kf_ref, vf_ref = rest[4:]
    tokens, q_heads, dim = q_ref.shape
    group = q_heads // 4
    leaf_slots = bias_ref.shape[0] - 4 * tokens
    rank = lax.axis_index("tp")

    key = lax.broadcasted_iota(jnp.int32, (leaf_slots, dim), 0)
    bias_ref[0:leaf_slots] = jnp.where(key < leaf_len_ref[0] * page, 0.0, MASKED).astype(jnp.bfloat16)
    key = lax.broadcasted_iota(jnp.int32, (tokens, dim), 0)
    row = lax.broadcasted_iota(jnp.int32, (tokens, dim), 1)
    for step in range(4):
        seen = key <= row if step == 0 else jnp.full((tokens, dim), rank ^ step, jnp.int32) < rank
        bias_ref[leaf_slots + step * tokens : leaf_slots + (step + 1) * tokens] = jnp.where(
            seen, 0.0, MASKED
        ).astype(jnp.bfloat16)

    fresh_rows = local_refs[0].shape[0] - 2 * leaf_slots

    def fresh_source(out_row):
        head, kind, token = out_row // (2 * tokens), (out_row // tokens) % 2, out_row % tokens
        return token * 8 + head * 2 + kind

    fresh_pick = pick((fresh_rows, fresh_rows), fresh_source)
    for step in range(4):
        parts = dot(fresh_pick, local_refs[step][2 * leaf_slots :]).astype(jnp.bfloat16)
        for head in range(4):
            base = head * 2 * tokens
            kf_ref[head, step * tokens : (step + 1) * tokens] = parts[base : base + tokens]
            vf_ref[head, step * tokens : (step + 1) * tokens] = parts[base + tokens : base + 2 * tokens]

    chunk = 256
    half = chunk // 2
    leaf_pick = pick((chunk, chunk), lambda out_row: (out_row % half) * 2 + out_row // half)
    bias = bias_ref[...]
    token = lax.broadcasted_iota(jnp.int32, (tokens * group, dim), 0) // group
    column = lax.broadcasted_iota(jnp.int32, (tokens * group, dim), 1)
    own_row = jnp.where(token == column, 1.0, 0.0).astype(jnp.bfloat16)
    for step in range(4):
        head = rank ^ step
        leaf_k, leaf_v = [], []
        for piece in range(leaf_slots // half):
            parts = dot(leaf_pick, local_refs[step][piece * chunk : (piece + 1) * chunk]).astype(jnp.bfloat16)
            leaf_k.append(parts[:half])
            leaf_v.append(parts[half:])
        keys = jnp.concatenate([jnp.concatenate(leaf_k + [kf_ref[head]], 0), bias], 1)
        values = jnp.concatenate(leaf_v + [vf_ref[head]], 0)
        rows = q_ref[:, pl.ds(pl.multiple_of(head * group, group), group), :].reshape(tokens * group, dim)
        scores = scores_of(jnp.concatenate([rows, own_row], 1), keys)
        top = jnp.max(scores, axis=1, keepdims=True)
        sums, totals = weigh(jnp.exp2(scores - top), values)
        result_ref[step] = sums / totals
        level_ref[step] = jnp.log2(totals) + top


def shared_kernel(q_ref, bias_ref, other_ref, level_ref, mine_ref, theirs_ref, out_hbm, stage_ref, sems):
    tokens, q_heads, dim = q_ref.shape
    group = q_heads // 4
    shared_keys = bias_ref.shape[1]
    rank = lax.axis_index("tp")
    has_keys = rank % 2 == 0
    bias = bias_ref[0:1]
    places = [pl.ds(pl.multiple_of((rank ^ step) * group, group), group) for step in range(4)]
    part = tokens // 2
    parts = [(half, step) for half in range(2) for step in range(4)]

    def rows_of(ref, half, step):
        return ref[step, half * part * group : (half + 1) * part * group]

    def above_level(half, step):
        head = rank ^ step
        keys = jnp.where(has_keys, mine_ref[head], theirs_ref[head]).reshape(shared_keys, dim)
        rows = q_ref[half * part : (half + 1) * part, places[step], :].reshape(part * group, dim)
        level = rows_of(level_ref, half, step)
        return scores_of(rows, keys) + bias - jnp.concatenate([level] * (shared_keys // dim), 1)

    def weighted(step, weights):
        head = rank ^ step
        values = jnp.where(has_keys, theirs_ref[head], mine_ref[head]).reshape(shared_keys, dim)
        return weigh(weights, values)

    def store(half, step, result):
        tile = slice(half * part, (half + 1) * part)
        stage_ref[tile, places[step], :] = result.astype(jnp.bfloat16).reshape(part, group, dim)

    def write(half):
        tile = pl.ds(half * part, part)
        copy = pltpu.make_async_copy(stage_ref.at[tile], out_hbm.at[tile], sems.at[half])
        copy.start()
        return copy

    ahead = 2
    scores = [above_level(*parts[i]) for i in range(ahead)]
    writes, weights = [], []
    for i, (half, step) in enumerate(parts):
        if i + ahead < len(parts):
            scores.append(above_level(*parts[i + ahead]))
        weights.append(jnp.exp2(scores[i]).astype(jnp.bfloat16))
        sums, totals = weighted(step, weights[-1])
        store(half, step, over(sums + rows_of(other_ref, half, step), totals + 1.0))
        if step == 3:
            writes.append(write(half))
    too_high = jnp.max(functools.reduce(jnp.maximum, weights).astype(jnp.float32)) > 2.0**100
    for copy in writes:
        copy.wait()

    @pl.when(too_high)
    def _():
        for half, step in parts:
            score = above_level(half, step)
            top = jnp.maximum(jnp.max(score, axis=1, keepdims=True), 0.0)
            sums, totals = weighted(step, jnp.exp2(score - top))
            other = jnp.exp2(-top)
            store(half, step, over(sums + rows_of(other_ref, half, step) * other, totals + other))
        for half in range(2):
            write(half).wait()


def per_device(queries, fresh, pool, leaf, parent, node_pages, node_owner, leaf_len):
    tp = lax.axis_size("tp")
    stripes = lax.axis_size("pool")
    shared_count, _, page, _, _, dim = pool.shape
    tokens, q_heads, _ = queries.shape
    vmem = pl.BlockSpec(memory_space=pltpu.VMEM)
    swap = lambda array, bit: lax.ppermute(array, "tp", [(i, i ^ bit) for i in range(tp)])
    hbm = pl.BlockSpec(memory_space=pltpu.HBM)

    pool_rows = pool.reshape(-1, dim)
    leaf_rows = leaf.reshape(-1, dim)
    fresh_rows = fresh.reshape(-1, dim)
    operands = (parent, node_pages, node_owner, pool_rows, leaf_rows, fresh_rows)
    sent, local_0, bias = pl.pallas_call(
        functools.partial(select_kernel, page),
        out_shape=[
            jax.ShapeDtypeStruct((tp, stripes, 2 * page, dim), jnp.bfloat16),
            jax.ShapeDtypeStruct((leaf_rows.shape[0] + fresh_rows.shape[0], dim), jnp.bfloat16),
            jax.ShapeDtypeStruct((8, stripes * 2 * page), jnp.float32),
        ],
        in_specs=[hbm] * 6,
        out_specs=[hbm, vmem, vmem],
        scratch_shapes=[
            pltpu.SMEM(parent.shape, jnp.int32),
            pltpu.SMEM(node_pages.shape, jnp.int32),
            pltpu.SMEM(node_owner.shape, jnp.int32),
            pltpu.VMEM(pool_rows.shape, jnp.bfloat16),
            pltpu.VMEM(pool_rows.shape, jnp.float32),
            pltpu.VMEM((2, stripes, 2 * page, dim), jnp.bfloat16),
            pltpu.SemaphoreType.DMA((6 + tp,)),
        ],
        compiler_params=pltpu.CompilerParams(vmem_limit_bytes=16 * 2**20),
        cost_estimate=LONG,
    )(*[pltpu.with_memory_space_constraint(operand, pltpu.HBM) for operand in operands])
    local_2 = swap(local_0, 2)
    mine = lax.all_to_all(
        sent.reshape(tp * stripes, 2 * page, dim), ("tp", "pool"), split_axis=0, concat_axis=0, tiled=True
    ).reshape(tp, stripes, 2 * page, dim)
    local_0, local_2 = hand_over(LONG, local_0, local_2)
    local_1, local_3 = swap(local_0, 1), swap(local_2, 1)

    rows = tokens * q_heads // tp
    other, level = pl.pallas_call(
        functools.partial(own_kernel, page=page),
        out_shape=[jax.ShapeDtypeStruct((tp, rows, dim), jnp.float32)] * 2,
        in_specs=[pl.BlockSpec(memory_space=pltpu.SMEM)] + [vmem] * 5,
        out_specs=[vmem] * 2,
        scratch_shapes=[pltpu.VMEM((leaf.shape[1] + tp * tokens, dim), jnp.bfloat16)]
        + [pltpu.VMEM((tp, tp * tokens, dim), jnp.bfloat16)] * 2,
        compiler_params=pltpu.CompilerParams(vmem_limit_bytes=24 * 2**20),
        cost_estimate=SHORT,
    )(leaf_len, queries, local_0, local_1, local_2, local_3)
    mine, level = hand_over(SHORT, mine, level)
    theirs = swap(mine, 1)
    return pl.pallas_call(
        shared_kernel,
        out_shape=jax.ShapeDtypeStruct(queries.shape, jnp.bfloat16),
        in_specs=[vmem] * 6,
        out_specs=hbm,
        scratch_shapes=[
            pltpu.VMEM(queries.shape, jnp.bfloat16),
            pltpu.SemaphoreType.DMA((2,)),
        ],
        compiler_params=pltpu.CompilerParams(vmem_limit_bytes=(24 if stripes <= 8 else 48) * 2**20),
    )(queries, bias, other, level, mine, theirs)


def solution(mesh):
    return jax.shard_map(
        per_device,
        mesh=mesh,
        in_specs=(
            P(("pool", "tp"), None, None),
            P(("pool", "tp"), None, None, None),
            P(None, "pool", None, "tp", None, None),
            P("pool", None, "tp", None, None),
            P(),
            P(),
            P(),
            P("pool"),
        ),
        out_specs=P(("pool", "tp"), None, None),
        check_vma=False,
    )
```

```python
import functools

import jax
import jax.numpy as jnp
from jax import lax
from jax.experimental import pallas as pl
from jax.experimental.pallas import tpu as pltpu
from jax.sharding import PartitionSpec as P

LOG2_E = 1.4426950408889634
MASKED = -1e30
LONG = pl.CostEstimate(flops=5 * 10**10, bytes_accessed=10**6, transcendentals=0)
SHORT = pl.CostEstimate(flops=10**6, bytes_accessed=10**5, transcendentals=0)


def pick(shape, source_row):
    row = lax.broadcasted_iota(jnp.int32, shape, 0)
    column = lax.broadcasted_iota(jnp.int32, shape, 1)
    return jnp.where(column == source_row(row), 1.0, 0.0).astype(jnp.bfloat16)


def dot(a, b):
    return lax.dot_general(a, b, (((1,), (0,)), ((), ())), preferred_element_type=jnp.float32)


def select_kernel(
    page, parent_hbm, pages_hbm, owner_hbm, pool_hbm, leaf_hbm, fresh_hbm,
    out_hbm, local_ref, bias_ref,
    parent_ref, pages_ref, owner_ref, pool_ref, rows_ref, block_ref, sems,
):
    leaf_rows, fresh_rows = leaf_hbm.shape[0], fresh_hbm.shape[0]
    pairs = [
        (pool_hbm, pool_ref),
        (parent_hbm, parent_ref),
        (pages_hbm, pages_ref),
        (owner_hbm, owner_ref),
        (leaf_hbm, local_ref.at[pl.ds(0, leaf_rows)]),
        (fresh_hbm, local_ref.at[pl.ds(leaf_rows, fresh_rows)]),
    ]
    fetches = [pltpu.make_async_copy(*pair, sems.at[i]) for i, pair in enumerate(pairs)]
    for fetch in fetches:
        fetch.start()
    node_count = pool_ref.shape[0] // (2 * page)
    copies, requests = out_hbm.shape[:2]
    fetches[0].wait()
    rows_ref[...] = pool_ref[...].astype(jnp.float32)
    root = [rows_ref[pl.ds(kind, page, stride=2)] for kind in range(2)]
    fetches[1].wait()

    def one(request, carry):
        mid = parent_ref[node_count + request] * (2 * page)
        for kind in range(2):
            chosen = rows_ref[pl.ds(mid + kind, page, stride=2)]
            block_ref[kind, request] = jnp.concatenate([root[kind], chosen], 0).astype(jnp.bfloat16)
        return carry

    lax.fori_loop(0, requests, one, 0, unroll=requests <= 8)
    sends = [
        pltpu.make_async_copy(block_ref.at[copy % 2], out_hbm.at[copy], sems.at[len(pairs) + copy])
        for copy in range(copies)
    ]
    for send in sends:
        send.start()

    fetches[2].wait()
    fetches[3].wait()
    mid = parent_ref[node_count + lax.axis_index("pool")]
    key = lax.broadcasted_iota(jnp.int32, bias_ref.shape, 1)
    stripe, is_mid = key // (2 * page), (key % (2 * page)) >= page
    offset = stripe - jnp.where(is_mid, owner_ref[mid], owner_ref[0])
    offset = jnp.where(offset < 0, offset + requests, offset)
    used = offset < jnp.where(is_mid, pages_ref[mid], pages_ref[0])
    bias_ref[...] = jnp.where(used, 0.0, MASKED)
    for copy in fetches[4:] + sends:
        copy.wait()


def hand_over_kernel(*refs):
    pass


def hand_over(cost, *arrays):
    anywhere = pl.BlockSpec(memory_space=pl.ANY)
    return pl.pallas_call(
        hand_over_kernel,
        out_shape=[jax.ShapeDtypeStruct(array.shape, array.dtype) for array in arrays],
        in_specs=[anywhere] * len(arrays),
        out_specs=[anywhere] * len(arrays),
        input_output_aliases={i: i for i in range(len(arrays))},
        compiler_params=pltpu.CompilerParams(vmem_limit_bytes=2**20),
        cost_estimate=cost,
    )(*arrays)


def scores_of(rows, keys):
    scores = lax.dot_general(rows, keys, (((1,), (1,)), ((), ())), preferred_element_type=jnp.float32)
    return scores * (LOG2_E * 128 ** (-0.5))


def over(sums, totals):
    inverse = pl.reciprocal(totals, approx=True)
    return sums * (inverse * (2.0 - totals * inverse))


def weigh(weights, values):
    sums = dot(weights.astype(jnp.bfloat16), jnp.concatenate([values, jnp.ones_like(values)], 1))
    return sums[:, : values.shape[1]], sums[:, values.shape[1] :]


def own_kernel(leaf_len_ref, q_ref, *rest, page):
    local_refs = rest[:4]
    result_ref, level_ref, bias_ref, kf_ref, vf_ref = rest[4:]
    tokens, q_heads, dim = q_ref.shape
    group = q_heads // 4
    leaf_slots = bias_ref.shape[0] - 4 * tokens
    rank = lax.axis_index("tp")

    key = lax.broadcasted_iota(jnp.int32, (leaf_slots, dim), 0)
    bias_ref[0:leaf_slots] = jnp.where(key < leaf_len_ref[0] * page, 0.0, MASKED).astype(jnp.bfloat16)
    key = lax.broadcasted_iota(jnp.int32, (tokens, dim), 0)
    row = lax.broadcasted_iota(jnp.int32, (tokens, dim), 1)
    for step in range(4):
        seen = key <= row if step == 0 else jnp.full((tokens, dim), rank ^ step, jnp.int32) < rank
        bias_ref[leaf_slots + step * tokens : leaf_slots + (step + 1) * tokens] = jnp.where(
            seen, 0.0, MASKED
        ).astype(jnp.bfloat16)

    fresh_rows = local_refs[0].shape[0] - 2 * leaf_slots

    def fresh_source(out_row):
        head, kind, token = out_row // (2 * tokens), (out_row // tokens) % 2, out_row % tokens
        return token * 8 + head * 2 + kind

    fresh_pick = pick((fresh_rows, fresh_rows), fresh_source)
    for step in range(4):
        parts = dot(fresh_pick, local_refs[step][2 * leaf_slots :]).astype(jnp.bfloat16)
        for head in range(4):
            base = head * 2 * tokens
            kf_ref[head, step * tokens : (step + 1) * tokens] = parts[base : base + tokens]
            vf_ref[head, step * tokens : (step + 1) * tokens] = parts[base + tokens : base + 2 * tokens]

    chunk = 256
    half = chunk // 2
    leaf_pick = pick((chunk, chunk), lambda out_row: (out_row % half) * 2 + out_row // half)
    bias = bias_ref[...]
    token = lax.broadcasted_iota(jnp.int32, (tokens * group, dim), 0) // group
    column = lax.broadcasted_iota(jnp.int32, (tokens * group, dim), 1)
    own_row = jnp.where(token == column, 1.0, 0.0).astype(jnp.bfloat16)
    for step in range(4):
        head = rank ^ step
        leaf_k, leaf_v = [], []
        for piece in range(leaf_slots // half):
            parts = dot(leaf_pick, local_refs[step][piece * chunk : (piece + 1) * chunk]).astype(jnp.bfloat16)
            leaf_k.append(parts[:half])
            leaf_v.append(parts[half:])
        keys = jnp.concatenate([jnp.concatenate(leaf_k + [kf_ref[head]], 0), bias], 1)
        values = jnp.concatenate(leaf_v + [vf_ref[head]], 0)
        rows = q_ref[:, pl.ds(pl.multiple_of(head * group, group), group), :].reshape(tokens * group, dim)
        scores = scores_of(jnp.concatenate([rows, own_row], 1), keys)
        top = jnp.max(scores, axis=1, keepdims=True)
        sums, totals = weigh(jnp.exp2(scores - top), values)
        result_ref[step] = sums / totals
        level_ref[step] = jnp.log2(totals) + top


def shared_kernel(q_ref, bias_ref, other_ref, level_ref, mine_ref, theirs_ref, out_hbm, stage_ref, sems):
    tokens, q_heads, dim = q_ref.shape
    group = q_heads // 4
    shared_keys = bias_ref.shape[1]
    rank = lax.axis_index("tp")
    has_keys = rank % 2 == 0
    bias = bias_ref[0:1]
    place = lambda step: pl.ds(pl.multiple_of((rank ^ step) * group, group), group)

    def above_level(step):
        head = rank ^ step
        keys = jnp.where(has_keys, mine_ref[head], theirs_ref[head]).reshape(shared_keys, dim)
        scores = scores_of(q_ref[:, place(step), :].reshape(tokens * group, dim), keys)
        return scores + bias - jnp.concatenate([level_ref[step]] * (shared_keys // dim), 1)

    def weighted(step, weights):
        head = rank ^ step
        values = jnp.where(has_keys, theirs_ref[head], mine_ref[head]).reshape(shared_keys, dim)
        return weigh(weights, values)

    def write(step, result):
        stage_ref[step] = result.astype(jnp.bfloat16).reshape(tokens, group, dim)
        copy = pltpu.make_async_copy(stage_ref.at[step], out_hbm.at[:, place(step)], sems.at[step])
        copy.start()
        return copy

    scores = [above_level(step) for step in range(4)]
    writes, weights = [], []
    for step in range(4):
        weights.append(jnp.exp2(scores[step]).astype(jnp.bfloat16))
        sums, totals = weighted(step, weights[-1])
        writes.append(write(step, over(sums + other_ref[step], totals + 1.0)))
    too_high = jnp.max(functools.reduce(jnp.maximum, weights).astype(jnp.float32)) > 2.0**100
    for copy in writes:
        copy.wait()

    @pl.when(too_high)
    def _():
        @pl.loop(0, 4)
        def _(step):
            scores = above_level(step)
            top = jnp.maximum(jnp.max(scores, axis=1, keepdims=True), 0.0)
            sums, totals = weighted(step, jnp.exp2(scores - top))
            other = jnp.exp2(-top)
            write(step, over(sums + other_ref[step] * other, totals + other)).wait()


def per_device(queries, fresh, pool, leaf, parent, node_pages, node_owner, leaf_len):
    tp = lax.axis_size("tp")
    stripes = lax.axis_size("pool")
    shared_count, _, page, _, _, dim = pool.shape
    tokens, q_heads, _ = queries.shape
    vmem = pl.BlockSpec(memory_space=pltpu.VMEM)
    swap = lambda array, bit: lax.ppermute(array, "tp", [(i, i ^ bit) for i in range(tp)])
    hbm = pl.BlockSpec(memory_space=pltpu.HBM)

    pool_rows = pool.reshape(-1, dim)
    leaf_rows = leaf.reshape(-1, dim)
    fresh_rows = fresh.reshape(-1, dim)
    operands = (parent, node_pages, node_owner, pool_rows, leaf_rows, fresh_rows)
    sent, local_0, bias = pl.pallas_call(
        functools.partial(select_kernel, page),
        out_shape=[
            jax.ShapeDtypeStruct((tp, stripes, 2 * page, dim), jnp.bfloat16),
            jax.ShapeDtypeStruct((leaf_rows.shape[0] + fresh_rows.shape[0], dim), jnp.bfloat16),
            jax.ShapeDtypeStruct((8, stripes * 2 * page), jnp.float32),
        ],
        in_specs=[hbm] * 6,
        out_specs=[hbm, vmem, vmem],
        scratch_shapes=[
            pltpu.SMEM(parent.shape, jnp.int32),
            pltpu.SMEM(node_pages.shape, jnp.int32),
            pltpu.SMEM(node_owner.shape, jnp.int32),
            pltpu.VMEM(pool_rows.shape, jnp.bfloat16),
            pltpu.VMEM(pool_rows.shape, jnp.float32),
            pltpu.VMEM((2, stripes, 2 * page, dim), jnp.bfloat16),
            pltpu.SemaphoreType.DMA((6 + tp,)),
        ],
        compiler_params=pltpu.CompilerParams(vmem_limit_bytes=16 * 2**20),
        cost_estimate=LONG,
    )(*[pltpu.with_memory_space_constraint(operand, pltpu.HBM) for operand in operands])
    local_2 = swap(local_0, 2)
    mine = lax.all_to_all(
        sent.reshape(tp * stripes, 2 * page, dim), ("tp", "pool"), split_axis=0, concat_axis=0, tiled=True
    ).reshape(tp, stripes, 2 * page, dim)
    local_0, local_2 = hand_over(LONG, local_0, local_2)
    local_1, local_3 = swap(local_0, 1), swap(local_2, 1)

    rows = tokens * q_heads // tp
    other, level = pl.pallas_call(
        functools.partial(own_kernel, page=page),
        out_shape=[jax.ShapeDtypeStruct((tp, rows, dim), jnp.float32)] * 2,
        in_specs=[pl.BlockSpec(memory_space=pltpu.SMEM)] + [vmem] * 5,
        out_specs=[vmem] * 2,
        scratch_shapes=[pltpu.VMEM((leaf.shape[1] + tp * tokens, dim), jnp.bfloat16)]
        + [pltpu.VMEM((tp, tp * tokens, dim), jnp.bfloat16)] * 2,
        compiler_params=pltpu.CompilerParams(vmem_limit_bytes=24 * 2**20),
        cost_estimate=SHORT,
    )(leaf_len, queries, local_0, local_1, local_2, local_3)
    mine, level = hand_over(SHORT, mine, level)
    theirs = swap(mine, 1)
    return pl.pallas_call(
        shared_kernel,
        out_shape=jax.ShapeDtypeStruct(queries.shape, jnp.bfloat16),
        in_specs=[vmem] * 6,
        out_specs=hbm,
        scratch_shapes=[
            pltpu.VMEM((tp, tokens, q_heads // tp, dim), jnp.bfloat16),
            pltpu.SemaphoreType.DMA((tp,)),
        ],
        compiler_params=pltpu.CompilerParams(vmem_limit_bytes=(24 if stripes <= 8 else 48) * 2**20),
    )(queries, bias, other, level, mine, theirs)


def solution(mesh):
    return jax.shard_map(
        per_device,
        mesh=mesh,
        in_specs=(
            P(("pool", "tp"), None, None),
            P(("pool", "tp"), None, None, None),
            P(None, "pool", None, "tp", None, None),
            P("pool", None, "tp", None, None),
            P(),
            P(),
            P(),
            P("pool"),
        ),
        out_specs=P(("pool", "tp"), None, None),
        check_vma=False,
    )
```

```python
import functools

import jax
import jax.numpy as jnp
from jax import lax
from jax.experimental import pallas as pl
from jax.experimental.pallas import tpu as pltpu
from jax.sharding import PartitionSpec as P

LOG2_E = 1.4426950408889634
MASKED = -1e30
LONG = pl.CostEstimate(flops=5 * 10**10, bytes_accessed=10**6, transcendentals=0)
SHORT = pl.CostEstimate(flops=10**6, bytes_accessed=10**5, transcendentals=0)


def pick(shape, source_row):
    row = lax.broadcasted_iota(jnp.int32, shape, 0)
    column = lax.broadcasted_iota(jnp.int32, shape, 1)
    return jnp.where(column == source_row(row), 1.0, 0.0).astype(jnp.bfloat16)


def dot(a, b):
    return lax.dot_general(a, b, (((1,), (0,)), ((), ())), preferred_element_type=jnp.float32)


def select_kernel(
    page, parent_hbm, pages_hbm, owner_hbm, pool_hbm, leaf_hbm, fresh_hbm,
    out_hbm, local_ref, bias_ref,
    parent_ref, pages_ref, owner_ref, pool_ref, rows_ref, block_ref, sems,
):
    leaf_rows, fresh_rows = leaf_hbm.shape[0], fresh_hbm.shape[0]
    pairs = [
        (pool_hbm, pool_ref),
        (parent_hbm, parent_ref),
        (pages_hbm, pages_ref),
        (owner_hbm, owner_ref),
        (leaf_hbm, local_ref.at[pl.ds(0, leaf_rows)]),
        (fresh_hbm, local_ref.at[pl.ds(leaf_rows, fresh_rows)]),
    ]
    fetches = [pltpu.make_async_copy(*pair, sems.at[i]) for i, pair in enumerate(pairs)]
    for fetch in fetches:
        fetch.start()
    node_count = pool_ref.shape[0] // (2 * page)
    copies, requests = out_hbm.shape[:2]
    fetches[0].wait()
    rows_ref[...] = pool_ref[...].astype(jnp.float32)
    root = [rows_ref[pl.ds(kind, page, stride=2)] for kind in range(2)]
    fetches[1].wait()

    def one(request, carry):
        mid = parent_ref[node_count + request] * (2 * page)
        for kind in range(2):
            chosen = rows_ref[pl.ds(mid + kind, page, stride=2)]
            block = jnp.concatenate([root[kind], chosen], 0).astype(jnp.bfloat16)
            for copy in range(kind, copies, 2):
                block_ref[copy, request] = block
        return carry

    lax.fori_loop(0, requests, one, 0, unroll=requests <= 8)
    send = pltpu.make_async_copy(block_ref, out_hbm, sems.at[len(pairs)])
    send.start()

    fetches[2].wait()
    fetches[3].wait()
    mid = parent_ref[node_count + lax.axis_index("pool")]
    key = lax.broadcasted_iota(jnp.int32, bias_ref.shape, 1)
    stripe, is_mid = key // (2 * page), (key % (2 * page)) >= page
    offset = stripe - jnp.where(is_mid, owner_ref[mid], owner_ref[0])
    offset = jnp.where(offset < 0, offset + requests, offset)
    used = offset < jnp.where(is_mid, pages_ref[mid], pages_ref[0])
    bias_ref[...] = jnp.where(used, 0.0, MASKED)
    for copy in fetches[4:] + [send]:
        copy.wait()


def hand_over_kernel(*refs):
    pass


def hand_over(cost, *arrays):
    anywhere = pl.BlockSpec(memory_space=pl.ANY)
    return pl.pallas_call(
        hand_over_kernel,
        out_shape=[jax.ShapeDtypeStruct(array.shape, array.dtype) for array in arrays],
        in_specs=[anywhere] * len(arrays),
        out_specs=[anywhere] * len(arrays),
        input_output_aliases={i: i for i in range(len(arrays))},
        compiler_params=pltpu.CompilerParams(vmem_limit_bytes=2**20),
        cost_estimate=cost,
    )(*arrays)


def scores_of(rows, keys):
    scores = lax.dot_general(rows, keys, (((1,), (1,)), ((), ())), preferred_element_type=jnp.float32)
    return scores * (LOG2_E * 128 ** (-0.5))


def over(sums, totals):
    inverse = pl.reciprocal(totals, approx=True)
    return sums * (inverse * (2.0 - totals * inverse))


def weigh(weights, values):
    sums = dot(weights.astype(jnp.bfloat16), jnp.concatenate([values, jnp.ones_like(values)], 1))
    return sums[:, : values.shape[1]], sums[:, values.shape[1] :]


def own_kernel(leaf_len_ref, q_ref, *rest, page):
    local_refs = rest[:4]
    result_ref, level_ref, bias_ref, kf_ref, vf_ref = rest[4:]
    tokens, q_heads, dim = q_ref.shape
    group = q_heads // 4
    leaf_slots = bias_ref.shape[0] - 4 * tokens
    rank = lax.axis_index("tp")

    key = lax.broadcasted_iota(jnp.int32, (leaf_slots, dim), 0)
    bias_ref[0:leaf_slots] = jnp.where(key < leaf_len_ref[0] * page, 0.0, MASKED).astype(jnp.bfloat16)
    key = lax.broadcasted_iota(jnp.int32, (tokens, dim), 0)
    row = lax.broadcasted_iota(jnp.int32, (tokens, dim), 1)
    for step in range(4):
        seen = key <= row if step == 0 else jnp.full((tokens, dim), rank ^ step, jnp.int32) < rank
        bias_ref[leaf_slots + step * tokens : leaf_slots + (step + 1) * tokens] = jnp.where(
            seen, 0.0, MASKED
        ).astype(jnp.bfloat16)

    fresh_rows = local_refs[0].shape[0] - 2 * leaf_slots

    def fresh_source(out_row):
        head, kind, token = out_row // (2 * tokens), (out_row // tokens) % 2, out_row % tokens
        return token * 8 + head * 2 + kind

    fresh_pick = pick((fresh_rows, fresh_rows), fresh_source)
    for step in range(4):
        parts = dot(fresh_pick, local_refs[step][2 * leaf_slots :]).astype(jnp.bfloat16)
        for head in range(4):
            base = head * 2 * tokens
            kf_ref[head, step * tokens : (step + 1) * tokens] = parts[base : base + tokens]
            vf_ref[head, step * tokens : (step + 1) * tokens] = parts[base + tokens : base + 2 * tokens]

    chunk = 256
    half = chunk // 2
    leaf_pick = pick((chunk, chunk), lambda out_row: (out_row % half) * 2 + out_row // half)
    bias = bias_ref[...]
    token = lax.broadcasted_iota(jnp.int32, (tokens * group, dim), 0) // group
    column = lax.broadcasted_iota(jnp.int32, (tokens * group, dim), 1)
    own_row = jnp.where(token == column, 1.0, 0.0).astype(jnp.bfloat16)
    for step in range(4):
        head = rank ^ step
        leaf_k, leaf_v = [], []
        for piece in range(leaf_slots // half):
            parts = dot(leaf_pick, local_refs[step][piece * chunk : (piece + 1) * chunk]).astype(jnp.bfloat16)
            leaf_k.append(parts[:half])
            leaf_v.append(parts[half:])
        keys = jnp.concatenate([jnp.concatenate(leaf_k + [kf_ref[head]], 0), bias], 1)
        values = jnp.concatenate(leaf_v + [vf_ref[head]], 0)
        rows = q_ref[:, pl.ds(pl.multiple_of(head * group, group), group), :].reshape(tokens * group, dim)
        scores = scores_of(jnp.concatenate([rows, own_row], 1), keys)
        top = jnp.max(scores, axis=1, keepdims=True)
        sums, totals = weigh(jnp.exp2(scores - top), values)
        result_ref[step] = sums / totals
        level_ref[step] = jnp.log2(totals) + top


def shared_kernel(q_ref, bias_ref, other_ref, level_ref, mine_ref, theirs_ref, out_hbm, stage_ref, sems):
    tokens, q_heads, dim = q_ref.shape
    group = q_heads // 4
    shared_keys = bias_ref.shape[1]
    rank = lax.axis_index("tp")
    has_keys = rank % 2 == 0
    bias = bias_ref[0:1]
    place = lambda step: pl.ds(pl.multiple_of((rank ^ step) * group, group), group)

    def above_level(step):
        head = rank ^ step
        keys = jnp.where(has_keys, mine_ref[head], theirs_ref[head]).reshape(shared_keys, dim)
        scores = scores_of(q_ref[:, place(step), :].reshape(tokens * group, dim), keys)
        return scores + bias - jnp.concatenate([level_ref[step]] * (shared_keys // dim), 1)

    def weighted(step, weights):
        head = rank ^ step
        values = jnp.where(has_keys, theirs_ref[head], mine_ref[head]).reshape(shared_keys, dim)
        return weigh(weights, values)

    def write(step, result):
        stage_ref[step] = result.astype(jnp.bfloat16).reshape(tokens, group, dim)
        copy = pltpu.make_async_copy(stage_ref.at[step], out_hbm.at[:, place(step)], sems.at[step])
        copy.start()
        return copy

    scores = [above_level(step) for step in range(4)]
    writes, weights = [], []
    for step in range(4):
        weights.append(jnp.exp2(scores[step]).astype(jnp.bfloat16))
        sums, totals = weighted(step, weights[-1])
        writes.append(write(step, over(sums + other_ref[step], totals + 1.0)))
    too_high = jnp.max(functools.reduce(jnp.maximum, weights).astype(jnp.float32)) > 2.0**100
    for copy in writes:
        copy.wait()

    @pl.when(too_high)
    def _():
        @pl.loop(0, 4)
        def _(step):
            scores = above_level(step)
            top = jnp.maximum(jnp.max(scores, axis=1, keepdims=True), 0.0)
            sums, totals = weighted(step, jnp.exp2(scores - top))
            other = jnp.exp2(-top)
            write(step, over(sums + other_ref[step] * other, totals + other)).wait()


def per_device(queries, fresh, pool, leaf, parent, node_pages, node_owner, leaf_len):
    tp = lax.axis_size("tp")
    stripes = lax.axis_size("pool")
    shared_count, _, page, _, _, dim = pool.shape
    tokens, q_heads, _ = queries.shape
    vmem = pl.BlockSpec(memory_space=pltpu.VMEM)
    swap = lambda array, bit: lax.ppermute(array, "tp", [(i, i ^ bit) for i in range(tp)])
    hbm = pl.BlockSpec(memory_space=pltpu.HBM)

    pool_rows = pool.reshape(-1, dim)
    leaf_rows = leaf.reshape(-1, dim)
    fresh_rows = fresh.reshape(-1, dim)
    operands = (parent, node_pages, node_owner, pool_rows, leaf_rows, fresh_rows)
    sent, local_0, bias = pl.pallas_call(
        functools.partial(select_kernel, page),
        out_shape=[
            jax.ShapeDtypeStruct((tp, stripes, 2 * page, dim), jnp.bfloat16),
            jax.ShapeDtypeStruct((leaf_rows.shape[0] + fresh_rows.shape[0], dim), jnp.bfloat16),
            jax.ShapeDtypeStruct((8, stripes * 2 * page), jnp.float32),
        ],
        in_specs=[hbm] * 6,
        out_specs=[hbm, vmem, vmem],
        scratch_shapes=[
            pltpu.SMEM(parent.shape, jnp.int32),
            pltpu.SMEM(node_pages.shape, jnp.int32),
            pltpu.SMEM(node_owner.shape, jnp.int32),
            pltpu.VMEM(pool_rows.shape, jnp.bfloat16),
            pltpu.VMEM(pool_rows.shape, jnp.float32),
            pltpu.VMEM((tp, stripes, 2 * page, dim), jnp.bfloat16),
            pltpu.SemaphoreType.DMA((7,)),
        ],
        compiler_params=pltpu.CompilerParams(vmem_limit_bytes=16 * 2**20),
        cost_estimate=LONG,
    )(*[pltpu.with_memory_space_constraint(operand, pltpu.HBM) for operand in operands])
    local_2 = swap(local_0, 2)
    mine = lax.all_to_all(
        sent.reshape(tp * stripes, 2 * page, dim), ("tp", "pool"), split_axis=0, concat_axis=0, tiled=True
    ).reshape(tp, stripes, 2 * page, dim)
    local_0, local_2 = hand_over(LONG, local_0, local_2)
    local_1, local_3 = swap(local_0, 1), swap(local_2, 1)

    rows = tokens * q_heads // tp
    other, level = pl.pallas_call(
        functools.partial(own_kernel, page=page),
        out_shape=[jax.ShapeDtypeStruct((tp, rows, dim), jnp.float32)] * 2,
        in_specs=[pl.BlockSpec(memory_space=pltpu.SMEM)] + [vmem] * 5,
        out_specs=[vmem] * 2,
        scratch_shapes=[pltpu.VMEM((leaf.shape[1] + tp * tokens, dim), jnp.bfloat16)]
        + [pltpu.VMEM((tp, tp * tokens, dim), jnp.bfloat16)] * 2,
        compiler_params=pltpu.CompilerParams(vmem_limit_bytes=24 * 2**20),
        cost_estimate=SHORT,
    )(leaf_len, queries, local_0, local_1, local_2, local_3)
    mine, level = hand_over(SHORT, mine, level)
    theirs = swap(mine, 1)
    return pl.pallas_call(
        shared_kernel,
        out_shape=jax.ShapeDtypeStruct(queries.shape, jnp.bfloat16),
        in_specs=[vmem] * 6,
        out_specs=hbm,
        scratch_shapes=[
            pltpu.VMEM((tp, tokens, q_heads // tp, dim), jnp.bfloat16),
            pltpu.SemaphoreType.DMA((tp,)),
        ],
        compiler_params=pltpu.CompilerParams(vmem_limit_bytes=(24 if stripes <= 8 else 48) * 2**20),
    )(queries, bias, other, level, mine, theirs)


def solution(mesh):
    return jax.shard_map(
        per_device,
        mesh=mesh,
        in_specs=(
            P(("pool", "tp"), None, None),
            P(("pool", "tp"), None, None, None),
            P(None, "pool", None, "tp", None, None),
            P("pool", None, "tp", None, None),
            P(),
            P(),
            P(),
            P("pool"),
        ),
        out_specs=P(("pool", "tp"), None, None),
        check_vma=False,
    )
```

```python
import functools

import jax
import jax.numpy as jnp
from jax import lax
from jax.experimental import pallas as pl
from jax.experimental.pallas import tpu as pltpu
from jax.sharding import PartitionSpec as P

LOG2_E = 1.4426950408889634
MASKED = -1e30
LONG = pl.CostEstimate(flops=5 * 10**10, bytes_accessed=10**6, transcendentals=0)
SHORT = pl.CostEstimate(flops=10**6, bytes_accessed=10**5, transcendentals=0)


def pick(shape, source_row):
    row = lax.broadcasted_iota(jnp.int32, shape, 0)
    column = lax.broadcasted_iota(jnp.int32, shape, 1)
    return jnp.where(column == source_row(row), 1.0, 0.0).astype(jnp.bfloat16)


def dot(a, b):
    return lax.dot_general(a, b, (((1,), (0,)), ((), ())), preferred_element_type=jnp.float32)


def select_kernel(
    page, parent_hbm, pages_hbm, owner_hbm, pool_hbm, leaf_hbm, fresh_hbm,
    out_hbm, local_ref, bias_ref,
    parent_ref, pages_ref, owner_ref, pool_ref, rows_ref, block_ref, sems,
):
    leaf_rows, fresh_rows = leaf_hbm.shape[0], fresh_hbm.shape[0]
    pairs = [
        (pool_hbm, pool_ref),
        (parent_hbm, parent_ref),
        (pages_hbm, pages_ref),
        (owner_hbm, owner_ref),
        (leaf_hbm, local_ref.at[pl.ds(0, leaf_rows)]),
        (fresh_hbm, local_ref.at[pl.ds(leaf_rows, fresh_rows)]),
    ]
    fetches = [pltpu.make_async_copy(*pair, sems.at[i]) for i, pair in enumerate(pairs)]
    for fetch in fetches:
        fetch.start()
    node_count = pool_ref.shape[0] // (2 * page)
    copies, requests = out_hbm.shape[:2]
    fetches[0].wait()
    rows_ref[...] = pool_ref[...].astype(jnp.float32)
    root = [rows_ref[pl.ds(kind, page, stride=2)] for kind in range(2)]
    fetches[1].wait()

    def one(request, carry):
        mid = parent_ref[node_count + request] * (2 * page)
        chosen = [rows_ref[pl.ds(mid + kind, page, stride=2)] for kind in range(2)]
        for copy in range(copies):
            block = jnp.concatenate(root if copy % 2 == 0 else chosen, 0)
            block_ref[copy, request] = block.astype(jnp.bfloat16)
        return carry

    lax.fori_loop(0, requests, one, 0, unroll=requests <= 8)
    send = pltpu.make_async_copy(block_ref, out_hbm, sems.at[len(pairs)])
    send.start()

    fetches[2].wait()
    fetches[3].wait()
    mid = parent_ref[node_count + lax.axis_index("pool")]
    half = lax.broadcasted_iota(jnp.int32, bias_ref.shape, 0) // 8
    is_mid = (lax.axis_index("tp") + half) % 2 == 1
    key = lax.broadcasted_iota(jnp.int32, bias_ref.shape, 1) % (requests * page)
    offset = key // page - jnp.where(is_mid, owner_ref[mid], owner_ref[0])
    offset = jnp.where(offset < 0, offset + requests, offset)
    used = offset < jnp.where(is_mid, pages_ref[mid], pages_ref[0])
    bias_ref[...] = jnp.where(used, 0.0, MASKED)
    for copy in fetches[4:] + [send]:
        copy.wait()


def hand_over_kernel(*refs):
    pass


def hand_over(cost, *arrays):
    anywhere = pl.BlockSpec(memory_space=pl.ANY)
    return pl.pallas_call(
        hand_over_kernel,
        out_shape=[jax.ShapeDtypeStruct(array.shape, array.dtype) for array in arrays],
        in_specs=[anywhere] * len(arrays),
        out_specs=[anywhere] * len(arrays),
        input_output_aliases={i: i for i in range(len(arrays))},
        compiler_params=pltpu.CompilerParams(vmem_limit_bytes=2**20),
        cost_estimate=cost,
    )(*arrays)


def scores_of(rows, keys):
    scores = lax.dot_general(rows, keys, (((1,), (1,)), ((), ())), preferred_element_type=jnp.float32)
    return scores * (LOG2_E * 128 ** (-0.5))


def over(sums, totals):
    inverse = pl.reciprocal(totals, approx=True)
    return sums * (inverse * (2.0 - totals * inverse))


def weigh(weights, values):
    sums = dot(weights.astype(jnp.bfloat16), jnp.concatenate([values, jnp.ones_like(values)], 1))
    return sums[:, : values.shape[1]], sums[:, values.shape[1] :]


def own_kernel(leaf_len_ref, q_ref, *rest, page):
    local_refs = rest[:4]
    result_ref, level_ref, bias_ref, kf_ref, vf_ref = rest[4:]
    tokens, q_heads, dim = q_ref.shape
    group = q_heads // 4
    leaf_slots = bias_ref.shape[0] - 4 * tokens
    rank = lax.axis_index("tp")

    key = lax.broadcasted_iota(jnp.int32, (leaf_slots, dim), 0)
    bias_ref[0:leaf_slots] = jnp.where(key < leaf_len_ref[0] * page, 0.0, MASKED).astype(jnp.bfloat16)
    key = lax.broadcasted_iota(jnp.int32, (tokens, dim), 0)
    row = lax.broadcasted_iota(jnp.int32, (tokens, dim), 1)
    for step in range(4):
        seen = key <= row if step == 0 else jnp.full((tokens, dim), rank ^ step, jnp.int32) < rank
        bias_ref[leaf_slots + step * tokens : leaf_slots + (step + 1) * tokens] = jnp.where(
            seen, 0.0, MASKED
        ).astype(jnp.bfloat16)

    fresh_rows = local_refs[0].shape[0] - 2 * leaf_slots

    def fresh_source(out_row):
        head, kind, token = out_row // (2 * tokens), (out_row // tokens) % 2, out_row % tokens
        return token * 8 + head * 2 + kind

    fresh_pick = pick((fresh_rows, fresh_rows), fresh_source)
    for step in range(4):
        parts = dot(fresh_pick, local_refs[step][2 * leaf_slots :]).astype(jnp.bfloat16)
        for head in range(4):
            base = head * 2 * tokens
            kf_ref[head, step * tokens : (step + 1) * tokens] = parts[base : base + tokens]
            vf_ref[head, step * tokens : (step + 1) * tokens] = parts[base + tokens : base + 2 * tokens]

    chunk = 256
    half = chunk // 2
    leaf_pick = pick((chunk, chunk), lambda out_row: (out_row % half) * 2 + out_row // half)
    bias = bias_ref[...]
    token = lax.broadcasted_iota(jnp.int32, (tokens * group, dim), 0) // group
    column = lax.broadcasted_iota(jnp.int32, (tokens * group, dim), 1)
    own_row = jnp.where(token == column, 1.0, 0.0).astype(jnp.bfloat16)
    for step in range(4):
        head = rank ^ step
        leaf_k, leaf_v = [], []
        for piece in range(leaf_slots // half):
            parts = dot(leaf_pick, local_refs[step][piece * chunk : (piece + 1) * chunk]).astype(jnp.bfloat16)
            leaf_k.append(parts[:half])
            leaf_v.append(parts[half:])
        keys = jnp.concatenate([jnp.concatenate(leaf_k + [kf_ref[head]], 0), bias], 1)
        values = jnp.concatenate(leaf_v + [vf_ref[head]], 0)
        rows = q_ref[:, pl.ds(pl.multiple_of(head * group, group), group), :].reshape(tokens * group, dim)
        scores = scores_of(jnp.concatenate([rows, own_row], 1), keys)
        top = jnp.max(scores, axis=1, keepdims=True)
        sums, totals = weigh(jnp.exp2(scores - top), values)
        result_ref[step] = sums / totals
        level_ref[step] = jnp.log2(totals) + top


PAIRS = ((0, 1), (2, 3))


def blocks(a, b):
    zero = jnp.zeros_like(a)
    return jnp.concatenate([jnp.concatenate([a, zero], 1), jnp.concatenate([zero, b], 1)], 0)


def spread(a, b, width):
    lanes = a.shape[1]
    if width == lanes:
        return jnp.where(lax.broadcasted_iota(jnp.int32, a.shape, 1) < width // 2, a, b)
    return jnp.concatenate([a] * (width // 2 // lanes) + [b] * (width // 2 // lanes), 1)


def place_of(step, group):
    return pl.ds(pl.multiple_of((lax.axis_index("tp") ^ step) * group, group), group)


def kinds_of(pool_ref, step):
    rows = pool_ref[lax.axis_index("tp") ^ step].astype(jnp.float32)
    page, dim = rows.shape[1] // 2, rows.shape[2]
    return [rows[:, i * page : (i + 1) * page].reshape(-1, dim).astype(jnp.bfloat16) for i in range(2)]


def above_level(pair, q_ref, bias, level_ref, pool_ref):
    tokens, q_heads, dim = q_ref.shape
    group = q_heads // 4
    rows = [q_ref[:, place_of(step, group), :].reshape(tokens * group, dim) for step in pair]
    keys = blocks(*[kinds_of(pool_ref, step)[0] for step in pair])
    scores = scores_of(jnp.concatenate(rows, 1), keys)
    return scores + bias - spread(level_ref[pair[0]], level_ref[pair[1]], scores.shape[1])


def weigh_pair(pair, weights, pool_ref):
    values = [kinds_of(pool_ref, step)[1] for step in pair]
    ones = jnp.ones_like(values[0])
    return dot(weights, blocks(*values)), dot(weights, blocks(ones, ones))


def side_by_side(ref, pair):
    return jnp.concatenate([ref[step] for step in pair], 1)


def first_half_kernel(q_ref, bias_ref, other_ref, level_ref, pool_ref, sums_ref, totals_ref, peak_ref):
    peak = None
    scores = [above_level(pair, q_ref, bias_ref[0:1], level_ref, pool_ref) for pair in PAIRS]
    for i, pair in enumerate(PAIRS):
        weights = jnp.exp2(scores[i]).astype(jnp.bfloat16)
        peak = weights if peak is None else jnp.maximum(peak, weights)
        sums, totals = weigh_pair(pair, weights, pool_ref)
        sums_ref[i] = sums + side_by_side(other_ref, pair)
        totals_ref[i] = totals + 1.0
    peak = jnp.max(peak.astype(jnp.float32), axis=0, keepdims=True)
    peak_ref[...] = jnp.broadcast_to(peak, peak_ref.shape)


def second_half_kernel(
    q_ref, bias_ref, other_ref, level_ref, mine_ref, sums_ref, totals_ref, peak_ref, theirs_ref,
    out_hbm, stage_ref, sems,
):
    tokens, q_heads, dim = q_ref.shape
    group = q_heads // 4

    def write(pair, result):
        copies = []
        for i, step in enumerate(pair):
            part = result[:, i * dim : (i + 1) * dim]
            stage_ref[step] = part.astype(jnp.bfloat16).reshape(tokens, group, dim)
            target = out_hbm.at[:, place_of(step, group)]
            copies.append(pltpu.make_async_copy(stage_ref.at[step], target, sems.at[step]))
            copies[-1].start()
        return copies

    scores = [above_level(pair, q_ref, bias_ref[8:9], level_ref, theirs_ref) for pair in PAIRS]
    writes, weights = [], []
    for i, pair in enumerate(PAIRS):
        weights.append(jnp.exp2(scores[i]).astype(jnp.bfloat16))
        sums, totals = weigh_pair(pair, weights[-1], theirs_ref)
        writes += write(pair, over(sums + sums_ref[i], totals + totals_ref[i]))
    peak = jnp.maximum(jnp.max(functools.reduce(jnp.maximum, weights).astype(jnp.float32)), jnp.max(peak_ref[...]))
    for copy in writes:
        copy.wait()

    @pl.when(peak > 2.0**100)
    def _():
        for pair in PAIRS:
            mine = above_level(pair, q_ref, bias_ref[0:1], level_ref, mine_ref)
            theirs = above_level(pair, q_ref, bias_ref[8:9], level_ref, theirs_ref)
            both = jnp.maximum(mine, theirs)
            half = both.shape[1] // 2
            first = lax.broadcasted_iota(jnp.int32, both.shape, 1) < half
            tops = [
                jnp.maximum(jnp.max(jnp.where(first == (i == 0), both, 0.0), axis=1, keepdims=True), 0.0)
                for i in range(2)
            ]
            tops = [jnp.broadcast_to(top, (tokens * group, dim)) for top in tops]
            top = spread(*tops, both.shape[1])
            rest = jnp.exp2(-jnp.concatenate(tops, 1))
            sums, totals = weigh_pair(pair, jnp.exp2(mine - top).astype(jnp.bfloat16), mine_ref)
            more, added = weigh_pair(pair, jnp.exp2(theirs - top).astype(jnp.bfloat16), theirs_ref)
            sums = sums + more + side_by_side(other_ref, pair) * rest
            for copy in write(pair, over(sums, totals + added + rest)):
                copy.wait()


def per_device(queries, fresh, pool, leaf, parent, node_pages, node_owner, leaf_len):
    tp = lax.axis_size("tp")
    stripes = lax.axis_size("pool")
    shared_count, _, page, _, _, dim = pool.shape
    tokens, q_heads, _ = queries.shape
    vmem = pl.BlockSpec(memory_space=pltpu.VMEM)
    swap = lambda array, bit: lax.ppermute(array, "tp", [(i, i ^ bit) for i in range(tp)])
    hbm = pl.BlockSpec(memory_space=pltpu.HBM)

    pool_rows = pool.reshape(-1, dim)
    leaf_rows = leaf.reshape(-1, dim)
    fresh_rows = fresh.reshape(-1, dim)
    operands = (parent, node_pages, node_owner, pool_rows, leaf_rows, fresh_rows)
    sent, local_0, bias = pl.pallas_call(
        functools.partial(select_kernel, page),
        out_shape=[
            jax.ShapeDtypeStruct((tp, stripes, 2 * page, dim), jnp.bfloat16),
            jax.ShapeDtypeStruct((leaf_rows.shape[0] + fresh_rows.shape[0], dim), jnp.bfloat16),
            jax.ShapeDtypeStruct((16, stripes * 2 * page), jnp.float32),
        ],
        in_specs=[hbm] * 6,
        out_specs=[hbm, vmem, vmem],
        scratch_shapes=[
            pltpu.SMEM(parent.shape, jnp.int32),
            pltpu.SMEM(node_pages.shape, jnp.int32),
            pltpu.SMEM(node_owner.shape, jnp.int32),
            pltpu.VMEM(pool_rows.shape, jnp.bfloat16),
            pltpu.VMEM(pool_rows.shape, jnp.float32),
            pltpu.VMEM((tp, stripes, 2 * page, dim), jnp.bfloat16),
            pltpu.SemaphoreType.DMA((7,)),
        ],
        compiler_params=pltpu.CompilerParams(vmem_limit_bytes=16 * 2**20),
        cost_estimate=LONG,
    )(*[pltpu.with_memory_space_constraint(operand, pltpu.HBM) for operand in operands])
    local_2 = swap(local_0, 2)
    mine = lax.all_to_all(
        sent.reshape(tp * stripes, 2 * page, dim), ("tp", "pool"), split_axis=0, concat_axis=0, tiled=True
    ).reshape(tp, stripes, 2 * page, dim)
    local_0, local_2 = hand_over(LONG, local_0, local_2)
    local_1, local_3 = swap(local_0, 1), swap(local_2, 1)

    rows = tokens * q_heads // tp
    other, level = pl.pallas_call(
        functools.partial(own_kernel, page=page),
        out_shape=[jax.ShapeDtypeStruct((tp, rows, dim), jnp.float32)] * 2,
        in_specs=[pl.BlockSpec(memory_space=pltpu.SMEM)] + [vmem] * 5,
        out_specs=[vmem] * 2,
        scratch_shapes=[pltpu.VMEM((leaf.shape[1] + tp * tokens, dim), jnp.bfloat16)]
        + [pltpu.VMEM((tp, tp * tokens, dim), jnp.bfloat16)] * 2,
        compiler_params=pltpu.CompilerParams(vmem_limit_bytes=24 * 2**20),
        cost_estimate=SHORT,
    )(leaf_len, queries, local_0, local_1, local_2, local_3)
    mine, level = hand_over(SHORT, mine, level)
    theirs = swap(mine, 1)
    limit = pltpu.CompilerParams(vmem_limit_bytes=(24 if stripes <= 8 else 48) * 2**20)
    sums, totals, peak = pl.pallas_call(
        first_half_kernel,
        out_shape=[jax.ShapeDtypeStruct((len(PAIRS), rows, 2 * dim), jnp.float32)] * 2
        + [jax.ShapeDtypeStruct((8, bias.shape[1]), jnp.float32)],
        in_specs=[vmem] * 5,
        out_specs=[vmem] * 3,
        compiler_params=limit,
        cost_estimate=SHORT,
    )(queries, bias, other, level, mine)
    return pl.pallas_call(
        second_half_kernel,
        out_shape=jax.ShapeDtypeStruct(queries.shape, jnp.bfloat16),
        in_specs=[vmem] * 9,
        out_specs=hbm,
        scratch_shapes=[
            pltpu.VMEM((tp, tokens, q_heads // tp, dim), jnp.bfloat16),
            pltpu.SemaphoreType.DMA((tp,)),
        ],
        compiler_params=limit,
    )(queries, bias, other, level, mine, sums, totals, peak, theirs)


def solution(mesh):
    return jax.shard_map(
        per_device,
        mesh=mesh,
        in_specs=(
            P(("pool", "tp"), None, None),
            P(("pool", "tp"), None, None, None),
            P(None, "pool", None, "tp", None, None),
            P("pool", None, "tp", None, None),
            P(),
            P(),
            P(),
            P("pool"),
        ),
        out_specs=P(("pool", "tp"), None, None),
        check_vma=False,
    )
```

```python
import functools

import jax
import jax.numpy as jnp
from jax import lax
from jax.experimental import pallas as pl
from jax.experimental.pallas import tpu as pltpu
from jax.sharding import PartitionSpec as P

LOG2_E = 1.4426950408889634
MASKED = -1e30
LONG = pl.CostEstimate(flops=5 * 10**10, bytes_accessed=10**6, transcendentals=0)
SHORT = pl.CostEstimate(flops=10**6, bytes_accessed=10**5, transcendentals=0)


def pick(shape, source_row):
    row = lax.broadcasted_iota(jnp.int32, shape, 0)
    column = lax.broadcasted_iota(jnp.int32, shape, 1)
    return jnp.where(column == source_row(row), 1.0, 0.0).astype(jnp.bfloat16)


def dot(a, b):
    return lax.dot_general(a, b, (((1,), (0,)), ((), ())), preferred_element_type=jnp.float32)


def select_kernel(
    page, parent_hbm, pages_hbm, owner_hbm, pool_hbm, leaf_hbm, fresh_hbm,
    out_hbm, local_ref, bias_ref,
    parent_ref, pages_ref, owner_ref, pool_ref, rows_ref, block_ref, sems,
):
    leaf_rows, fresh_rows = leaf_hbm.shape[0], fresh_hbm.shape[0]
    pairs = [
        (pool_hbm, pool_ref),
        (parent_hbm, parent_ref),
        (pages_hbm, pages_ref),
        (owner_hbm, owner_ref),
        (leaf_hbm, local_ref.at[pl.ds(0, leaf_rows)]),
        (fresh_hbm, local_ref.at[pl.ds(leaf_rows, fresh_rows)]),
    ]
    fetches = [pltpu.make_async_copy(*pair, sems.at[i]) for i, pair in enumerate(pairs)]
    for fetch in fetches:
        fetch.start()
    node_count = pool_ref.shape[0] // (2 * page)
    copies, requests = out_hbm.shape[:2]
    fetches[0].wait()
    rows_ref[...] = pool_ref[...].astype(jnp.float32)
    root = [rows_ref[pl.ds(kind, page, stride=2)] for kind in range(2)]
    fetches[1].wait()

    def one(request, carry):
        mid = parent_ref[node_count + request] * (2 * page)
        chosen = [rows_ref[pl.ds(mid + kind, page, stride=2)] for kind in range(2)]
        for copy in range(copies):
            block = jnp.concatenate(root if copy % 2 == 0 else chosen, 0)
            block_ref[copy, request] = block.astype(jnp.bfloat16)
        return carry

    lax.fori_loop(0, requests, one, 0, unroll=requests <= 8)
    send = pltpu.make_async_copy(block_ref, out_hbm, sems.at[len(pairs)])
    send.start()

    fetches[2].wait()
    fetches[3].wait()
    mid = parent_ref[node_count + lax.axis_index("pool")]
    half = lax.broadcasted_iota(jnp.int32, bias_ref.shape, 0) // 8
    is_mid = (lax.axis_index("tp") + half) % 2 == 1
    key = lax.broadcasted_iota(jnp.int32, bias_ref.shape, 1) % (requests * page)
    offset = key // page - jnp.where(is_mid, owner_ref[mid], owner_ref[0])
    offset = jnp.where(offset < 0, offset + requests, offset)
    used = offset < jnp.where(is_mid, pages_ref[mid], pages_ref[0])
    bias_ref[...] = jnp.where(used, 0.0, MASKED)
    for copy in fetches[4:] + [send]:
        copy.wait()


def hand_over_kernel(*refs):
    pass


def hand_over(cost, *arrays):
    anywhere = pl.BlockSpec(memory_space=pl.ANY)
    return pl.pallas_call(
        hand_over_kernel,
        out_shape=[jax.ShapeDtypeStruct(array.shape, array.dtype) for array in arrays],
        in_specs=[anywhere] * len(arrays),
        out_specs=[anywhere] * len(arrays),
        input_output_aliases={i: i for i in range(len(arrays))},
        compiler_params=pltpu.CompilerParams(vmem_limit_bytes=2**20),
        cost_estimate=cost,
    )(*arrays)


def scores_of(rows, keys):
    scores = lax.dot_general(rows, keys, (((1,), (1,)), ((), ())), preferred_element_type=jnp.float32)
    return scores * (LOG2_E * 128 ** (-0.5))


def over(sums, totals):
    inverse = pl.reciprocal(totals, approx=True)
    return sums * (inverse * (2.0 - totals * inverse))


def weigh(weights, values):
    sums = dot(weights.astype(jnp.bfloat16), jnp.concatenate([values, jnp.ones_like(values)], 1))
    return sums[:, : values.shape[1]], sums[:, values.shape[1] :]


def own_kernel(leaf_len_ref, q_ref, *rest, page):
    local_refs = rest[:4]
    result_ref, level_ref, bias_ref, kf_ref, vf_ref = rest[4:]
    tokens, q_heads, dim = q_ref.shape
    group = q_heads // 4
    leaf_slots = bias_ref.shape[0] - 4 * tokens
    rank = lax.axis_index("tp")

    key = lax.broadcasted_iota(jnp.int32, (leaf_slots, dim), 0)
    bias_ref[0:leaf_slots] = jnp.where(key < leaf_len_ref[0] * page, 0.0, MASKED).astype(jnp.bfloat16)
    key = lax.broadcasted_iota(jnp.int32, (tokens, dim), 0)
    row = lax.broadcasted_iota(jnp.int32, (tokens, dim), 1)
    for step in range(4):
        seen = key <= row if step == 0 else jnp.full((tokens, dim), rank ^ step, jnp.int32) < rank
        bias_ref[leaf_slots + step * tokens : leaf_slots + (step + 1) * tokens] = jnp.where(
            seen, 0.0, MASKED
        ).astype(jnp.bfloat16)

    fresh_rows = local_refs[0].shape[0] - 2 * leaf_slots

    def fresh_source(out_row):
        head, kind, token = out_row // (2 * tokens), (out_row // tokens) % 2, out_row % tokens
        return token * 8 + head * 2 + kind

    fresh_pick = pick((fresh_rows, fresh_rows), fresh_source)
    for step in range(4):
        parts = dot(fresh_pick, local_refs[step][2 * leaf_slots :]).astype(jnp.bfloat16)
        for head in range(4):
            base = head * 2 * tokens
            kf_ref[head, step * tokens : (step + 1) * tokens] = parts[base : base + tokens]
            vf_ref[head, step * tokens : (step + 1) * tokens] = parts[base + tokens : base + 2 * tokens]

    chunk = 256
    half = chunk // 2
    leaf_pick = pick((chunk, chunk), lambda out_row: (out_row % half) * 2 + out_row // half)
    bias = bias_ref[...]
    token = lax.broadcasted_iota(jnp.int32, (tokens * group, dim), 0) // group
    column = lax.broadcasted_iota(jnp.int32, (tokens * group, dim), 1)
    own_row = jnp.where(token == column, 1.0, 0.0).astype(jnp.bfloat16)
    for step in range(4):
        head = rank ^ step
        leaf_k, leaf_v = [], []
        for piece in range(leaf_slots // half):
            parts = dot(leaf_pick, local_refs[step][piece * chunk : (piece + 1) * chunk]).astype(jnp.bfloat16)
            leaf_k.append(parts[:half])
            leaf_v.append(parts[half:])
        keys = jnp.concatenate([jnp.concatenate(leaf_k + [kf_ref[head]], 0), bias], 1)
        values = jnp.concatenate(leaf_v + [vf_ref[head]], 0)
        rows = q_ref[:, pl.ds(pl.multiple_of(head * group, group), group), :].reshape(tokens * group, dim)
        scores = scores_of(jnp.concatenate([rows, own_row], 1), keys)
        top = jnp.max(scores, axis=1, keepdims=True)
        sums, totals = weigh(jnp.exp2(scores - top), values)
        result_ref[step] = sums / totals
        level_ref[step] = jnp.log2(totals) + top


PAIRS = ((0, 1), (2, 3))


def blocks(a, b):
    zero = jnp.zeros_like(a)
    return jnp.concatenate([jnp.concatenate([a, zero], 1), jnp.concatenate([zero, b], 1)], 0)


def spread(a, b, width):
    lanes = a.shape[1]
    if width == lanes:
        return jnp.where(lax.broadcasted_iota(jnp.int32, a.shape, 1) < width // 2, a, b)
    return jnp.concatenate([a] * (width // 2 // lanes) + [b] * (width // 2 // lanes), 1)


def place_of(step, group):
    return pl.ds(pl.multiple_of((lax.axis_index("tp") ^ step) * group, group), group)


def kinds_of(pool_ref, step):
    rows = pool_ref[lax.axis_index("tp") ^ step].astype(jnp.float32)
    page, dim = rows.shape[1] // 2, rows.shape[2]
    return [rows[:, i * page : (i + 1) * page].reshape(-1, dim).astype(jnp.bfloat16) for i in range(2)]


def shift_of(pair, bias, level_ref):
    return bias - spread(level_ref[pair[0]], level_ref[pair[1]], bias.shape[1])


def above_level(pair, q_ref, shift, pool_ref):
    tokens, q_heads, dim = q_ref.shape
    group = q_heads // 4
    rows = [q_ref[:, place_of(step, group), :].reshape(tokens * group, dim) for step in pair]
    keys = blocks(*[kinds_of(pool_ref, step)[0] for step in pair])
    return scores_of(jnp.concatenate(rows, 1), keys) + shift


def weigh_pair(pair, weights, pool_ref):
    values = [kinds_of(pool_ref, step)[1] for step in pair]
    ones = jnp.ones_like(values[0])
    return dot(weights, blocks(*values)), dot(weights, blocks(ones, ones))


def side_by_side(ref, pair):
    return jnp.concatenate([ref[step] for step in pair], 1)


def first_half_kernel(q_ref, bias_ref, other_ref, level_ref, pool_ref, sums_ref, totals_ref, peak_ref, shift_ref):
    peak = None
    scores = [above_level(pair, q_ref, shift_of(pair, bias_ref[0:1], level_ref), pool_ref) for pair in PAIRS]
    for i, pair in enumerate(PAIRS):
        weights = jnp.exp2(scores[i]).astype(jnp.bfloat16)
        peak = weights if peak is None else jnp.maximum(peak, weights)
        sums, totals = weigh_pair(pair, weights, pool_ref)
        sums_ref[i] = sums + side_by_side(other_ref, pair)
        totals_ref[i] = totals + 1.0
        shift_ref[i] = shift_of(pair, bias_ref[8:9], level_ref)
    peak = jnp.max(peak.astype(jnp.float32), axis=0, keepdims=True)
    peak_ref[...] = jnp.broadcast_to(peak, peak_ref.shape)


def second_half_kernel(
    q_ref, bias_ref, other_ref, level_ref, mine_ref, sums_ref, totals_ref, peak_ref, shift_ref, theirs_ref,
    out_hbm, stage_ref, sems,
):
    tokens, q_heads, dim = q_ref.shape
    group = q_heads // 4

    def write(pair, result):
        copies = []
        for i, step in enumerate(pair):
            part = result[:, i * dim : (i + 1) * dim]
            stage_ref[step] = part.astype(jnp.bfloat16).reshape(tokens, group, dim)
            target = out_hbm.at[:, place_of(step, group)]
            copies.append(pltpu.make_async_copy(stage_ref.at[step], target, sems.at[step]))
            copies[-1].start()
        return copies

    scores = [above_level(pair, q_ref, shift_ref[i], theirs_ref) for i, pair in enumerate(PAIRS)]
    writes, weights = [], []
    for i, pair in enumerate(PAIRS):
        weights.append(jnp.exp2(scores[i]).astype(jnp.bfloat16))
        sums, totals = weigh_pair(pair, weights[-1], theirs_ref)
        writes += write(pair, over(sums + sums_ref[i], totals + totals_ref[i]))
    peak = jnp.maximum(jnp.max(functools.reduce(jnp.maximum, weights).astype(jnp.float32)), jnp.max(peak_ref[...]))
    for copy in writes:
        copy.wait()

    @pl.when(peak > 2.0**100)
    def _():
        for i, pair in enumerate(PAIRS):
            mine = above_level(pair, q_ref, shift_of(pair, bias_ref[0:1], level_ref), mine_ref)
            theirs = above_level(pair, q_ref, shift_ref[i], theirs_ref)
            both = jnp.maximum(mine, theirs)
            half = both.shape[1] // 2
            first = lax.broadcasted_iota(jnp.int32, both.shape, 1) < half
            tops = [
                jnp.maximum(jnp.max(jnp.where(first == (i == 0), both, 0.0), axis=1, keepdims=True), 0.0)
                for i in range(2)
            ]
            tops = [jnp.broadcast_to(top, (tokens * group, dim)) for top in tops]
            top = spread(*tops, both.shape[1])
            rest = jnp.exp2(-jnp.concatenate(tops, 1))
            sums, totals = weigh_pair(pair, jnp.exp2(mine - top).astype(jnp.bfloat16), mine_ref)
            more, added = weigh_pair(pair, jnp.exp2(theirs - top).astype(jnp.bfloat16), theirs_ref)
            sums = sums + more + side_by_side(other_ref, pair) * rest
            for copy in write(pair, over(sums, totals + added + rest)):
                copy.wait()


def per_device(queries, fresh, pool, leaf, parent, node_pages, node_owner, leaf_len):
    tp = lax.axis_size("tp")
    stripes = lax.axis_size("pool")
    shared_count, _, page, _, _, dim = pool.shape
    tokens, q_heads, _ = queries.shape
    vmem = pl.BlockSpec(memory_space=pltpu.VMEM)
    swap = lambda array, bit: lax.ppermute(array, "tp", [(i, i ^ bit) for i in range(tp)])
    hbm = pl.BlockSpec(memory_space=pltpu.HBM)

    pool_rows = pool.reshape(-1, dim)
    leaf_rows = leaf.reshape(-1, dim)
    fresh_rows = fresh.reshape(-1, dim)
    operands = (parent, node_pages, node_owner, pool_rows, leaf_rows, fresh_rows)
    sent, local_0, bias = pl.pallas_call(
        functools.partial(select_kernel, page),
        out_shape=[
            jax.ShapeDtypeStruct((tp, stripes, 2 * page, dim), jnp.bfloat16),
            jax.ShapeDtypeStruct((leaf_rows.shape[0] + fresh_rows.shape[0], dim), jnp.bfloat16),
            jax.ShapeDtypeStruct((16, stripes * 2 * page), jnp.float32),
        ],
        in_specs=[hbm] * 6,
        out_specs=[hbm, vmem, vmem],
        scratch_shapes=[
            pltpu.SMEM(parent.shape, jnp.int32),
            pltpu.SMEM(node_pages.shape, jnp.int32),
            pltpu.SMEM(node_owner.shape, jnp.int32),
            pltpu.VMEM(pool_rows.shape, jnp.bfloat16),
            pltpu.VMEM(pool_rows.shape, jnp.float32),
            pltpu.VMEM((tp, stripes, 2 * page, dim), jnp.bfloat16),
            pltpu.SemaphoreType.DMA((7,)),
        ],
        compiler_params=pltpu.CompilerParams(vmem_limit_bytes=16 * 2**20),
        cost_estimate=LONG,
    )(*[pltpu.with_memory_space_constraint(operand, pltpu.HBM) for operand in operands])
    local_2 = swap(local_0, 2)
    mine = lax.all_to_all(
        sent.reshape(tp * stripes, 2 * page, dim), ("tp", "pool"), split_axis=0, concat_axis=0, tiled=True
    ).reshape(tp, stripes, 2 * page, dim)
    local_0, local_2 = hand_over(LONG, local_0, local_2)
    local_1, local_3 = swap(local_0, 1), swap(local_2, 1)

    rows = tokens * q_heads // tp
    other, level = pl.pallas_call(
        functools.partial(own_kernel, page=page),
        out_shape=[jax.ShapeDtypeStruct((tp, rows, dim), jnp.float32)] * 2,
        in_specs=[pl.BlockSpec(memory_space=pltpu.SMEM)] + [vmem] * 5,
        out_specs=[vmem] * 2,
        scratch_shapes=[pltpu.VMEM((leaf.shape[1] + tp * tokens, dim), jnp.bfloat16)]
        + [pltpu.VMEM((tp, tp * tokens, dim), jnp.bfloat16)] * 2,
        compiler_params=pltpu.CompilerParams(vmem_limit_bytes=24 * 2**20),
        cost_estimate=SHORT,
    )(leaf_len, queries, local_0, local_1, local_2, local_3)
    mine, level = hand_over(SHORT, mine, level)
    theirs = swap(mine, 1)
    limit = pltpu.CompilerParams(vmem_limit_bytes=(24 if stripes <= 8 else 48) * 2**20)
    sums, totals, peak, shift = pl.pallas_call(
        first_half_kernel,
        out_shape=[jax.ShapeDtypeStruct((len(PAIRS), rows, 2 * dim), jnp.float32)] * 2
        + [jax.ShapeDtypeStruct((8, bias.shape[1]), jnp.float32)]
        + [jax.ShapeDtypeStruct((len(PAIRS), rows, bias.shape[1]), jnp.float32)],
        in_specs=[vmem] * 5,
        out_specs=[vmem] * 4,
        compiler_params=limit,
        cost_estimate=SHORT,
    )(queries, bias, other, level, mine)
    return pl.pallas_call(
        second_half_kernel,
        out_shape=jax.ShapeDtypeStruct(queries.shape, jnp.bfloat16),
        in_specs=[vmem] * 10,
        out_specs=hbm,
        scratch_shapes=[
            pltpu.VMEM((tp, tokens, q_heads // tp, dim), jnp.bfloat16),
            pltpu.SemaphoreType.DMA((tp,)),
        ],
        compiler_params=limit,
    )(queries, bias, other, level, mine, sums, totals, peak, shift, theirs)


def solution(mesh):
    return jax.shard_map(
        per_device,
        mesh=mesh,
        in_specs=(
            P(("pool", "tp"), None, None),
            P(("pool", "tp"), None, None, None),
            P(None, "pool", None, "tp", None, None),
            P("pool", None, "tp", None, None),
            P(),
            P(),
            P(),
            P("pool"),
        ),
        out_specs=P(("pool", "tp"), None, None),
        check_vma=False,
    )
```

```python
import functools

import jax
import jax.numpy as jnp
from jax import lax
from jax.experimental import pallas as pl
from jax.experimental.pallas import tpu as pltpu
from jax.sharding import PartitionSpec as P

LOG2_E = 1.4426950408889634
MASKED = -1e30
LONG = pl.CostEstimate(flops=5 * 10**10, bytes_accessed=10**6, transcendentals=0)
SHORT = pl.CostEstimate(flops=10**6, bytes_accessed=10**5, transcendentals=0)


def pick(shape, source_row):
    row = lax.broadcasted_iota(jnp.int32, shape, 0)
    column = lax.broadcasted_iota(jnp.int32, shape, 1)
    return jnp.where(column == source_row(row), 1.0, 0.0).astype(jnp.bfloat16)


def dot(a, b):
    return lax.dot_general(a, b, (((1,), (0,)), ((), ())), preferred_element_type=jnp.float32)


def select_kernel(
    page, parent_hbm, pages_hbm, owner_hbm, pool_hbm, leaf_hbm, fresh_hbm,
    out_hbm, local_ref, bias_ref,
    parent_ref, pages_ref, owner_ref, pool_ref, rows_ref, block_ref, sems,
):
    leaf_rows, fresh_rows = leaf_hbm.shape[0], fresh_hbm.shape[0]
    pairs = [
        (pool_hbm, pool_ref),
        (parent_hbm, parent_ref),
        (pages_hbm, pages_ref),
        (owner_hbm, owner_ref),
        (leaf_hbm, local_ref.at[pl.ds(0, leaf_rows)]),
        (fresh_hbm, local_ref.at[pl.ds(leaf_rows, fresh_rows)]),
    ]
    fetches = [pltpu.make_async_copy(*pair, sems.at[i]) for i, pair in enumerate(pairs)]
    for fetch in fetches[:4]:
        fetch.start()
    for fetch in fetches[4:]:
        fetch.start(priority=1)
    node_count = pool_ref.shape[0] // (2 * page)
    copies, requests = out_hbm.shape[:2]
    fetches[0].wait()
    rows_ref[...] = pool_ref[...].astype(jnp.float32)
    root = [rows_ref[pl.ds(kind, page, stride=2)] for kind in range(2)]
    fetches[1].wait()

    def one(request, carry):
        mid = parent_ref[node_count + request] * (2 * page)
        chosen = [rows_ref[pl.ds(mid + kind, page, stride=2)] for kind in range(2)]
        for copy in range(copies):
            block = jnp.concatenate(root if copy % 2 == 0 else chosen, 0)
            block_ref[copy, request] = block.astype(jnp.bfloat16)
        return carry

    lax.fori_loop(0, requests, one, 0, unroll=requests <= 8)
    send = pltpu.make_async_copy(block_ref, out_hbm, sems.at[len(pairs)])
    send.start()

    fetches[2].wait()
    fetches[3].wait()
    mid = parent_ref[node_count + lax.axis_index("pool")]
    half = lax.broadcasted_iota(jnp.int32, bias_ref.shape, 0) // 8
    is_mid = (lax.axis_index("tp") + half) % 2 == 1
    key = lax.broadcasted_iota(jnp.int32, bias_ref.shape, 1) % (requests * page)
    offset = key // page - jnp.where(is_mid, owner_ref[mid], owner_ref[0])
    offset = jnp.where(offset < 0, offset + requests, offset)
    used = offset < jnp.where(is_mid, pages_ref[mid], pages_ref[0])
    bias_ref[...] = jnp.where(used, 0.0, MASKED)
    for copy in fetches[4:] + [send]:
        copy.wait()


def hand_over_kernel(*refs):
    pass


def hand_over(cost, *arrays):
    anywhere = pl.BlockSpec(memory_space=pl.ANY)
    return pl.pallas_call(
        hand_over_kernel,
        out_shape=[jax.ShapeDtypeStruct(array.shape, array.dtype) for array in arrays],
        in_specs=[anywhere] * len(arrays),
        out_specs=[anywhere] * len(arrays),
        input_output_aliases={i: i for i in range(len(arrays))},
        compiler_params=pltpu.CompilerParams(vmem_limit_bytes=2**20),
        cost_estimate=cost,
    )(*arrays)


def scores_of(rows, keys):
    scores = lax.dot_general(rows, keys, (((1,), (1,)), ((), ())), preferred_element_type=jnp.float32)
    return scores * (LOG2_E * 128 ** (-0.5))


def over(sums, totals):
    inverse = pl.reciprocal(totals, approx=True)
    return sums * (inverse * (2.0 - totals * inverse))


def weigh(weights, values):
    sums = dot(weights.astype(jnp.bfloat16), jnp.concatenate([values, jnp.ones_like(values)], 1))
    return sums[:, : values.shape[1]], sums[:, values.shape[1] :]


def own_kernel(leaf_len_ref, q_ref, *rest, page):
    local_refs = rest[:4]
    result_ref, level_ref, bias_ref, kf_ref, vf_ref = rest[4:]
    tokens, q_heads, dim = q_ref.shape
    group = q_heads // 4
    leaf_slots = bias_ref.shape[0] - 4 * tokens
    rank = lax.axis_index("tp")

    key = lax.broadcasted_iota(jnp.int32, (leaf_slots, dim), 0)
    bias_ref[0:leaf_slots] = jnp.where(key < leaf_len_ref[0] * page, 0.0, MASKED).astype(jnp.bfloat16)
    key = lax.broadcasted_iota(jnp.int32, (tokens, dim), 0)
    row = lax.broadcasted_iota(jnp.int32, (tokens, dim), 1)
    for step in range(4):
        seen = key <= row if step == 0 else jnp.full((tokens, dim), rank ^ step, jnp.int32) < rank
        bias_ref[leaf_slots + step * tokens : leaf_slots + (step + 1) * tokens] = jnp.where(
            seen, 0.0, MASKED
        ).astype(jnp.bfloat16)

    fresh_rows = local_refs[0].shape[0] - 2 * leaf_slots

    def fresh_source(out_row):
        head, kind, token = out_row // (2 * tokens), (out_row // tokens) % 2, out_row % tokens
        return token * 8 + head * 2 + kind

    fresh_pick = pick((fresh_rows, fresh_rows), fresh_source)
    for step in range(4):
        parts = dot(fresh_pick, local_refs[step][2 * leaf_slots :]).astype(jnp.bfloat16)
        for head in range(4):
            base = head * 2 * tokens
            kf_ref[head, step * tokens : (step + 1) * tokens] = parts[base : base + tokens]
            vf_ref[head, step * tokens : (step + 1) * tokens] = parts[base + tokens : base + 2 * tokens]

    chunk = 256
    half = chunk // 2
    leaf_pick = pick((chunk, chunk), lambda out_row: (out_row % half) * 2 + out_row // half)
    bias = bias_ref[...]
    token = lax.broadcasted_iota(jnp.int32, (tokens * group, dim), 0) // group
    column = lax.broadcasted_iota(jnp.int32, (tokens * group, dim), 1)
    own_row = jnp.where(token == column, 1.0, 0.0).astype(jnp.bfloat16)
    for step in range(4):
        head = rank ^ step
        leaf_k, leaf_v = [], []
        for piece in range(leaf_slots // half):
            parts = dot(leaf_pick, local_refs[step][piece * chunk : (piece + 1) * chunk]).astype(jnp.bfloat16)
            leaf_k.append(parts[:half])
            leaf_v.append(parts[half:])
        keys = jnp.concatenate([jnp.concatenate(leaf_k + [kf_ref[head]], 0), bias], 1)
        values = jnp.concatenate(leaf_v + [vf_ref[head]], 0)
        rows = q_ref[:, pl.ds(pl.multiple_of(head * group, group), group), :].reshape(tokens * group, dim)
        scores = scores_of(jnp.concatenate([rows, own_row], 1), keys)
        top = jnp.max(scores, axis=1, keepdims=True)
        sums, totals = weigh(jnp.exp2(scores - top), values)
        result_ref[step] = sums / totals
        level_ref[step] = jnp.log2(totals) + top


PAIRS = ((0, 1), (2, 3))


def blocks(a, b):
    zero = jnp.zeros_like(a)
    return jnp.concatenate([jnp.concatenate([a, zero], 1), jnp.concatenate([zero, b], 1)], 0)


def spread(a, b, width):
    lanes = a.shape[1]
    if width == lanes:
        return jnp.where(lax.broadcasted_iota(jnp.int32, a.shape, 1) < width // 2, a, b)
    return jnp.concatenate([a] * (width // 2 // lanes) + [b] * (width // 2 // lanes), 1)


def place_of(step, group):
    return pl.ds(pl.multiple_of((lax.axis_index("tp") ^ step) * group, group), group)


def kinds_of(pool_ref, step):
    rows = pool_ref[lax.axis_index("tp") ^ step].astype(jnp.float32)
    page, dim = rows.shape[1] // 2, rows.shape[2]
    return [rows[:, i * page : (i + 1) * page].reshape(-1, dim).astype(jnp.bfloat16) for i in range(2)]


def above_level(pair, q_ref, bias, level_ref, pool_ref):
    tokens, q_heads, dim = q_ref.shape
    group = q_heads // 4
    rows = [q_ref[:, place_of(step, group), :].reshape(tokens * group, dim) for step in pair]
    keys = blocks(*[kinds_of(pool_ref, step)[0] for step in pair])
    scores = scores_of(jnp.concatenate(rows, 1), keys)
    return scores + bias - spread(level_ref[pair[0]], level_ref[pair[1]], scores.shape[1])


def weigh_pair(pair, weights, pool_ref):
    values = [kinds_of(pool_ref, step)[1] for step in pair]
    ones = jnp.ones_like(values[0])
    return dot(weights, blocks(*values)), dot(weights, blocks(ones, ones))


def side_by_side(ref, pair):
    return jnp.concatenate([ref[step] for step in pair], 1)


def first_half_kernel(q_ref, bias_ref, other_ref, level_ref, pool_ref, sums_ref, totals_ref, peak_ref):
    peak = None
    scores = [above_level(pair, q_ref, bias_ref[0:1], level_ref, pool_ref) for pair in PAIRS]
    for i, pair in enumerate(PAIRS):
        weights = jnp.exp2(scores[i]).astype(jnp.bfloat16)
        peak = weights if peak is None else jnp.maximum(peak, weights)
        sums, totals = weigh_pair(pair, weights, pool_ref)
        sums_ref[i] = sums + side_by_side(other_ref, pair)
        totals_ref[i] = totals + 1.0
    peak = jnp.max(peak.astype(jnp.float32), axis=0, keepdims=True)
    peak_ref[...] = jnp.broadcast_to(peak, peak_ref.shape)


def second_half_kernel(
    q_ref, bias_ref, other_ref, level_ref, mine_ref, sums_ref, totals_ref, peak_ref, theirs_ref,
    out_hbm, stage_ref, sems,
):
    tokens, q_heads, dim = q_ref.shape
    group = q_heads // 4

    def write(pair, result):
        copies = []
        for i, step in enumerate(pair):
            part = result[:, i * dim : (i + 1) * dim]
            stage_ref[step] = part.astype(jnp.bfloat16).reshape(tokens, group, dim)
            target = out_hbm.at[:, place_of(step, group)]
            copies.append(pltpu.make_async_copy(stage_ref.at[step], target, sems.at[step]))
            copies[-1].start(priority=i)
        return copies

    scores = [above_level(pair, q_ref, bias_ref[8:9], level_ref, theirs_ref) for pair in PAIRS]
    writes, weights = [], []
    for i, pair in enumerate(PAIRS):
        weights.append(jnp.exp2(scores[i]).astype(jnp.bfloat16))
        sums, totals = weigh_pair(pair, weights[-1], theirs_ref)
        writes += write(pair, over(sums + sums_ref[i], totals + totals_ref[i]))
    peak = jnp.maximum(jnp.max(functools.reduce(jnp.maximum, weights).astype(jnp.float32)), jnp.max(peak_ref[...]))
    for copy in writes:
        copy.wait()

    @pl.when(peak > 2.0**100)
    def _():
        for pair in PAIRS:
            mine = above_level(pair, q_ref, bias_ref[0:1], level_ref, mine_ref)
            theirs = above_level(pair, q_ref, bias_ref[8:9], level_ref, theirs_ref)
            both = jnp.maximum(mine, theirs)
            half = both.shape[1] // 2
            first = lax.broadcasted_iota(jnp.int32, both.shape, 1) < half
            tops = [
                jnp.maximum(jnp.max(jnp.where(first == (i == 0), both, 0.0), axis=1, keepdims=True), 0.0)
                for i in range(2)
            ]
            tops = [jnp.broadcast_to(top, (tokens * group, dim)) for top in tops]
            top = spread(*tops, both.shape[1])
            rest = jnp.exp2(-jnp.concatenate(tops, 1))
            sums, totals = weigh_pair(pair, jnp.exp2(mine - top).astype(jnp.bfloat16), mine_ref)
            more, added = weigh_pair(pair, jnp.exp2(theirs - top).astype(jnp.bfloat16), theirs_ref)
            sums = sums + more + side_by_side(other_ref, pair) * rest
            for copy in write(pair, over(sums, totals + added + rest)):
                copy.wait()


def per_device(queries, fresh, pool, leaf, parent, node_pages, node_owner, leaf_len):
    tp = lax.axis_size("tp")
    stripes = lax.axis_size("pool")
    shared_count, _, page, _, _, dim = pool.shape
    tokens, q_heads, _ = queries.shape
    vmem = pl.BlockSpec(memory_space=pltpu.VMEM)
    swap = lambda array, bit: lax.ppermute(array, "tp", [(i, i ^ bit) for i in range(tp)])
    hbm = pl.BlockSpec(memory_space=pltpu.HBM)

    pool_rows = pool.reshape(-1, dim)
    leaf_rows = leaf.reshape(-1, dim)
    fresh_rows = fresh.reshape(-1, dim)
    operands = (parent, node_pages, node_owner, pool_rows, leaf_rows, fresh_rows)
    sent, local_0, bias = pl.pallas_call(
        functools.partial(select_kernel, page),
        out_shape=[
            jax.ShapeDtypeStruct((tp, stripes, 2 * page, dim), jnp.bfloat16),
            jax.ShapeDtypeStruct((leaf_rows.shape[0] + fresh_rows.shape[0], dim), jnp.bfloat16),
            jax.ShapeDtypeStruct((16, stripes * 2 * page), jnp.float32),
        ],
        in_specs=[hbm] * 6,
        out_specs=[hbm, vmem, vmem],
        scratch_shapes=[
            pltpu.SMEM(parent.shape, jnp.int32),
            pltpu.SMEM(node_pages.shape, jnp.int32),
            pltpu.SMEM(node_owner.shape, jnp.int32),
            pltpu.VMEM(pool_rows.shape, jnp.bfloat16),
            pltpu.VMEM(pool_rows.shape, jnp.float32),
            pltpu.VMEM((tp, stripes, 2 * page, dim), jnp.bfloat16),
            pltpu.SemaphoreType.DMA((7,)),
        ],
        compiler_params=pltpu.CompilerParams(vmem_limit_bytes=16 * 2**20),
        cost_estimate=LONG,
    )(*[pltpu.with_memory_space_constraint(operand, pltpu.HBM) for operand in operands])
    local_2 = swap(local_0, 2)
    mine = lax.all_to_all(
        sent.reshape(tp * stripes, 2 * page, dim), ("tp", "pool"), split_axis=0, concat_axis=0, tiled=True
    ).reshape(tp, stripes, 2 * page, dim)
    local_0, local_2 = hand_over(LONG, local_0, local_2)
    local_1, local_3 = swap(local_0, 1), swap(local_2, 1)

    rows = tokens * q_heads // tp
    other, level = pl.pallas_call(
        functools.partial(own_kernel, page=page),
        out_shape=[jax.ShapeDtypeStruct((tp, rows, dim), jnp.float32)] * 2,
        in_specs=[pl.BlockSpec(memory_space=pltpu.SMEM)] + [vmem] * 5,
        out_specs=[vmem] * 2,
        scratch_shapes=[pltpu.VMEM((leaf.shape[1] + tp * tokens, dim), jnp.bfloat16)]
        + [pltpu.VMEM((tp, tp * tokens, dim), jnp.bfloat16)] * 2,
        compiler_params=pltpu.CompilerParams(vmem_limit_bytes=24 * 2**20),
        cost_estimate=SHORT,
    )(leaf_len, queries, local_0, local_1, local_2, local_3)
    mine, level = hand_over(SHORT, mine, level)
    theirs = swap(mine, 1)
    limit = pltpu.CompilerParams(vmem_limit_bytes=(24 if stripes <= 8 else 48) * 2**20)
    sums, totals, peak = pl.pallas_call(
        first_half_kernel,
        out_shape=[jax.ShapeDtypeStruct((len(PAIRS), rows, 2 * dim), jnp.float32)] * 2
        + [jax.ShapeDtypeStruct((8, bias.shape[1]), jnp.float32)],
        in_specs=[vmem] * 5,
        out_specs=[vmem] * 3,
        compiler_params=limit,
        cost_estimate=SHORT,
    )(queries, bias, other, level, mine)
    return pl.pallas_call(
        second_half_kernel,
        out_shape=jax.ShapeDtypeStruct(queries.shape, jnp.bfloat16),
        in_specs=[vmem] * 9,
        out_specs=hbm,
        scratch_shapes=[
            pltpu.VMEM((tp, tokens, q_heads // tp, dim), jnp.bfloat16),
            pltpu.SemaphoreType.DMA((tp,)),
        ],
        compiler_params=limit,
    )(queries, bias, other, level, mine, sums, totals, peak, theirs)


def solution(mesh):
    return jax.shard_map(
        per_device,
        mesh=mesh,
        in_specs=(
            P(("pool", "tp"), None, None),
            P(("pool", "tp"), None, None, None),
            P(None, "pool", None, "tp", None, None),
            P("pool", None, "tp", None, None),
            P(),
            P(),
            P(),
            P("pool"),
        ),
        out_specs=P(("pool", "tp"), None, None),
        check_vma=False,
    )
```

```python
import functools

import jax
import jax.numpy as jnp
from jax import lax
from jax.experimental import pallas as pl
from jax.experimental.pallas import tpu as pltpu
from jax.sharding import PartitionSpec as P

LOG2_E = 1.4426950408889634
MASKED = -1e30
LONG = pl.CostEstimate(flops=5 * 10**10, bytes_accessed=10**6, transcendentals=0)
SHORT = pl.CostEstimate(flops=10**6, bytes_accessed=10**5, transcendentals=0)


def pick(shape, source_row):
    row = lax.broadcasted_iota(jnp.int32, shape, 0)
    column = lax.broadcasted_iota(jnp.int32, shape, 1)
    return jnp.where(column == source_row(row), 1.0, 0.0).astype(jnp.bfloat16)


def dot(a, b):
    return lax.dot_general(a, b, (((1,), (0,)), ((), ())), preferred_element_type=jnp.float32)


def select_kernel(
    page, parent_hbm, pages_hbm, owner_hbm, pool_hbm, leaf_hbm, fresh_hbm,
    out_hbm, local_ref, bias_ref,
    parent_ref, pages_ref, owner_ref, pool_ref, rows_ref, block_ref, sems,
):
    leaf_rows, fresh_rows = leaf_hbm.shape[0], fresh_hbm.shape[0]
    pairs = [
        (pool_hbm, pool_ref),
        (parent_hbm, parent_ref),
        (pages_hbm, pages_ref),
        (owner_hbm, owner_ref),
        (leaf_hbm, local_ref.at[pl.ds(0, leaf_rows)]),
        (fresh_hbm, local_ref.at[pl.ds(leaf_rows, fresh_rows)]),
    ]
    fetches = [pltpu.make_async_copy(*pair, sems.at[i]) for i, pair in enumerate(pairs)]
    for fetch in fetches[:4]:
        fetch.start()
    node_count = pool_ref.shape[0] // (2 * page)
    copies, requests = out_hbm.shape[:2]
    fetches[0].wait()
    for fetch in fetches[4:]:
        fetch.start()
    rows_ref[...] = pool_ref[...].astype(jnp.float32)
    root = [rows_ref[pl.ds(kind, page, stride=2)] for kind in range(2)]
    fetches[1].wait()

    def one(request, carry):
        mid = parent_ref[node_count + request] * (2 * page)
        chosen = [rows_ref[pl.ds(mid + kind, page, stride=2)] for kind in range(2)]
        for copy in range(copies):
            block = jnp.concatenate(root if copy % 2 == 0 else chosen, 0)
            block_ref[copy, request] = block.astype(jnp.bfloat16)
        return carry

    lax.fori_loop(0, requests, one, 0, unroll=requests <= 8)
    send = pltpu.make_async_copy(block_ref, out_hbm, sems.at[len(pairs)])
    send.start()

    fetches[2].wait()
    fetches[3].wait()
    mid = parent_ref[node_count + lax.axis_index("pool")]
    half = lax.broadcasted_iota(jnp.int32, bias_ref.shape, 0) // 8
    is_mid = (lax.axis_index("tp") + half) % 2 == 1
    key = lax.broadcasted_iota(jnp.int32, bias_ref.shape, 1) % (requests * page)
    offset = key // page - jnp.where(is_mid, owner_ref[mid], owner_ref[0])
    offset = jnp.where(offset < 0, offset + requests, offset)
    used = offset < jnp.where(is_mid, pages_ref[mid], pages_ref[0])
    bias_ref[...] = jnp.where(used, 0.0, MASKED)
    for copy in fetches[4:] + [send]:
        copy.wait()


def hand_over_kernel(*refs):
    pass


def hand_over(cost, *arrays):
    anywhere = pl.BlockSpec(memory_space=pl.ANY)
    return pl.pallas_call(
        hand_over_kernel,
        out_shape=[jax.ShapeDtypeStruct(array.shape, array.dtype) for array in arrays],
        in_specs=[anywhere] * len(arrays),
        out_specs=[anywhere] * len(arrays),
        input_output_aliases={i: i for i in range(len(arrays))},
        compiler_params=pltpu.CompilerParams(vmem_limit_bytes=2**20),
        cost_estimate=cost,
    )(*arrays)


def scores_of(rows, keys):
    scores = lax.dot_general(rows, keys, (((1,), (1,)), ((), ())), preferred_element_type=jnp.float32)
    return scores * (LOG2_E * 128 ** (-0.5))


def over(sums, totals):
    inverse = pl.reciprocal(totals, approx=True)
    return sums * (inverse * (2.0 - totals * inverse))


def weigh(weights, values):
    sums = dot(weights.astype(jnp.bfloat16), jnp.concatenate([values, jnp.ones_like(values)], 1))
    return sums[:, : values.shape[1]], sums[:, values.shape[1] :]


def own_kernel(leaf_len_ref, q_ref, *rest, page):
    local_refs = rest[:4]
    result_ref, level_ref, bias_ref, kf_ref, vf_ref = rest[4:]
    tokens, q_heads, dim = q_ref.shape
    group = q_heads // 4
    leaf_slots = bias_ref.shape[0] - 4 * tokens
    rank = lax.axis_index("tp")

    key = lax.broadcasted_iota(jnp.int32, (leaf_slots, dim), 0)
    bias_ref[0:leaf_slots] = jnp.where(key < leaf_len_ref[0] * page, 0.0, MASKED).astype(jnp.bfloat16)
    key = lax.broadcasted_iota(jnp.int32, (tokens, dim), 0)
    row = lax.broadcasted_iota(jnp.int32, (tokens, dim), 1)
    for step in range(4):
        seen = key <= row if step == 0 else jnp.full((tokens, dim), rank ^ step, jnp.int32) < rank
        bias_ref[leaf_slots + step * tokens : leaf_slots + (step + 1) * tokens] = jnp.where(
            seen, 0.0, MASKED
        ).astype(jnp.bfloat16)

    fresh_rows = local_refs[0].shape[0] - 2 * leaf_slots

    def fresh_source(out_row):
        head, kind, token = out_row // (2 * tokens), (out_row // tokens) % 2, out_row % tokens
        return token * 8 + head * 2 + kind

    fresh_pick = pick((fresh_rows, fresh_rows), fresh_source)
    for step in range(4):
        parts = dot(fresh_pick, local_refs[step][2 * leaf_slots :]).astype(jnp.bfloat16)
        for head in range(4):
            base = head * 2 * tokens
            kf_ref[head, step * tokens : (step + 1) * tokens] = parts[base : base + tokens]
            vf_ref[head, step * tokens : (step + 1) * tokens] = parts[base + tokens : base + 2 * tokens]

    chunk = 256
    half = chunk // 2
    leaf_pick = pick((chunk, chunk), lambda out_row: (out_row % half) * 2 + out_row // half)
    bias = bias_ref[...]
    token = lax.broadcasted_iota(jnp.int32, (tokens * group, dim), 0) // group
    column = lax.broadcasted_iota(jnp.int32, (tokens * group, dim), 1)
    own_row = jnp.where(token == column, 1.0, 0.0).astype(jnp.bfloat16)
    for step in range(4):
        head = rank ^ step
        leaf_k, leaf_v = [], []
        for piece in range(leaf_slots // half):
            parts = dot(leaf_pick, local_refs[step][piece * chunk : (piece + 1) * chunk]).astype(jnp.bfloat16)
            leaf_k.append(parts[:half])
            leaf_v.append(parts[half:])
        keys = jnp.concatenate([jnp.concatenate(leaf_k + [kf_ref[head]], 0), bias], 1)
        values = jnp.concatenate(leaf_v + [vf_ref[head]], 0)
        rows = q_ref[:, pl.ds(pl.multiple_of(head * group, group), group), :].reshape(tokens * group, dim)
        scores = scores_of(jnp.concatenate([rows, own_row], 1), keys)
        top = jnp.max(scores, axis=1, keepdims=True)
        sums, totals = weigh(jnp.exp2(scores - top), values)
        result_ref[step] = sums / totals
        level_ref[step] = jnp.log2(totals) + top


PAIRS = ((0, 1), (2, 3))


def blocks(a, b):
    zero = jnp.zeros_like(a)
    return jnp.concatenate([jnp.concatenate([a, zero], 1), jnp.concatenate([zero, b], 1)], 0)


def spread(a, b, width):
    lanes = a.shape[1]
    if width == lanes:
        return jnp.where(lax.broadcasted_iota(jnp.int32, a.shape, 1) < width // 2, a, b)
    return jnp.concatenate([a] * (width // 2 // lanes) + [b] * (width // 2 // lanes), 1)


def place_of(step, group):
    return pl.ds(pl.multiple_of((lax.axis_index("tp") ^ step) * group, group), group)


def kinds_of(pool_ref, step):
    rows = pool_ref[lax.axis_index("tp") ^ step].astype(jnp.float32)
    page, dim = rows.shape[1] // 2, rows.shape[2]
    return [rows[:, i * page : (i + 1) * page].reshape(-1, dim).astype(jnp.bfloat16) for i in range(2)]


def above_level(pair, q_ref, bias, level_ref, pool_ref):
    tokens, q_heads, dim = q_ref.shape
    group = q_heads // 4
    rows = [q_ref[:, place_of(step, group), :].reshape(tokens * group, dim) for step in pair]
    keys = blocks(*[kinds_of(pool_ref, step)[0] for step in pair])
    scores = scores_of(jnp.concatenate(rows, 1), keys)
    return scores + bias - spread(level_ref[pair[0]], level_ref[pair[1]], scores.shape[1])


def weigh_pair(pair, weights, pool_ref):
    values = [kinds_of(pool_ref, step)[1] for step in pair]
    ones = jnp.ones_like(values[0])
    return dot(weights, blocks(*values)), dot(weights, blocks(ones, ones))


def side_by_side(ref, pair):
    return jnp.concatenate([ref[step] for step in pair], 1)


def first_half_kernel(q_ref, bias_ref, other_ref, level_ref, pool_ref, sums_ref, totals_ref, peak_ref):
    peak = None
    scores = [above_level(pair, q_ref, bias_ref[0:1], level_ref, pool_ref) for pair in PAIRS]
    for i, pair in enumerate(PAIRS):
        weights = jnp.exp2(scores[i]).astype(jnp.bfloat16)
        peak = weights if peak is None else jnp.maximum(peak, weights)
        sums, totals = weigh_pair(pair, weights, pool_ref)
        sums_ref[i] = sums + side_by_side(other_ref, pair)
        totals_ref[i] = totals + 1.0
    peak = jnp.max(peak.astype(jnp.float32), axis=0, keepdims=True)
    peak_ref[...] = jnp.broadcast_to(peak, peak_ref.shape)


def second_half_kernel(
    q_ref, bias_ref, other_ref, level_ref, mine_ref, sums_ref, totals_ref, peak_ref, theirs_ref,
    out_hbm, stage_ref, sems,
):
    tokens, q_heads, dim = q_ref.shape
    group = q_heads // 4

    def write(pair, result):
        copies = []
        for i, step in enumerate(pair):
            part = result[:, i * dim : (i + 1) * dim]
            stage_ref[step] = part.astype(jnp.bfloat16).reshape(tokens, group, dim)
            target = out_hbm.at[:, place_of(step, group)]
            copies.append(pltpu.make_async_copy(stage_ref.at[step], target, sems.at[step]))
            copies[-1].start()
        return copies

    writes, weights = [], []
    for i, pair in enumerate(PAIRS):
        scores = above_level(pair, q_ref, bias_ref[8:9], level_ref, theirs_ref)
        weights.append(jnp.exp2(scores).astype(jnp.bfloat16))
        sums, totals = weigh_pair(pair, weights[-1], theirs_ref)
        writes += write(pair, over(sums + sums_ref[i], totals + totals_ref[i]))
    peak = jnp.maximum(jnp.max(functools.reduce(jnp.maximum, weights).astype(jnp.float32)), jnp.max(peak_ref[...]))
    for copy in writes:
        copy.wait()

    @pl.when(peak > 2.0**100)
    def _():
        for pair in PAIRS:
            mine = above_level(pair, q_ref, bias_ref[0:1], level_ref, mine_ref)
            theirs = above_level(pair, q_ref, bias_ref[8:9], level_ref, theirs_ref)
            both = jnp.maximum(mine, theirs)
            half = both.shape[1] // 2
            first = lax.broadcasted_iota(jnp.int32, both.shape, 1) < half
            tops = [
                jnp.maximum(jnp.max(jnp.where(first == (i == 0), both, 0.0), axis=1, keepdims=True), 0.0)
                for i in range(2)
            ]
            tops = [jnp.broadcast_to(top, (tokens * group, dim)) for top in tops]
            top = spread(*tops, both.shape[1])
            rest = jnp.exp2(-jnp.concatenate(tops, 1))
            sums, totals = weigh_pair(pair, jnp.exp2(mine - top).astype(jnp.bfloat16), mine_ref)
            more, added = weigh_pair(pair, jnp.exp2(theirs - top).astype(jnp.bfloat16), theirs_ref)
            sums = sums + more + side_by_side(other_ref, pair) * rest
            for copy in write(pair, over(sums, totals + added + rest)):
                copy.wait()


def per_device(queries, fresh, pool, leaf, parent, node_pages, node_owner, leaf_len):
    tp = lax.axis_size("tp")
    stripes = lax.axis_size("pool")
    shared_count, _, page, _, _, dim = pool.shape
    tokens, q_heads, _ = queries.shape
    vmem = pl.BlockSpec(memory_space=pltpu.VMEM)
    swap = lambda array, bit: lax.ppermute(array, "tp", [(i, i ^ bit) for i in range(tp)])
    hbm = pl.BlockSpec(memory_space=pltpu.HBM)

    pool_rows = pool.reshape(-1, dim)
    leaf_rows = leaf.reshape(-1, dim)
    fresh_rows = fresh.reshape(-1, dim)
    operands = (parent, node_pages, node_owner, pool_rows, leaf_rows, fresh_rows)
    sent, local_0, bias = pl.pallas_call(
        functools.partial(select_kernel, page),
        out_shape=[
            jax.ShapeDtypeStruct((tp, stripes, 2 * page, dim), jnp.bfloat16),
            jax.ShapeDtypeStruct((leaf_rows.shape[0] + fresh_rows.shape[0], dim), jnp.bfloat16),
            jax.ShapeDtypeStruct((16, stripes * 2 * page), jnp.float32),
        ],
        in_specs=[hbm] * 6,
        out_specs=[hbm, vmem, vmem],
        scratch_shapes=[
            pltpu.SMEM(parent.shape, jnp.int32),
            pltpu.SMEM(node_pages.shape, jnp.int32),
            pltpu.SMEM(node_owner.shape, jnp.int32),
            pltpu.VMEM(pool_rows.shape, jnp.bfloat16),
            pltpu.VMEM(pool_rows.shape, jnp.float32),
            pltpu.VMEM((tp, stripes, 2 * page, dim), jnp.bfloat16),
            pltpu.SemaphoreType.DMA((7,)),
        ],
        compiler_params=pltpu.CompilerParams(vmem_limit_bytes=16 * 2**20),
        cost_estimate=LONG,
    )(*[pltpu.with_memory_space_constraint(operand, pltpu.HBM) for operand in operands])
    local_2 = swap(local_0, 2)
    mine = lax.all_to_all(
        sent.reshape(tp * stripes, 2 * page, dim), ("tp", "pool"), split_axis=0, concat_axis=0, tiled=True
    ).reshape(tp, stripes, 2 * page, dim)
    local_0, local_2 = hand_over(LONG, local_0, local_2)
    local_1, local_3 = swap(local_0, 1), swap(local_2, 1)

    rows = tokens * q_heads // tp
    other, level = pl.pallas_call(
        functools.partial(own_kernel, page=page),
        out_shape=[jax.ShapeDtypeStruct((tp, rows, dim), jnp.float32)] * 2,
        in_specs=[pl.BlockSpec(memory_space=pltpu.SMEM)] + [vmem] * 5,
        out_specs=[vmem] * 2,
        scratch_shapes=[pltpu.VMEM((leaf.shape[1] + tp * tokens, dim), jnp.bfloat16)]
        + [pltpu.VMEM((tp, tp * tokens, dim), jnp.bfloat16)] * 2,
        compiler_params=pltpu.CompilerParams(vmem_limit_bytes=24 * 2**20),
        cost_estimate=SHORT,
    )(leaf_len, queries, local_0, local_1, local_2, local_3)
    mine, level = hand_over(SHORT, mine, level)
    theirs = swap(mine, 1)
    limit = pltpu.CompilerParams(vmem_limit_bytes=(24 if stripes <= 8 else 48) * 2**20)
    sums, totals, peak = pl.pallas_call(
        first_half_kernel,
        out_shape=[jax.ShapeDtypeStruct((len(PAIRS), rows, 2 * dim), jnp.float32)] * 2
        + [jax.ShapeDtypeStruct((8, bias.shape[1]), jnp.float32)],
        in_specs=[vmem] * 5,
        out_specs=[vmem] * 3,
        compiler_params=limit,
        cost_estimate=SHORT,
    )(queries, bias, other, level, mine)
    return pl.pallas_call(
        second_half_kernel,
        out_shape=jax.ShapeDtypeStruct(queries.shape, jnp.bfloat16),
        in_specs=[vmem] * 9,
        out_specs=hbm,
        scratch_shapes=[
            pltpu.VMEM((tp, tokens, q_heads // tp, dim), jnp.bfloat16),
            pltpu.SemaphoreType.DMA((tp,)),
        ],
        compiler_params=limit,
    )(queries, bias, other, level, mine, sums, totals, peak, theirs)


def solution(mesh):
    return jax.shard_map(
        per_device,
        mesh=mesh,
        in_specs=(
            P(("pool", "tp"), None, None),
            P(("pool", "tp"), None, None, None),
            P(None, "pool", None, "tp", None, None),
            P("pool", None, "tp", None, None),
            P(),
            P(),
            P(),
            P("pool"),
        ),
        out_specs=P(("pool", "tp"), None, None),
        check_vma=False,
    )
```

```python
import functools

import jax
import jax.numpy as jnp
from jax import lax
from jax.experimental import pallas as pl
from jax.experimental.pallas import tpu as pltpu
from jax.sharding import PartitionSpec as P

LOG2_E = 1.4426950408889634
MASKED = -1e30
LONG = pl.CostEstimate(flops=5 * 10**10, bytes_accessed=10**6, transcendentals=0)
SHORT = pl.CostEstimate(flops=10**6, bytes_accessed=10**5, transcendentals=0)


def pick(shape, source_row):
    row = lax.broadcasted_iota(jnp.int32, shape, 0)
    column = lax.broadcasted_iota(jnp.int32, shape, 1)
    return jnp.where(column == source_row(row), 1.0, 0.0).astype(jnp.bfloat16)


def dot(a, b):
    return lax.dot_general(a, b, (((1,), (0,)), ((), ())), preferred_element_type=jnp.float32)


def select_kernel(
    page, parent_hbm, pages_hbm, owner_hbm, pool_hbm, leaf_hbm, fresh_hbm,
    out_hbm, local_ref, bias_ref,
    parent_ref, pages_ref, owner_ref, pool_ref, rows_ref, block_ref, sems,
):
    leaf_rows, fresh_rows = leaf_hbm.shape[0], fresh_hbm.shape[0]
    pairs = [
        (pool_hbm, pool_ref),
        (parent_hbm, parent_ref),
        (pages_hbm, pages_ref),
        (owner_hbm, owner_ref),
        (leaf_hbm, local_ref.at[pl.ds(0, leaf_rows)]),
        (fresh_hbm, local_ref.at[pl.ds(leaf_rows, fresh_rows)]),
    ]
    fetches = [pltpu.make_async_copy(*pair, sems.at[i]) for i, pair in enumerate(pairs)]
    for fetch in fetches:
        fetch.start()
    node_count = pool_ref.shape[0] // (2 * page)
    copies, requests = out_hbm.shape[:2]
    fetches[0].wait()
    rows_ref[...] = pool_ref[...].astype(jnp.float32)
    root = [rows_ref[pl.ds(kind, page, stride=2)] for kind in range(2)]
    fetches[1].wait()

    def one(request, carry):
        mid = parent_ref[node_count + request] * (2 * page)
        chosen = [rows_ref[pl.ds(mid + kind, page, stride=2)] for kind in range(2)]
        for copy in range(copies):
            block = jnp.concatenate(root if copy % 2 == 0 else chosen, 0)
            block_ref[copy, request] = block.astype(jnp.bfloat16)
        return carry

    lax.fori_loop(0, requests, one, 0, unroll=requests <= 8)
    send = pltpu.make_async_copy(block_ref, out_hbm, sems.at[len(pairs)])
    send.start()

    fetches[2].wait()
    fetches[3].wait()
    mid = parent_ref[node_count + lax.axis_index("pool")]
    half = lax.broadcasted_iota(jnp.int32, bias_ref.shape, 0) // 8
    is_mid = (lax.axis_index("tp") + half) % 2 == 1
    key = lax.broadcasted_iota(jnp.int32, bias_ref.shape, 1) % (requests * page)
    offset = key // page - jnp.where(is_mid, owner_ref[mid], owner_ref[0])
    offset = jnp.where(offset < 0, offset + requests, offset)
    used = offset < jnp.where(is_mid, pages_ref[mid], pages_ref[0])
    bias_ref[...] = jnp.where(used, 0.0, MASKED)
    for copy in fetches[4:] + [send]:
        copy.wait()


def hand_over_kernel(*refs):
    pass


def hand_over(cost, *arrays):
    anywhere = pl.BlockSpec(memory_space=pl.ANY)
    return pl.pallas_call(
        hand_over_kernel,
        out_shape=[jax.ShapeDtypeStruct(array.shape, array.dtype) for array in arrays],
        in_specs=[anywhere] * len(arrays),
        out_specs=[anywhere] * len(arrays),
        input_output_aliases={i: i for i in range(len(arrays))},
        compiler_params=pltpu.CompilerParams(vmem_limit_bytes=2**20),
        cost_estimate=cost,
    )(*arrays)


def scores_of(rows, keys):
    scores = lax.dot_general(rows, keys, (((1,), (1,)), ((), ())), preferred_element_type=jnp.float32)
    return scores * (LOG2_E * 128 ** (-0.5))


def over(sums, totals):
    inverse = pl.reciprocal(totals, approx=True)
    return sums * (inverse * (2.0 - totals * inverse))


def weigh(weights, values):
    sums = dot(weights.astype(jnp.bfloat16), jnp.concatenate([values, jnp.ones_like(values)], 1))
    return sums[:, : values.shape[1]], sums[:, values.shape[1] :]


def own_kernel(leaf_len_ref, q_ref, *rest, page):
    local_refs = rest[:4]
    result_ref, level_ref, bias_ref, kf_ref, vf_ref = rest[4:]
    tokens, q_heads, dim = q_ref.shape
    group = q_heads // 4
    leaf_slots = bias_ref.shape[0] - 4 * tokens
    rank = lax.axis_index("tp")

    key = lax.broadcasted_iota(jnp.int32, (leaf_slots, dim), 0)
    bias_ref[0:leaf_slots] = jnp.where(key < leaf_len_ref[0] * page, 0.0, MASKED).astype(jnp.bfloat16)
    key = lax.broadcasted_iota(jnp.int32, (tokens, dim), 0)
    row = lax.broadcasted_iota(jnp.int32, (tokens, dim), 1)
    for step in range(4):
        seen = key <= row if step == 0 else jnp.full((tokens, dim), rank ^ step, jnp.int32) < rank
        bias_ref[leaf_slots + step * tokens : leaf_slots + (step + 1) * tokens] = jnp.where(
            seen, 0.0, MASKED
        ).astype(jnp.bfloat16)

    fresh_rows = local_refs[0].shape[0] - 2 * leaf_slots

    def fresh_source(out_row):
        head, kind, token = out_row // (2 * tokens), (out_row // tokens) % 2, out_row % tokens
        return token * 8 + head * 2 + kind

    fresh_pick = pick((fresh_rows, fresh_rows), fresh_source)
    for step in range(4):
        parts = dot(fresh_pick, local_refs[step][2 * leaf_slots :]).astype(jnp.bfloat16)
        for head in range(4):
            base = head * 2 * tokens
            kf_ref[head, step * tokens : (step + 1) * tokens] = parts[base : base + tokens]
            vf_ref[head, step * tokens : (step + 1) * tokens] = parts[base + tokens : base + 2 * tokens]

    chunk = 256
    half = chunk // 2
    leaf_pick = pick((chunk, chunk), lambda out_row: (out_row % half) * 2 + out_row // half)
    bias = bias_ref[...]
    token = lax.broadcasted_iota(jnp.int32, (tokens * group, dim), 0) // group
    column = lax.broadcasted_iota(jnp.int32, (tokens * group, dim), 1)
    own_row = jnp.where(token == column, 1.0, 0.0).astype(jnp.bfloat16)
    for step in range(4):
        head = rank ^ step
        leaf_k, leaf_v = [], []
        for piece in range(leaf_slots // half):
            parts = dot(leaf_pick, local_refs[step][piece * chunk : (piece + 1) * chunk]).astype(jnp.bfloat16)
            leaf_k.append(parts[:half])
            leaf_v.append(parts[half:])
        keys = jnp.concatenate([jnp.concatenate(leaf_k + [kf_ref[head]], 0), bias], 1)
        values = jnp.concatenate(leaf_v + [vf_ref[head]], 0)
        rows = q_ref[:, pl.ds(pl.multiple_of(head * group, group), group), :].reshape(tokens * group, dim)
        scores = scores_of(jnp.concatenate([rows, own_row], 1), keys)
        top = jnp.max(scores, axis=1, keepdims=True)
        sums, totals = weigh(jnp.exp2(scores - top), values)
        result_ref[step] = sums / totals
        level_ref[step] = jnp.log2(totals) + top


PAIRS = ((0, 1), (2, 3))


def blocks(a, b):
    zero = jnp.zeros_like(a)
    return jnp.concatenate([jnp.concatenate([a, zero], 1), jnp.concatenate([zero, b], 1)], 0)


def spread(a, b, width):
    lanes = a.shape[1]
    if width == lanes:
        return jnp.where(lax.broadcasted_iota(jnp.int32, a.shape, 1) < width // 2, a, b)
    return jnp.concatenate([a] * (width // 2 // lanes) + [b] * (width // 2 // lanes), 1)


def place_of(step, group):
    return pl.ds(pl.multiple_of((lax.axis_index("tp") ^ step) * group, group), group)


def kinds_of(pool_ref, step):
    rows = pool_ref[lax.axis_index("tp") ^ step].astype(jnp.float32)
    page, dim = rows.shape[1] // 2, rows.shape[2]
    return [rows[:, i * page : (i + 1) * page].reshape(-1, dim).astype(jnp.bfloat16) for i in range(2)]


def above_level(pair, q_ref, bias, level_ref, pool_ref):
    tokens, q_heads, dim = q_ref.shape
    group = q_heads // 4
    rows = [q_ref[:, place_of(step, group), :].reshape(tokens * group, dim) for step in pair]
    keys = blocks(*[kinds_of(pool_ref, step)[0] for step in pair])
    scores = scores_of(jnp.concatenate(rows, 1), keys)
    return scores + bias - spread(level_ref[pair[0]], level_ref[pair[1]], scores.shape[1])


def weigh_pair(pair, weights, pool_ref):
    values = [kinds_of(pool_ref, step)[1] for step in pair]
    ones = jnp.ones_like(values[0])
    return dot(weights, blocks(*values)), dot(weights, blocks(ones, ones))


def side_by_side(ref, pair):
    return jnp.concatenate([ref[step] for step in pair], 1)


def first_half_kernel(q_ref, bias_ref, other_ref, level_ref, pool_ref, sums_ref, totals_ref, peak_ref):
    peak = None
    scores = [above_level(pair, q_ref, bias_ref[0:1], level_ref, pool_ref) for pair in PAIRS]
    for i, pair in enumerate(PAIRS):
        weights = jnp.exp2(scores[i]).astype(jnp.bfloat16)
        peak = weights if peak is None else jnp.maximum(peak, weights)
        sums, totals = weigh_pair(pair, weights, pool_ref)
        sums_ref[i] = sums + side_by_side(other_ref, pair)
        totals_ref[i] = totals + 1.0
    peak = jnp.max(peak.astype(jnp.float32), axis=0, keepdims=True)
    peak_ref[...] = jnp.broadcast_to(peak, peak_ref.shape)


def second_half_kernel(
    q_ref, bias_ref, other_ref, level_ref, mine_ref, sums_ref, totals_ref, peak_ref, theirs_ref,
    out_hbm, stage_ref, sems,
):
    tokens, q_heads, dim = q_ref.shape
    group = q_heads // 4

    def write(pair, result):
        copies = []
        for i, step in enumerate(pair):
            part = result[:, i * dim : (i + 1) * dim]
            stage_ref[step] = part.astype(jnp.bfloat16).reshape(tokens, group, dim)
            target = out_hbm.at[:, place_of(step, group)]
            copies.append(pltpu.make_async_copy(stage_ref.at[step], target, sems.at[step]))
            copies[-1].start()
        return copies

    scores = [above_level(pair, q_ref, bias_ref[8:9], level_ref, theirs_ref) for pair in PAIRS]
    weights = [jnp.exp2(score).astype(jnp.bfloat16) for score in scores]
    found = [weigh_pair(pair, weights[i], theirs_ref) for i, pair in enumerate(PAIRS)]
    writes = []
    for i, (pair, (sums, totals)) in enumerate(zip(PAIRS, found)):
        writes += write(pair, over(sums + sums_ref[i], totals + totals_ref[i]))
    peak = jnp.maximum(jnp.max(functools.reduce(jnp.maximum, weights).astype(jnp.float32)), jnp.max(peak_ref[...]))
    for copy in writes:
        copy.wait()

    @pl.when(peak > 2.0**100)
    def _():
        for pair in PAIRS:
            mine = above_level(pair, q_ref, bias_ref[0:1], level_ref, mine_ref)
            theirs = above_level(pair, q_ref, bias_ref[8:9], level_ref, theirs_ref)
            both = jnp.maximum(mine, theirs)
            half = both.shape[1] // 2
            first = lax.broadcasted_iota(jnp.int32, both.shape, 1) < half
            tops = [
                jnp.maximum(jnp.max(jnp.where(first == (i == 0), both, 0.0), axis=1, keepdims=True), 0.0)
                for i in range(2)
            ]
            tops = [jnp.broadcast_to(top, (tokens * group, dim)) for top in tops]
            top = spread(*tops, both.shape[1])
            rest = jnp.exp2(-jnp.concatenate(tops, 1))
            sums, totals = weigh_pair(pair, jnp.exp2(mine - top).astype(jnp.bfloat16), mine_ref)
            more, added = weigh_pair(pair, jnp.exp2(theirs - top).astype(jnp.bfloat16), theirs_ref)
            sums = sums + more + side_by_side(other_ref, pair) * rest
            for copy in write(pair, over(sums, totals + added + rest)):
                copy.wait()


def per_device(queries, fresh, pool, leaf, parent, node_pages, node_owner, leaf_len):
    tp = lax.axis_size("tp")
    stripes = lax.axis_size("pool")
    shared_count, _, page, _, _, dim = pool.shape
    tokens, q_heads, _ = queries.shape
    vmem = pl.BlockSpec(memory_space=pltpu.VMEM)
    swap = lambda array, bit: lax.ppermute(array, "tp", [(i, i ^ bit) for i in range(tp)])
    hbm = pl.BlockSpec(memory_space=pltpu.HBM)

    pool_rows = pool.reshape(-1, dim)
    leaf_rows = leaf.reshape(-1, dim)
    fresh_rows = fresh.reshape(-1, dim)
    operands = (parent, node_pages, node_owner, pool_rows, leaf_rows, fresh_rows)
    sent, local_0, bias = pl.pallas_call(
        functools.partial(select_kernel, page),
        out_shape=[
            jax.ShapeDtypeStruct((tp, stripes, 2 * page, dim), jnp.bfloat16),
            jax.ShapeDtypeStruct((leaf_rows.shape[0] + fresh_rows.shape[0], dim), jnp.bfloat16),
            jax.ShapeDtypeStruct((16, stripes * 2 * page), jnp.float32),
        ],
        in_specs=[hbm] * 6,
        out_specs=[hbm, vmem, vmem],
        scratch_shapes=[
            pltpu.SMEM(parent.shape, jnp.int32),
            pltpu.SMEM(node_pages.shape, jnp.int32),
            pltpu.SMEM(node_owner.shape, jnp.int32),
            pltpu.VMEM(pool_rows.shape, jnp.bfloat16),
            pltpu.VMEM(pool_rows.shape, jnp.float32),
            pltpu.VMEM((tp, stripes, 2 * page, dim), jnp.bfloat16),
            pltpu.SemaphoreType.DMA((7,)),
        ],
        compiler_params=pltpu.CompilerParams(vmem_limit_bytes=16 * 2**20),
        cost_estimate=LONG,
    )(*[pltpu.with_memory_space_constraint(operand, pltpu.HBM) for operand in operands])
    local_2 = swap(local_0, 2)
    mine = lax.all_to_all(
        sent.reshape(tp * stripes, 2 * page, dim), ("tp", "pool"), split_axis=0, concat_axis=0, tiled=True
    ).reshape(tp, stripes, 2 * page, dim)
    local_0, local_2 = hand_over(LONG, local_0, local_2)
    local_1, local_3 = swap(local_0, 1), swap(local_2, 1)

    rows = tokens * q_heads // tp
    other, level = pl.pallas_call(
        functools.partial(own_kernel, page=page),
        out_shape=[jax.ShapeDtypeStruct((tp, rows, dim), jnp.float32)] * 2,
        in_specs=[pl.BlockSpec(memory_space=pltpu.SMEM)] + [vmem] * 5,
        out_specs=[vmem] * 2,
        scratch_shapes=[pltpu.VMEM((leaf.shape[1] + tp * tokens, dim), jnp.bfloat16)]
        + [pltpu.VMEM((tp, tp * tokens, dim), jnp.bfloat16)] * 2,
        compiler_params=pltpu.CompilerParams(vmem_limit_bytes=24 * 2**20),
        cost_estimate=SHORT,
    )(leaf_len, queries, local_0, local_1, local_2, local_3)
    mine, level = hand_over(SHORT, mine, level)
    theirs = swap(mine, 1)
    limit = pltpu.CompilerParams(vmem_limit_bytes=(24 if stripes <= 8 else 48) * 2**20)
    sums, totals, peak = pl.pallas_call(
        first_half_kernel,
        out_shape=[jax.ShapeDtypeStruct((len(PAIRS), rows, 2 * dim), jnp.float32)] * 2
        + [jax.ShapeDtypeStruct((8, bias.shape[1]), jnp.float32)],
        in_specs=[vmem] * 5,
        out_specs=[vmem] * 3,
        compiler_params=limit,
        cost_estimate=SHORT,
    )(queries, bias, other, level, mine)
    return pl.pallas_call(
        second_half_kernel,
        out_shape=jax.ShapeDtypeStruct(queries.shape, jnp.bfloat16),
        in_specs=[vmem] * 9,
        out_specs=hbm,
        scratch_shapes=[
            pltpu.VMEM((tp, tokens, q_heads // tp, dim), jnp.bfloat16),
            pltpu.SemaphoreType.DMA((tp,)),
        ],
        compiler_params=limit,
    )(queries, bias, other, level, mine, sums, totals, peak, theirs)


def solution(mesh):
    return jax.shard_map(
        per_device,
        mesh=mesh,
        in_specs=(
            P(("pool", "tp"), None, None),
            P(("pool", "tp"), None, None, None),
            P(None, "pool", None, "tp", None, None),
            P("pool", None, "tp", None, None),
            P(),
            P(),
            P(),
            P("pool"),
        ),
        out_specs=P(("pool", "tp"), None, None),
        check_vma=False,
    )
```
